32 devices in a mesh: seq: 16 (over z, y, x), head: 2 (over core).
Axes of the slice: x: 2, y: 2, z: 4, core: 2. Of those that a mesh axis runs over, the one named last changes fastest.
Arguments:
- tokens: bfloat16 [32768, 512], P(('seq', 'head')), may hold values from -6 to 6
- first_values: bfloat16 [32768, 256], P(('seq', 'head')), may hold values from -6 to 6
- cotangent: bfloat16 [32768, 512], P(('seq', 'head')), may hold values from -6 to 6
- slot_count: int32 [16], P('seq'), may hold values from 1 to 8, as said below
- seq_lengths: int32 [16, 8], P('seq'), may hold values from 129 to 2048, as said below
- query_weight: bfloat16 [512, 512], replicated, may hold values from -0.5 to 0.5
- key_weight: bfloat16 [512, 512], replicated, may hold values from -0.25 to 0.25
- value_weight: bfloat16 [512, 256], replicated, may hold values from -0.25 to 0.25
- mixing_weight: bfloat16 [512, 512], replicated, may hold values from -1 to 1
- expand_weight: bfloat16 [512, 2048], replicated, may hold values from -0.25 to 0.25
- shrink_weight: bfloat16 [2048, 512], replicated, may hold values from -0.125 to 0.125
- expand_bias: float32 [2048], replicated, may hold values from -3 to 3
- before_gain: float32 [512], replicated, may hold values from 0.5 to 1.5
- before_shift: float32 [512], replicated, may hold values from -2 to 2
- middle_gain: float32 [512], replicated, may hold values from 0.5 to 1.5
- middle_shift: float32 [512], replicated, may hold values from -2 to 2
Outputs:
- output: bfloat16 [32768, 512], P(('seq', 'head'))
- input_grad: bfloat16 [32768, 512], P(('seq', 'head'))
- skip_grad: bfloat16 [32768, 256], P(('seq', 'head'))
- query_grad: float32 [512, 512], replicated
- key_grad: float32 [512, 512], replicated
- value_grad: float32 [512, 256], replicated
- mixing_grad: float32 [512, 512], replicated
- expand_grad: float32 [512, 2048], replicated
- shrink_grad: float32 [2048, 512], replicated
- bias_grad: float32 [2048], replicated
- before_gain_grad: float32 [512], replicated
- before_shift_grad: float32 [512], replicated
- middle_gain_grad: float32 [512], replicated
- middle_shift_grad: float32 [512], replicated
The draws below stay inside these ranges and needn't reach their ends.
Inputs may be any that keep to these rules, and one draw needn't show every extreme that they name: `slot_count`: each bucket holds 1, 2, 4 or 8 sequences; the first bucket holds one and the second eight. `seq_lengths`: for a bucket of c sequences each slot below c holds a length above 2048 / (2 c) and at most 2048 / c; slots from c on are not read. The first bucket's sequence has 2048 tokens.
All inputs are finite; a program needn't handle non-finite values.
Results may differ from the reference program's by a relative error of at most 0.013.
The reference program's roundings to bfloat16 on the way count: a program that leaves them out, or rounds other values in their place, can miss the bound.
Values may be sent and summed in bfloat16 or wider, within the bound.
No kernel may reach another device: no remote copies, remote signals or barrier semaphores. Data moves between devices by JAX's collectives and lax.ppermute only.
A program may use at most 256 MiB of HBM per device.

```python
import math
import jax
import jax.numpy as jnp
from jax import lax

D = 512
HEADS = 8
HEAD_DIM = 64
FF = 2048
ROWS = 2048
MAX_SLOTS = 8
BUCKETS = 16
TOKENS = 32768
N_HEAD = 2


def bucket_draw(key):
    first_key, second_key = jax.random.split(key)
    powers = jax.random.randint(first_key, (BUCKETS,), 0, 4, dtype=jnp.int32)
    powers = powers.at[0].set(0).at[1].set(3)
    counts = jnp.array([1, 2, 4, 8], dtype=jnp.int32)[powers]
    slot_rows = ROWS // counts
    raw_bits = jax.random.randint(second_key, (BUCKETS, MAX_SLOTS), 0, 1 << 20, dtype=jnp.int32)
    halves = slot_rows[:, None] // 2
    lengths = halves + 1 + raw_bits % halves
    lengths = lengths.at[0, 0].set(ROWS).at[1, 0].set(ROWS // 16 + 1)
    return (counts, lengths)


def draw_slot_count(key, part):
    return bucket_draw(key)[0]


def draw_seq_lengths(key, part):
    return bucket_draw(key)[1]


def levels(own_key, dims, shards, least, top_value):
    factor_of, own = 1.0, jax.random.fold_in(own_key, 6)
    for dim, parts in shards:
        heights = jnp.exp(jax.random.uniform(jax.random.fold_in(own, dim), (parts,), jnp.float32, least / len(shards), top_value / len(shards)))
        factor_of = factor_of * jnp.repeat(heights, dims[dim] // parts).reshape([-1 if axis == dim else 1 for axis in range(len(dims))])
    return factor_of


def noise(own_key, extent, scale, most, cuts=(), kind=jnp.bfloat16):
    values = jax.random.normal(own_key, extent, jnp.float32) * scale
    if len(cuts) > 0:
        values = levels(own_key, extent, cuts, -0.22, 0.18) * values
    return jnp.clip(values, min=-most, max=most).astype(kind)


def setup_inputs(seed: int = 0) -> dict:
    splits = jax.random.split(jax.random.key(seed), 17)
    return {
        "tokens": noise(splits[0], (TOKENS, D), 1.0, 6.0, ((0, 32),)),
        "first_values": noise(splits[1], (TOKENS, D // 2), 1.0, 6.0, ((0, 32),)),
        "cotangent": noise(splits[2], (TOKENS, D), 1.0, 6.0, ((0, 32),)),
        "slot_count": draw_slot_count(jax.random.fold_in(splits[16], 71), 0),
        "seq_lengths": draw_seq_lengths(jax.random.fold_in(splits[16], 71), 0),
        "query_weight": noise(splits[5], (D, D), (D // 4) ** -0.5, 0.5),
        "key_weight": noise(splits[6], (D, D), D ** -0.5, 0.25),
        "value_weight": noise(splits[7], (D, D // 2), D ** -0.5, 0.25),
        "mixing_weight": noise(splits[8], (D, D), (D // 16) ** -0.5, 1.0),
        "expand_weight": noise(splits[9], (D, FF), D ** -0.5, 0.25),
        "shrink_weight": noise(splits[10], (FF, D), FF ** -0.5, 0.125),
        "expand_bias": noise(splits[11], (FF,), 0.5, 3.0, (), jnp.float32),
        "before_gain": jnp.clip(1.0 + 0.1 * jax.random.normal(splits[12], (D,), jnp.float32), 0.5, 1.5),
        "before_shift": noise(splits[13], (D,), 0.3, 2.0, (), jnp.float32),
        "middle_gain": jnp.clip(1.0 + 0.1 * jax.random.normal(splits[14], (D,), jnp.float32), 0.5, 1.5),
        "middle_shift": noise(splits[15], (D,), 0.3, 2.0, (), jnp.float32),
    }


@jax.custom_vjp
def low(v):
    return lax.optimization_barrier(v.astype(jnp.bfloat16)).astype(jnp.float32)

@jax.custom_vjp
def low_back(v):
    return v

def low_keep(v):
    return (low(v), None)

def low_pass(kept, grad):
    return (grad,)

def back_keep(v):
    return (v, None)

def back_low(kept, grad):
    return (low(grad),)
low.defvjp(low_keep, low_pass)
low_back.defvjp(back_keep, back_low)
epsilon = 1e-05
negative = -1e+30

def matmul(left_side, right_side):
    return jnp.dot(left_side, right_side, precision=lax.Precision.HIGHEST)

def layer_norm(row_values, norm_gain, norm_shift):
    average = lax.optimization_barrier(jnp.mean(row_values, axis=-1, keepdims=True))
    centred = row_values - average
    spread = lax.optimization_barrier(jnp.mean(centred * centred, axis=-1, keepdims=True))
    return centred * lax.rsqrt(spread + epsilon) * norm_gain + norm_shift

def bucket_block(params, row_values, first_rows, slots, lengths):
    query_weight, key_weight, value_weight, mixing_weight, expand_weight, shrink_weight, expand_bias, before_gain, before_shift, middle_gain, middle_shift = params
    row_total = row_values.shape[0]
    indices = jnp.arange(row_total, dtype=jnp.int32)
    slot_of = indices % slots
    position = indices // slots
    table = jnp.arange(lengths.shape[0], dtype=jnp.int32)
    limit = lax.optimization_barrier(jnp.sum(jnp.where(slot_of[:, None] == table[None, :], lengths[None, :], 0), axis=1))
    valid_rows = position < limit
    normed = low(layer_norm(row_values, before_gain, before_shift))
    query = low_back(low(matmul(normed, query_weight)))
    key_rows = low_back(low(matmul(normed, key_weight)))
    fresh = low_back(low(matmul(normed, value_weight)))
    skipped = low_back(first_rows)
    group = HEADS // N_HEAD
    fresh_heads = fresh.reshape(row_total, N_HEAD, group // 2, HEAD_DIM)
    skip_heads = skipped.reshape(row_total, N_HEAD, group // 2, HEAD_DIM)
    values = jnp.concatenate([fresh_heads, skip_heads], axis=2).reshape(row_total, HEADS, HEAD_DIM)
    query_heads = query.reshape(row_total, HEADS, HEAD_DIM)
    key_heads = key_rows.reshape(row_total, HEADS, HEAD_DIM)
    scaling = 1.0 / math.sqrt(HEAD_DIM)
    scores = jnp.einsum('qhd,khd->hqk', query_heads, key_heads, precision=lax.Precision.HIGHEST) * scaling
    scores = low_back(scores)
    allowed = (slot_of[:, None] == slot_of[None, :]) & (indices[None, :] <= indices[:, None])
    masked = jnp.where(allowed[None], scores, negative)
    weights = low(jax.nn.softmax(masked, axis=-1))
    mixed = jnp.einsum('hqk,khd->qhd', weights, values, precision=lax.Precision.HIGHEST).reshape(row_total, D)
    mixed = low_back(low(mixed))
    branch = low_back(matmul(mixed, mixing_weight))
    after = row_values + branch
    middle = low(layer_norm(after, middle_gain, middle_shift))
    pre_act = low_back(matmul(middle, expand_weight) + expand_bias)
    active = low(jax.nn.gelu(pre_act, approximate=True))
    grown = low_back(matmul(active, shrink_weight))
    return jnp.where(valid_rows[:, None], after + grown, 0.0)

def add_pair(first_one, second_one):
    return first_one + second_one

def reference(tokens, first_values, cotangent, slot_count, seq_lengths, query_weight, key_weight, value_weight, mixing_weight, expand_weight, shrink_weight, expand_bias, before_gain, before_shift, middle_gain, middle_shift):
    params = tuple((item.astype(jnp.float32) for item in (query_weight, key_weight, value_weight, mixing_weight, expand_weight, shrink_weight, expand_bias, before_gain, before_shift, middle_gain, middle_shift)))
    token_blocks = tokens.astype(jnp.float32).reshape(BUCKETS, ROWS, D)
    first_blocks = first_values.astype(jnp.float32).reshape(BUCKETS, ROWS, D // 2)
    cot_blocks = cotangent.astype(jnp.float32).reshape(BUCKETS, ROWS, D)

    def bucket_step(totals, item):
        row_values, first_rows, cot_rows, slots, lengths = item

        def forward(weights_in, rows_in, first_in):
            return bucket_block(weights_in, rows_in, first_in, slots, lengths)
        result, pullback = jax.vjp(forward, params, row_values, first_rows)
        grad_params, grad_rows, grad_first = pullback(cot_rows)
        totals = jax.tree.map(add_pair, totals, grad_params)
        return (totals, (result.astype(jnp.bfloat16), grad_rows.astype(jnp.bfloat16), grad_first.astype(jnp.bfloat16)))
    zeros = tuple((jnp.zeros_like(item) for item in params))
    totals, (results, row_grads, first_grads) = lax.scan(bucket_step, zeros, (token_blocks, first_blocks, cot_blocks, slot_count, seq_lengths))
    return (results.reshape(TOKENS, D), row_grads.reshape(TOKENS, D), first_grads.reshape(TOKENS, D // 2), totals[0], totals[1], totals[2], totals[3], totals[4], totals[5], totals[6], totals[7], totals[8], totals[9], totals[10])
```

```python
from functools import partial
import math
import jax
import jax.numpy as jnp
from jax import lax
from jax.experimental import pallas as pl
from jax.experimental.pallas import tpu as pltpu
from jax.sharding import PartitionSpec as P

BLOCK = 256
SLOT_OPTIONS = (1, 2, 4, 8)
LOG2E = math.log2(math.e)
F32, BF16 = jnp.float32, jnp.bfloat16
MASKED = -1e30
EPS = 1e-05
MIB = 1 << 20


def nn(a, b):
    return lax.dot_general(a, b, (((1,), (0,)), ((), ())), preferred_element_type=F32)


def nt(a, b):
    return lax.dot_general(a, b, (((1,), (1,)), ((), ())), preferred_element_type=F32)


def tn(a, b):
    return lax.dot_general(a, b, (((0,), (0,)), ((), ())), preferred_element_type=F32)


def sorter(count, transposed=False):
    each = BLOCK // count
    grouped = lax.broadcasted_iota(jnp.int32, (BLOCK, BLOCK), 1 if transposed else 0)
    plain = lax.broadcasted_iota(jnp.int32, (BLOCK, BLOCK), 0 if transposed else 1)
    place = (plain & (count - 1)) * each + (plain >> (count.bit_length() - 1))
    return jnp.where(grouped == place, 1.0, 0.0).astype(BF16)


def store_grouped(write, values, tile, total, count):
    each = BLOCK // count
    for group in range(count):
        start = pl.multiple_of(group * (total // count) + tile * each, each)
        write(pl.ds(start, each), values[group * each : (group + 1) * each])


def load_grouped(read, tile, total, count):
    each = BLOCK // count
    parts = []
    for group in range(count):
        start = pl.multiple_of(group * (total // count) + tile * each, each)
        parts.append(read(pl.ds(start, each)))
    return parts[0] if count == 1 else jnp.concatenate(parts, axis=0)


def normalized(rows):
    average = jnp.mean(rows, axis=-1, keepdims=True)
    centred = rows - average
    spread = jnp.mean(centred * centred, axis=-1, keepdims=True)
    scale = lax.rsqrt(spread + EPS)
    return centred * scale, scale


def as_columns(vectors):
    stack = jnp.concatenate(vectors + [jnp.zeros((128 - len(vectors), vectors[0].shape[1]), F32)], axis=0)
    return jnp.transpose(stack).astype(BF16)


def forward_kernel(
    info, own, other, skip_own, skip_other, query_weight, key_weight, value_weight, gain, shift,
    mixed_own, mixed_other, query, keys, saved, mixed, logsum, normed, values,
):
    count, head = info[0], info[1]
    half = own.shape[0]
    total = 2 * half
    blocks = total // BLOCK
    values[:, :, 128:] = jnp.ones((2, total, 128), BF16)

    for rows_ref, skip_ref, which in ((own, skip_own, head), (other, skip_other, 1 - head)):

        def project(step, _, rows_ref=rows_ref, skip_ref=skip_ref, which=which):
            at = pl.ds(pl.multiple_of(step * BLOCK, BLOCK), BLOCK)
            tile = which * (half // BLOCK) + step
            hat, _s = normalized(rows_ref[at, :].astype(F32))
            low = (hat * gain[...] + shift[...]).astype(BF16)
            skip = skip_ref[at, :]

            def put(count_here):
                rows, skipped = low, skip
                if count_here > 1:
                    order = sorter(count_here)
                    rows = nn(order, low).astype(BF16)
                    skipped = nn(order, skip).astype(BF16)
                q = nn(rows, query_weight[...]).astype(BF16)
                q = q * jnp.asarray(0.125, BF16)
                k = nn(rows, key_weight[...]).astype(BF16)
                f = nn(rows, value_weight[...]).astype(BF16)

                def put_in(ref, part, value):
                    def write(dst, piece):
                        if part is None:
                            ref[dst, :] = piece
                        else:
                            ref[part, dst, :128] = piece
                            if ref is values:
                                saved[part, dst, :] = piece

                    store_grouped(write, value, tile, total, count_here)

                put_in(normed, None, rows)
                put_in(query, 0, q[:, :128])
                put_in(query, 1, q[:, 128:])
                put_in(keys, 0, k[:, :128])
                put_in(keys, 1, k[:, 128:])
                put_in(values, 0, f)
                put_in(values, 1, skipped)

            for option in SLOT_OPTIONS:
                pl.when(count == option)(partial(put, option))
            return 0

        lax.fori_loop(0, half // BLOCK, project, 0)

    per_slot = blocks // count
    lane = lax.broadcasted_iota(jnp.int32, (1, 128), 1)
    tri = lax.broadcasted_iota(jnp.int32, (BLOCK, BLOCK), 1) <= lax.broadcasted_iota(
        jnp.int32, (BLOCK, BLOCK), 0
    )

    def attend(block, _):
        width = block % per_slot + 1
        here = pl.multiple_of(block * BLOCK, BLOCK)

        def run(wide):
            first = pl.multiple_of((block - (wide - 1)) * BLOCK, BLOCK)

            def score(h):
                pair, sub = h // 2, h % 2
                q = query[pair, pl.ds(here, BLOCK), :]
                qm = jnp.where((lane < 64) == (sub == 0), q, jnp.zeros_like(q))
                diag = nt(qm, keys[pair, pl.ds(here, BLOCK), :]) * LOG2E
                rest = None
                if wide > 1:
                    rest = nt(qm, keys[pair, pl.ds(first, (wide - 1) * BLOCK), :]) * LOG2E
                return diag, rest

            def finish(h, diag, rest):
                pair, sub = h // 2, h % 2
                diag = jnp.where(tri, diag, MASKED)
                top = jnp.max(diag, axis=1, keepdims=True)
                if wide > 1:
                    top = jnp.maximum(top, jnp.max(rest, axis=1, keepdims=True))
                raised = jnp.exp2(diag - top).astype(BF16)
                acc = nn(raised, values[pair, pl.ds(here, BLOCK), :])
                if wide > 1:
                    raised = jnp.exp2(rest - top).astype(BF16)
                    acc += nn(raised, values[pair, pl.ds(first, (wide - 1) * BLOCK), :])
                sums = acc[:, 128:]
                return acc[:, :128] / sums, jnp.transpose(top + jnp.log2(sums))[0:1, :]

            nxt = score(0)
            outs = []
            for h in range(4):
                cur = nxt
                if h < 3:
                    nxt = score(h + 1)
                outs.append(finish(h, *cur))
            for pair in range(2):
                mixed[pair, pl.ds(here, BLOCK), :] = jnp.where(lane < 64, outs[2*pair][0], outs[2*pair+1][0]).astype(BF16)
                for sub in range(2):
                    logsum[pair, sub : sub + 1, pl.ds(here, BLOCK)] = outs[2*pair+sub][1]

        for wide in range(1, blocks + 1):
            pl.when(width == wide)(partial(run, wide))
        return 0

    lax.fori_loop(0, blocks, attend, 0)

    for out_ref, which in ((mixed_own, head), (mixed_other, 1 - head)):

        def give(step, _, out_ref=out_ref, which=which):
            at = pl.ds(pl.multiple_of(step * BLOCK, BLOCK), BLOCK)
            tile = which * (half // BLOCK) + step

            def put(count_here):
                for pair in range(2):
                    part = load_grouped(lambda s: mixed[pair, s, :], tile, total, count_here)
                    if count_here > 1:
                        part = nn(sorter(count_here, True), part).astype(BF16)
                    out_ref[at, pair * 128 : (pair + 1) * 128] = part

            for option in SLOT_OPTIONS:
                pl.when(count == option)(partial(put, option))
            return 0

        lax.fori_loop(0, half // BLOCK, give, 0)


def whole(shape):
    return pl.BlockSpec(shape, lambda i, s: (0,) * len(shape))


def forward_attention(info, own, other, skip_own, skip_other, wq, wk, wv, gain, shift):
    half, width = own.shape
    total = 2 * half
    group = wq.shape[1] // 2
    outs = [
        ((half, group), BF16),
        ((half, group), BF16),
        ((2, total, 128), BF16),
        ((2, total, 128), BF16),
        ((2, total, 128), BF16),
        ((2, total, 128), BF16),
        ((2, 8, total), F32),
        ((total, width), BF16),
    ]
    return pl.pallas_call(
        forward_kernel,
        grid_spec=pltpu.PrefetchScalarGridSpec(
            num_scalar_prefetch=1,
            grid=(1,),
            in_specs=[
                whole(own.shape),
                whole(other.shape),
                pl.BlockSpec((half, 128), lambda i, s: (0, s[1])),
                whole(skip_other.shape),
                pl.BlockSpec((width, group), lambda i, s: (0, s[1])),
                pl.BlockSpec((width, group), lambda i, s: (0, s[1])),
                pl.BlockSpec((width, 128), lambda i, s: (0, s[1])),
                whole(gain.shape),
                whole(shift.shape),
            ],
            out_specs=[whole(s) for s, _ in outs],
            scratch_shapes=[pltpu.VMEM((2, total, 256), BF16)],
        ),
        out_shape=[jax.ShapeDtypeStruct(s, d) for s, d in outs],
        compiler_params=pltpu.CompilerParams(vmem_limit_bytes=56 * MIB),
        name="forward_attention",
    )(info, own, other, skip_own, skip_other, wq, wk, wv, gain, shift)


COLS = 512
GELU_SLOPE = math.sqrt(2.0 / math.pi)
GELU_CUBE = 0.044715


def gelu_pair(v):
    square = v * v
    bend = jnp.tanh(v * (GELU_SLOPE + (GELU_SLOPE * GELU_CUBE) * square))
    front = 0.5 + 0.5 * bend
    slope = front + (0.5 * v) * (1.0 - bend * bend) * (
        GELU_SLOPE + (3.0 * GELU_SLOPE * GELU_CUBE) * square
    )
    return v * front, slope


def rows_kernel(
    info, lengths, tokens, mixed_own, mixed_other, cotangent, mixing_weight, expand_weight,
    shrink_weight, expand_bias, gain, shift,
    output, after_grad, send_own, send_other, shrink_grad, wide_grad,
    bias_grad, gain_grads, active, slope, pre_grad, middle, out_grad, after_low,
):
    count, head = info[0], info[1]
    half, width = tokens.shape
    hidden = expand_weight.shape[1]
    group = mixed_own.shape[1]
    shift_by = (
        (count >= 2).astype(jnp.int32)
        + (count >= 4).astype(jnp.int32)
        + (count >= 8).astype(jnp.int32)
    )
    here = pl.ds(pl.multiple_of(head * group, group), group)
    there = pl.ds(pl.multiple_of((1 - head) * group, group), group)
    bias_grad[...] = jnp.zeros_like(bias_grad)
    gain_grads[...] = jnp.zeros_like(gain_grads)

    def tile(step, _):
        at = pl.ds(pl.multiple_of(step * BLOCK, BLOCK), BLOCK)
        row = head * half + step * BLOCK + lax.broadcasted_iota(jnp.int32, (BLOCK, 1), 0)
        slot = row & (count - 1)
        limit = jnp.zeros_like(row)
        for s in range(lengths.shape[0]):
            limit = jnp.where(slot == s, lengths[s], limit)
        valid = (row >> shift_by) < limit
        after = (
            tokens[at, :].astype(F32)
            + nn(mixed_own[at, :], mixing_weight[here, :])
            + nn(mixed_other[at, :], mixing_weight[there, :])
        )
        hat, scale = normalized(after)
        low = (hat * gain[...] + shift[...]).astype(BF16)
        middle[at, :] = low
        for c in range(0, hidden, COLS):
            cs = slice(c, c + COLS)
            act, slo = gelu_pair(nn(low, expand_weight[:, cs]) + expand_bias[:, cs])
            active[at, cs] = act.astype(BF16)
            slope[:, cs] = slo
        grown = nn(active[at, :], shrink_weight[...])
        output[at, :] = jnp.where(valid, after + grown, 0.0).astype(BF16)
        grad_out = jnp.where(valid, cotangent[at, :].astype(F32), 0.0)
        grad_low = grad_out.astype(BF16)
        out_grad[at, :] = grad_low
        for c in range(0, hidden, COLS):
            cs = slice(c, c + COLS)
            g = nt(grad_low, shrink_weight[cs, :]) * slope[:, cs]
            bias_grad[0:1, cs] += jnp.sum(g, axis=0, keepdims=True)
            pre_grad[at, cs] = g.astype(BF16)
        g_middle = nt(pre_grad[at, :], expand_weight[...])
        gain_grads[0:1, :] += jnp.sum(g_middle * hat, axis=0, keepdims=True)
        gain_grads[1:2, :] += jnp.sum(g_middle, axis=0, keepdims=True)
        y = g_middle * gain[...]
        g_after = grad_out + scale * (
            y
            - jnp.mean(y, axis=-1, keepdims=True)
            - hat * jnp.mean(y * hat, axis=-1, keepdims=True)
        )
        after_grad[at, :] = g_after
        g_low = g_after.astype(BF16)
        after_low[at, :] = g_low
        send_own[at, :] = nt(g_low, mixing_weight[here, :]).astype(BF16)
        send_other[at, :] = nt(g_low, mixing_weight[there, :]).astype(BF16)
        return 0

    lax.fori_loop(0, half // BLOCK, tile, 0)

    def weights(step, _):
        cs = pl.ds(pl.multiple_of(step * COLS, COLS), COLS)
        shrink_grad[cs, :] = tn(active[:, cs], out_grad[...]).astype(BF16)
        wide_grad[:, cs] = tn(middle[...], pre_grad[:, cs]).astype(BF16)
        return 0

    lax.fori_loop(0, hidden // COLS, weights, 0)
    mix = slice(hidden, hidden + width)
    wide_grad[here, mix] = tn(mixed_own[...], after_low[...]).astype(BF16)
    wide_grad[there, mix] = tn(mixed_other[...], after_low[...]).astype(BF16)
    vectors = [bias_grad[0:1, c : c + width] for c in range(0, hidden, width)]
    vectors += [gain_grads[0:1, :], gain_grads[1:2, :]]
    wide_grad[:, hidden + width :] = as_columns(vectors)


def row_part(info, lengths, tokens, mixed_own, mixed_other, cotangent, wo, we, ws, bias, gain, shift):
    half, width = tokens.shape
    hidden = we.shape[1]
    group = mixed_own.shape[1]
    outs = [
        ((half, width), BF16),
        ((half, width), F32),
        ((half, group), BF16),
        ((half, group), BF16),
        ((hidden, width), BF16),
        ((width, hidden + width + 128), BF16),
    ]
    args = (tokens, mixed_own, mixed_other, cotangent, wo, we, ws, bias, gain, shift)
    block = lambda shape: pl.BlockSpec(shape, lambda i, s, t: (0,) * len(shape))
    return pl.pallas_call(
        rows_kernel,
        grid_spec=pltpu.PrefetchScalarGridSpec(
            num_scalar_prefetch=2,
            grid=(1,),
            in_specs=[block(a.shape) for a in args],
            out_specs=[block(s) for s, _ in outs],
            scratch_shapes=[
                pltpu.VMEM((8, hidden), F32),
                pltpu.VMEM((8, width), F32),
                pltpu.VMEM((half, hidden), BF16),
                pltpu.VMEM((BLOCK, hidden), F32),
                pltpu.VMEM((half, hidden), BF16),
                pltpu.VMEM((half, width), BF16),
                pltpu.VMEM((half, width), BF16),
                pltpu.VMEM((half, width), BF16),
            ],
        ),
        out_shape=[jax.ShapeDtypeStruct(s, d) for s, d in outs],
        compiler_params=pltpu.CompilerParams(vmem_limit_bytes=60 * MIB),
        name="row_part",
    )(info, lengths, *args)


def backward_kernel(
    info, own, other, grad_own, grad_other, query, keys, values, mixed, logsum, normed,
    query_weight, key_weight, value_weight,
    weight_grad, back_own, back_other, skip_own, skip_other,
    gain_grads, grad, inner, query_total, packed, skipped, back,
):
    count, head = info[0], info[1]
    half = own.shape[0]
    total = 2 * half
    blocks = total // BLOCK
    query_total[...] = jnp.zeros_like(query_total)

    for rows_ref, which in ((grad_own, head), (grad_other, 1 - head)):

        def arrange(step, _, rows_ref=rows_ref, which=which):
            at = pl.ds(pl.multiple_of(step * BLOCK, BLOCK), BLOCK)
            tile = which * (half // BLOCK) + step
            rows = rows_ref[at, :]

            def put(count_here):
                value = rows
                if count_here > 1:
                    value = nn(sorter(count_here), rows).astype(BF16)
                for pair in range(2):

                    def write(dst, piece, pair=pair):
                        grad[pair, dst, :] = piece

                    store_grouped(
                        write, value[:, pair * 128 : (pair + 1) * 128], tile, total, count_here
                    )

            for option in SLOT_OPTIONS:
                pl.when(count == option)(partial(put, option))
            return 0

        lax.fori_loop(0, half // BLOCK, arrange, 0)

    def inners(block, _):
        at = pl.ds(pl.multiple_of(block * BLOCK, BLOCK), BLOCK)
        for pair in range(2):
            flipped = jnp.transpose(grad[pair, at, :].astype(F32) * mixed[pair, at, :].astype(F32))
            for sub in range(2):
                inner[pair, sub : sub + 1, at] = jnp.sum(
                    flipped[sub * 64 : (sub + 1) * 64], axis=0, keepdims=True
                )
        return 0

    lax.fori_loop(0, blocks, inners, 0)

    per_slot = blocks // count
    lane = lax.broadcasted_iota(jnp.int32, (1, 128), 1)
    tri = lax.broadcasted_iota(jnp.int32, (BLOCK, BLOCK), 0) <= lax.broadcasted_iota(
        jnp.int32, (BLOCK, BLOCK), 1
    )

    def attend(block, _):
        width = per_slot - block % per_slot
        here = pl.multiple_of(block * BLOCK, BLOCK)

        def run(wide):
            span = pl.ds(here, wide * BLOCK)
            at = pl.ds(here, BLOCK)

            def score(h):
                pair, sub = h // 2, h % 2
                pick = (lane < 64) == (sub == 0)
                k, v = keys[pair, at, :], values[pair, at, :]
                k = jnp.where(pick, k, jnp.zeros_like(k))
                v = jnp.where(pick, v, jnp.zeros_like(v))
                return k, nt(k, query[pair, span, :]), nt(v, grad[pair, span, :])

            def finish(h, k, raw, grad_probs):
                pair, sub = h // 2, h % 2
                probs = jnp.exp2(raw * LOG2E - logsum[pair, sub : sub + 1, span])
                diag = jnp.where(tri, probs[:, :BLOCK], 0.0)
                probs = diag if wide == 1 else jnp.concatenate([diag, probs[:, BLOCK:]], axis=1)
                grad_scores = (probs * (grad_probs - inner[pair, sub : sub + 1, span])).astype(BF16)
                grad_value = nn(probs.astype(BF16), grad[pair, span, :])
                grad_key = nn(grad_scores, query[pair, span, :])
                return grad_value, grad_key, tn(grad_scores, k)

            ahead = score(0)
            done = []
            for h in range(4):
                now = ahead
                if h < 3:
                    ahead = score(h + 1)
                done.append(finish(h, *now))
                if h % 2:
                    pair = h // 2
                    first, second = done[h - 1], done[h]
                    gv = jnp.where(lane < 64, first[0], second[0]).astype(BF16)
                    gk = jnp.where(lane < 64, first[1], second[1]).astype(BF16)
                    packed[at, 256 + pair * 128 : 256 + (pair + 1) * 128] = gk
                    if pair == 0:
                        packed[at, 512:] = gv
                    else:
                        skipped[at, :] = gv
                    query_total[pair, span, :] += first[2] + second[2]

        for wide in range(1, blocks + 1):
            pl.when(width == wide)(partial(run, wide))
        return 0

    lax.fori_loop(0, blocks, attend, 0)

    def close(block, _):
        at = pl.ds(pl.multiple_of(block * BLOCK, BLOCK), BLOCK)
        for pair in range(2):
            packed[at, pair * 128 : (pair + 1) * 128] = (query_total[pair, at, :] * 0.125).astype(BF16)
        back[at, :] = (
            nt(packed[at, :256], query_weight[...])
            + nt(packed[at, 256:512], key_weight[...])
            + nt(packed[at, 512:], value_weight[...])
        ).astype(BF16)
        return 0

    lax.fori_loop(0, blocks, close, 0)
    weight_grad[:, :640] = tn(normed[...], packed[...]).astype(BF16)
    gain_grads[...] = jnp.zeros_like(gain_grads)

    for rows_ref, back_ref, skip_ref, which in (
        (own, back_own, skip_own, head),
        (other, back_other, skip_other, 1 - head),
    ):

        def give(step, _, rows_ref=rows_ref, back_ref=back_ref, skip_ref=skip_ref, which=which):
            at = pl.ds(pl.multiple_of(step * BLOCK, BLOCK), BLOCK)
            tile = which * (half // BLOCK) + step

            def put(count_here):
                g = load_grouped(lambda s: back[s, :], tile, total, count_here)
                k = load_grouped(lambda s: skipped[s, :], tile, total, count_here)
                if count_here > 1:
                    order = sorter(count_here, True)
                    g = nn(order, g).astype(BF16)
                    k = nn(order, k).astype(BF16)
                back_ref[at, :] = g
                skip_ref[at, :] = k

            for option in SLOT_OPTIONS:
                pl.when(count == option)(partial(put, option))
            hat, _s = normalized(rows_ref[at, :].astype(F32))
            g = back_ref[at, :].astype(F32)
            gain_grads[0:1, :] += jnp.sum(g * hat, axis=0, keepdims=True)
            gain_grads[1:2, :] += jnp.sum(g, axis=0, keepdims=True)
            return 0

        lax.fori_loop(0, half // BLOCK, give, 0)
    weight_grad[:, 640:] = as_columns([gain_grads[0:1, :], gain_grads[1:2, :]])


def backward_attention(
    info, own, other, grad_own, grad_other, query, keys, values, mixed, logsum, normed, wq, wk, wv
):
    half, width = own.shape
    total = 2 * half
    group = wq.shape[1] // 2
    outs = [
        ((width, 768), BF16),
        ((half, width), BF16),
        ((half, width), BF16),
        ((half, 128), BF16),
        ((half, 128), BF16),
    ]
    args = (own, other, grad_own, grad_other, query, keys, values, mixed, logsum, normed)
    return pl.pallas_call(
        backward_kernel,
        grid_spec=pltpu.PrefetchScalarGridSpec(
            num_scalar_prefetch=1,
            grid=(1,),
            in_specs=[whole(a.shape) for a in args]
            + [
                pl.BlockSpec((width, group), lambda i, s: (0, s[1])),
                pl.BlockSpec((width, group), lambda i, s: (0, s[1])),
                pl.BlockSpec((width, 128), lambda i, s: (0, s[1])),
            ],
            out_specs=[whole(s) for s, _ in outs],
            scratch_shapes=[
                pltpu.VMEM((8, width), F32),
                pltpu.VMEM((2, total, 128), BF16),
                pltpu.VMEM((2, 8, total), F32),
                pltpu.VMEM((2, total, 128), F32),
                pltpu.VMEM((total, 640), BF16),
                pltpu.VMEM((total, 128), BF16),
                pltpu.VMEM((total, width), BF16),
            ],
        ),
        out_shape=[jax.ShapeDtypeStruct(s, d) for s, d in outs],
        compiler_params=pltpu.CompilerParams(vmem_limit_bytes=60 * MIB),
        name="backward_attention",
    )(info, *args, wq, wk, wv)


def close_kernel(info, tokens, after_grad, back_own, back_other, gain, kept, arrived, result, skip_grad):
    head = info[1]

    def tile(step, _):
        at = pl.ds(pl.multiple_of(step * BLOCK, BLOCK), BLOCK)
        hat, scale = normalized(tokens[at, :].astype(F32))
        y = (back_own[at, :].astype(F32) + back_other[at, :].astype(F32)) * gain[...]
        result[at, :] = (
            after_grad[at, :]
            + scale
            * (
                y
                - jnp.mean(y, axis=-1, keepdims=True)
                - hat * jnp.mean(y * hat, axis=-1, keepdims=True)
            )
        ).astype(BF16)
        return 0

    lax.fori_loop(0, tokens.shape[0] // BLOCK, tile, 0)
    skip_grad[:, pl.ds(pl.multiple_of(head * 128, 128), 128)] = kept[...]
    skip_grad[:, pl.ds(pl.multiple_of((1 - head) * 128, 128), 128)] = arrived[...]


def close_rows(info, tokens, after_grad, back_own, back_other, gain, kept, arrived):
    args = (tokens, after_grad, back_own, back_other, gain, kept, arrived)
    half = tokens.shape[0]
    return pl.pallas_call(
        close_kernel,
        grid_spec=pltpu.PrefetchScalarGridSpec(
            num_scalar_prefetch=1,
            grid=(1,),
            in_specs=[whole(a.shape) for a in args],
            out_specs=[whole(tokens.shape), whole((half, 256))],
        ),
        out_shape=[
            jax.ShapeDtypeStruct(tokens.shape, BF16),
            jax.ShapeDtypeStruct((half, 256), BF16),
        ],
        compiler_params=pltpu.CompilerParams(vmem_limit_bytes=32 * MIB),
        name="close_rows",
    )(info, *args)


def swap_cores(array):
    return lax.ppermute(array, "head", [(0, 1), (1, 0)])


def half_of(array, which):
    rows = array.shape[0] // 2
    return lax.dynamic_slice_in_dim(array, which * rows, rows, 0)


def add_low(a, b):
    return (a.astype(F32) + b.astype(F32)).astype(BF16)


def swap_bit(array, bit):
    size = lax.axis_size("seq")
    return lax.ppermute(array, "seq", [(i, i ^ (1 << bit)) for i in range(size)])


def bit_of(bit):
    return (lax.axis_index("seq") >> bit) & 1


def join(mine, theirs, which):
    both = jnp.concatenate([mine, mine], axis=0)
    return lax.dynamic_update_slice_in_dim(both, theirs, (1 - which) * mine.shape[0], 0)


def seq_sum(chunks, first_bits):
    bits = lax.axis_size("seq").bit_length() - 1
    orders = [[(f + s) % min(3, bits) for s in range(min(3, bits))] + list(range(3, bits)) for f in first_bits]
    trail = [[] for _ in chunks]
    for stage in range(bits):
        after = []
        for chunk, order, path in zip(chunks, orders, trail):
            bit = order[stage]
            if chunk.shape[0] % 32 == 0:
                mine = bit_of(bit)
                path.append(bit)
                after.append(add_low(half_of(chunk, mine), swap_bit(half_of(chunk, 1 - mine), bit)))
            else:
                after.append(add_low(chunk, swap_bit(chunk, bit)))
        chunks = after
    while any(trail):
        for n, path in enumerate(trail):
            if path:
                bit = path.pop()
                chunks[n] = join(chunks[n], swap_bit(chunks[n], bit), bit_of(bit))
    return chunks


def on_device(
    tokens, first_values, cotangent, slot_count, seq_lengths, query_weight, key_weight, value_weight,
    mixing_weight, expand_weight, shrink_weight, expand_bias, before_gain, before_shift,
    middle_gain, middle_shift,
):
    head = lax.axis_index("head")
    info = jnp.stack([slot_count[0], head.astype(jnp.int32)])
    lengths = seq_lengths[0]
    row = lambda v: v.reshape(1, -1)

    other = swap_cores(tokens)
    skip_other = swap_cores(lax.dynamic_slice_in_dim(first_values, (1 - head) * 128, 128, 1))
    mixed_own, mixed_away, query, keys, values, mixed, logsum, normed = forward_attention(
        info, tokens, other, first_values, skip_other, query_weight, key_weight, value_weight,
        row(before_gain), row(before_shift),
    )
    mixed_other = swap_cores(mixed_away)
    output, after_grad, grad_own, grad_away, shrink_part, wide_part = row_part(
        info, lengths, tokens, mixed_own, mixed_other, cotangent, mixing_weight, expand_weight,
        shrink_weight, row(expand_bias), row(middle_gain), row(middle_shift),
    )
    grad_other = swap_cores(grad_away)
    shrink_half = add_low(half_of(shrink_part, head), swap_cores(half_of(shrink_part, 1 - head)))
    wide_half = add_low(half_of(wide_part, head), swap_cores(half_of(wide_part, 1 - head)))
    shrink_half, wide_half = seq_sum([shrink_half, wide_half], (0, 1))

    projection_part, back_own, back_away, skip_own, skip_away = backward_attention(
        info, tokens, other, grad_own, grad_other, query, keys, values, mixed, logsum, normed,
        query_weight, key_weight, value_weight,
    )
    back_other = swap_cores(back_away)
    skip_arrived = swap_cores(skip_away)
    (projection,) = seq_sum([projection_part], (0,))
    input_grad, skip_grad = close_rows(
        info, tokens, after_grad, back_own, back_other, row(before_gain), skip_own, skip_arrived
    )
    shrink_grad = join(shrink_half, swap_cores(shrink_half), head).astype(F32)
    wide = join(wide_half, swap_cores(wide_half), head)
    hidden, width = shrink_grad.shape
    expand_grad = wide[:, :hidden].astype(F32)
    mixing_grad = wide[:, hidden : hidden + width].astype(F32)
    tail = wide[:, hidden + width : hidden + width + 8].astype(F32)
    bias_grad = tail[:, : hidden // width].T.reshape(hidden)
    middle_gain_grad, middle_shift_grad = tail[:, 4], tail[:, 5]
    arrived = swap_cores(projection)
    low_head = jnp.where(head == 0, projection, arrived).astype(F32)
    high_head = jnp.where(head == 0, arrived, projection).astype(F32)
    query_grad = jnp.concatenate([low_head[:, :256], high_head[:, :256]], axis=1)
    key_grad = jnp.concatenate([low_head[:, 256:512], high_head[:, 256:512]], axis=1)
    value_grad = jnp.concatenate([low_head[:, 512:640], high_head[:, 512:640]], axis=1)
    edges = low_head[:, 640:642] + high_head[:, 640:642]
    return (
        output, input_grad, skip_grad, query_grad, key_grad, value_grad, mixing_grad, expand_grad,
        shrink_grad, bias_grad, edges[:, 0], edges[:, 1], middle_gain_grad, middle_shift_grad,
    )


def solution(mesh):
    rows = P(("seq", "head"), None)
    return jax.shard_map(
        on_device,
        mesh=mesh,
        in_specs=(rows, rows, rows, P("seq"), P("seq", None)) + (P(),) * 11,
        out_specs=(rows, rows, rows) + (P(),) * 11,
        check_vma=False,
    )
```

```python
from functools import partial
import math
import jax
import jax.numpy as jnp
from jax import lax
from jax.experimental import pallas as pl
from jax.experimental.pallas import tpu as pltpu
from jax.sharding import PartitionSpec as P

BLOCK = 256
SLOT_OPTIONS = (1, 2, 4, 8)
LOG2E = math.log2(math.e)
F32, BF16 = jnp.float32, jnp.bfloat16
MASKED = -1e30
EPS = 1e-05
MIB = 1 << 20
VMEM_MIB = 52


def nn(a, b):
    return lax.dot_general(a, b, (((1,), (0,)), ((), ())), preferred_element_type=F32)


def nt(a, b):
    return lax.dot_general(a, b, (((1,), (1,)), ((), ())), preferred_element_type=F32)


def tn(a, b):
    return lax.dot_general(a, b, (((0,), (0,)), ((), ())), preferred_element_type=F32)


def sorter(count, transposed=False):
    each = BLOCK // count
    grouped = lax.broadcasted_iota(jnp.int32, (BLOCK, BLOCK), 1 if transposed else 0)
    plain = lax.broadcasted_iota(jnp.int32, (BLOCK, BLOCK), 0 if transposed else 1)
    place = (plain & (count - 1)) * each + (plain >> (count.bit_length() - 1))
    return jnp.where(grouped == place, 1.0, 0.0).astype(BF16)


def store_grouped(write, values, tile, total, count):
    each = BLOCK // count
    for group in range(count):
        start = pl.multiple_of(group * (total // count) + tile * each, each)
        write(pl.ds(start, each), values[group * each : (group + 1) * each])


def load_grouped(read, tile, total, count):
    each = BLOCK // count
    parts = []
    for group in range(count):
        start = pl.multiple_of(group * (total // count) + tile * each, each)
        parts.append(read(pl.ds(start, each)))
    return parts[0] if count == 1 else jnp.concatenate(parts, axis=0)


def normalized(rows):
    average = jnp.mean(rows, axis=-1, keepdims=True)
    centred = rows - average
    spread = jnp.mean(centred * centred, axis=-1, keepdims=True)
    scale = lax.rsqrt(spread + EPS)
    return centred * scale, scale


def as_columns(vectors):
    stack = jnp.concatenate(vectors + [jnp.zeros((128 - len(vectors), vectors[0].shape[1]), F32)], axis=0)
    return jnp.transpose(stack).astype(BF16)


def forward_kernel(
    info, own_in, other_in, skip_own_in, skip_other_in, query_in, key_in, value_in, gain_in, shift_in,
    mixed_own_out, mixed_other_out, query_out, keys_out, saved_out, mixed_out, logsum_out, normed_out,
    own, other, skip_own, skip_other, query_weight, key_weight, value_weight,
    mixed_own, mixed_other, query, keys, saved, mixed, logsum, normed, values, gain, shift, semaphores,
):
    count, head = info[0], info[1]
    half = own.shape[0]
    total = 2 * half
    blocks = total // BLOCK
    cols = pl.ds(pl.multiple_of(head * 256, 256), 256)
    fresh_cols = pl.ds(pl.multiple_of(head * 128, 128), 128)
    mover = Mover(semaphores)
    mover.start(own_in, own, "own")
    mover.start(gain_in, gain, "gain")
    mover.start(shift_in, shift, "shift")
    mover.start(query_in.at[:, cols], query_weight, "q")
    mover.start(key_in.at[:, cols], key_weight, "k")
    mover.start(value_in.at[:, fresh_cols], value_weight, "v")
    mover.start(skip_own_in.at[:, fresh_cols], skip_own, "skip")
    mover.start(other_in, other, "other")
    mover.start(skip_other_in.at[:, fresh_cols], skip_other, "skip_other")
    values[:, :, 128:] = jnp.ones((2, total, 128), BF16)

    for rows_ref, skip_ref, which, needs in (
        (own, skip_own, head, ("own", "gain", "shift", "q", "k", "v", "skip")),
        (other, skip_other, 1 - head, ("other", "skip_other")),
    ):
        mover.wait(*needs)

        def project(step, _, rows_ref=rows_ref, skip_ref=skip_ref, which=which):
            at = pl.ds(pl.multiple_of(step * BLOCK, BLOCK), BLOCK)
            tile = which * (half // BLOCK) + step
            hat, _s = normalized(rows_ref[at, :].astype(F32))
            low = (hat * gain[...] + shift[...]).astype(BF16)
            skip = skip_ref[at, :]

            def put(count_here):
                rows, skipped = low, skip
                if count_here > 1:
                    order = sorter(count_here)
                    rows = nn(order, low).astype(BF16)
                    skipped = nn(order, skip).astype(BF16)
                q = nn(rows, query_weight[...]).astype(BF16)
                q = q * jnp.asarray(0.125, BF16)
                k = nn(rows, key_weight[...]).astype(BF16)
                f = nn(rows, value_weight[...]).astype(BF16)

                def put_in(ref, part, value):
                    def write(dst, piece):
                        if part is None:
                            ref[dst, :] = piece
                        else:
                            ref[part, dst, :128] = piece
                            if ref is values:
                                saved[part, dst, :] = piece

                    store_grouped(write, value, tile, total, count_here)

                put_in(normed, None, rows)
                put_in(query, 0, q[:, :128])
                put_in(query, 1, q[:, 128:])
                put_in(keys, 0, k[:, :128])
                put_in(keys, 1, k[:, 128:])
                put_in(values, 0, f)
                put_in(values, 1, skipped)

            for option in SLOT_OPTIONS:
                pl.when(count == option)(partial(put, option))
            return 0

        lax.fori_loop(0, half // BLOCK, project, 0)

    for source, target in ((query, query_out), (keys, keys_out), (saved, saved_out), (normed, normed_out)):
        mover.start(source, target)

    per_slot = blocks // count
    lane = lax.broadcasted_iota(jnp.int32, (1, 128), 1)
    tri = lax.broadcasted_iota(jnp.int32, (BLOCK, BLOCK), 1) <= lax.broadcasted_iota(
        jnp.int32, (BLOCK, BLOCK), 0
    )

    def attend(block, _):
        width = block % per_slot + 1
        here = pl.multiple_of(block * BLOCK, BLOCK)

        def run(wide):
            first = pl.multiple_of((block - (wide - 1)) * BLOCK, BLOCK)

            def score(h):
                pair, sub = h // 2, h % 2
                q = query[pair, pl.ds(here, BLOCK), :]
                qm = jnp.where((lane < 64) == (sub == 0), q, jnp.zeros_like(q))
                diag = nt(qm, keys[pair, pl.ds(here, BLOCK), :]) * LOG2E
                rest = None
                if wide > 1:
                    rest = nt(qm, keys[pair, pl.ds(first, (wide - 1) * BLOCK), :]) * LOG2E
                return diag, rest

            def finish(h, diag, rest):
                pair, sub = h // 2, h % 2
                diag = jnp.where(tri, diag, MASKED)
                top = jnp.max(diag, axis=1, keepdims=True)
                if wide > 1:
                    top = jnp.maximum(top, jnp.max(rest, axis=1, keepdims=True))
                raised = jnp.exp2(diag - top).astype(BF16)
                acc = nn(raised, values[pair, pl.ds(here, BLOCK), :])
                if wide > 1:
                    raised = jnp.exp2(rest - top).astype(BF16)
                    acc += nn(raised, values[pair, pl.ds(first, (wide - 1) * BLOCK), :])
                sums = acc[:, 128:]
                return acc[:, :128] / sums, jnp.transpose(top + jnp.log2(sums))[0:1, :]

            nxt = score(0)
            outs = []
            for h in range(4):
                cur = nxt
                if h < 3:
                    nxt = score(h + 1)
                outs.append(finish(h, *cur))
            for pair in range(2):
                mixed[pair, pl.ds(here, BLOCK), :] = jnp.where(lane < 64, outs[2*pair][0], outs[2*pair+1][0]).astype(BF16)
                for sub in range(2):
                    logsum[pair, sub : sub + 1, pl.ds(here, BLOCK)] = outs[2*pair+sub][1]

        for wide in range(1, blocks + 1):
            pl.when(width == wide)(partial(run, wide))
        return 0

    lax.fori_loop(0, blocks, attend, 0)
    mover.start(mixed, mixed_out)
    mover.start(logsum, logsum_out)

    for out_ref, target, which in (
        (mixed_other, mixed_other_out, 1 - head),
        (mixed_own, mixed_own_out, head),
    ):

        def give(step, _, out_ref=out_ref, which=which):
            at = pl.ds(pl.multiple_of(step * BLOCK, BLOCK), BLOCK)
            tile = which * (half // BLOCK) + step

            def put(count_here):
                for pair in range(2):
                    part = load_grouped(lambda s: mixed[pair, s, :], tile, total, count_here)
                    if count_here > 1:
                        part = nn(sorter(count_here, True), part).astype(BF16)
                    out_ref[at, pair * 128 : (pair + 1) * 128] = part

            for option in SLOT_OPTIONS:
                pl.when(count == option)(partial(put, option))
            return 0

        lax.fori_loop(0, half // BLOCK, give, 0)
        mover.start(out_ref, target)
    mover.wait_all()


class Mover:
    def __init__(self, semaphores):
        self.semaphores, self.used, self.open = semaphores, 0, {}

    def start(self, source, target, name=None):
        copy = pltpu.make_async_copy(source, target, self.semaphores.at[self.used])
        copy.start()
        self.open[self.used if name is None else name] = copy
        self.used += 1

    def wait(self, *names):
        for name in names:
            self.open.pop(name).wait()

    def wait_all(self):
        self.wait(*list(self.open))


def run_kernel(kernel, name, scalars, args, outs, scratch, moves, flops, aliases=None):
    smem = pl.BlockSpec(memory_space=pltpu.SMEM)
    large = pl.BlockSpec(memory_space=pl.ANY)
    size = lambda shape, dtype: math.prod(shape) * jnp.dtype(dtype).itemsize
    moved = sum(size(a.shape, a.dtype) for a in args) + sum(size(*o) for o in outs)
    return pl.pallas_call(
        kernel,
        in_specs=[smem] * len(scalars) + [large] * len(args),
        out_specs=[large] * len(outs),
        out_shape=[jax.ShapeDtypeStruct(*o) for o in outs],
        scratch_shapes=[pltpu.VMEM(*s) for s in scratch] + [pltpu.SemaphoreType.DMA((moves,))],
        input_output_aliases=aliases or {},
        cost_estimate=pl.CostEstimate(flops=flops, bytes_accessed=moved, transcendentals=0),
        compiler_params=pltpu.CompilerParams(vmem_limit_bytes=VMEM_MIB * MIB),
        name=name,
    )(*scalars, *args)


def forward_attention(info, own, other, skip_own, skip_other, wq, wk, wv, gain, shift):
    half, width = own.shape
    total = 2 * half
    group = wq.shape[1] // 2
    outs = [
        ((half, group), BF16),
        ((half, group), BF16),
        ((2, total, 128), BF16),
        ((2, total, 128), BF16),
        ((2, total, 128), BF16),
        ((2, total, 128), BF16),
        ((2, 8, total), F32),
        ((total, width), BF16),
    ]
    scratch = [
        ((half, width), BF16),
        ((half, width), BF16),
        ((half, 128), BF16),
        ((half, 128), BF16),
        ((width, group), BF16),
        ((width, group), BF16),
        ((width, 128), BF16),
        *outs,
        ((2, total, 256), BF16),
        (gain.shape, F32),
        (shift.shape, F32),
    ]
    return run_kernel(
        forward_kernel, "forward_attention", (info,),
        (own, other, skip_own, skip_other, wq, wk, wv, gain, shift), outs, scratch, 17, 10 * 10**9,
    )


COLS = 512
GELU_SLOPE = math.sqrt(2.0 / math.pi)
GELU_CUBE = 0.044715


def gelu_pair(v):
    square = v * v
    bend = jnp.tanh(v * (GELU_SLOPE + (GELU_SLOPE * GELU_CUBE) * square))
    front = 0.5 + 0.5 * bend
    slope = front + (0.5 * v) * (1.0 - bend * bend) * (
        GELU_SLOPE + (3.0 * GELU_SLOPE * GELU_CUBE) * square
    )
    return v * front, slope


def rows_kernel(
    info, lengths, tokens_in, mixed_own_in, mixed_other_in, cotangent_in, mixing_in, expand_in,
    shrink_in, bias_in, gain_in, shift_in,
    output_out, after_grad_out, send_own_out, send_other_out, grads_own_out, grads_other_out,
    tokens, mixed_own, mixed_other, cotangent, mixing_weight, expand_weight, shrink_weight,
    expand_bias, gain, shift, output, after_grad, send_own, send_other, grads_own, grads_other,
    bias_grad, gain_grads, active, slope, pre_grad, middle, out_grad, after_low, semaphores,
):
    mover = Mover(semaphores)
    for source, target, name in (
        (mixing_in, mixing_weight, "mixing"),
        (tokens_in, tokens, "tokens"),
        (mixed_own_in, mixed_own, "own"),
        (mixed_other_in, mixed_other, "other"),
        (gain_in, gain, "gain"),
        (shift_in, shift, "shift"),
        (bias_in, expand_bias, "bias"),
        (expand_in, expand_weight, "expand"),
        (shrink_in, shrink_weight, "shrink"),
        (cotangent_in, cotangent, "cotangent"),
    ):
        mover.start(source, target, name)
    count, head = info[0], info[1]
    half, width = tokens.shape
    hidden = expand_weight.shape[1]
    group = mixed_own.shape[1]
    shift_by = (
        (count >= 2).astype(jnp.int32)
        + (count >= 4).astype(jnp.int32)
        + (count >= 8).astype(jnp.int32)
    )
    here = pl.ds(pl.multiple_of(head * group, group), group)
    there = pl.ds(pl.multiple_of((1 - head) * group, group), group)
    bias_grad[...] = jnp.zeros_like(bias_grad)
    gain_grads[...] = jnp.zeros_like(gain_grads)
    mover.wait_all()

    def tile(step, _):
        at = pl.ds(pl.multiple_of(step * BLOCK, BLOCK), BLOCK)
        row = head * half + step * BLOCK + lax.broadcasted_iota(jnp.int32, (BLOCK, 1), 0)
        slot = row & (count - 1)
        limit = jnp.zeros_like(row)
        for s in range(lengths.shape[0]):
            limit = jnp.where(slot == s, lengths[s], limit)
        valid = (row >> shift_by) < limit
        after = (
            tokens[at, :].astype(F32)
            + nn(mixed_own[at, :], mixing_weight[here, :])
            + nn(mixed_other[at, :], mixing_weight[there, :])
        )
        hat, scale = normalized(after)
        low = (hat * gain[...] + shift[...]).astype(BF16)
        middle[at, :] = low
        for c in range(0, hidden, COLS):
            cs = slice(c, c + COLS)
            act, slo = gelu_pair(nn(low, expand_weight[:, cs]) + expand_bias[:, cs])
            active[at, cs] = act.astype(BF16)
            slope[:, cs] = slo
        grown = nn(active[at, :], shrink_weight[...])
        output[at, :] = jnp.where(valid, after + grown, 0.0).astype(BF16)
        grad_out = jnp.where(valid, cotangent[at, :].astype(F32), 0.0)
        grad_low = grad_out.astype(BF16)
        out_grad[at, :] = grad_low
        for c in range(0, hidden, COLS):
            cs = slice(c, c + COLS)
            g = nt(grad_low, shrink_weight[cs, :]) * slope[:, cs]
            bias_grad[0:1, cs] += jnp.sum(g, axis=0, keepdims=True)
            pre_grad[at, cs] = g.astype(BF16)
        g_middle = nt(pre_grad[at, :], expand_weight[...])
        gain_grads[0:1, :] += jnp.sum(g_middle * hat, axis=0, keepdims=True)
        gain_grads[1:2, :] += jnp.sum(g_middle, axis=0, keepdims=True)
        y = g_middle * gain[...]
        g_after = grad_out + scale * (
            y
            - jnp.mean(y, axis=-1, keepdims=True)
            - hat * jnp.mean(y * hat, axis=-1, keepdims=True)
        )
        after_grad[at, :] = g_after
        g_low = g_after.astype(BF16)
        after_low[at, :] = g_low
        send_own[at, :] = nt(g_low, mixing_weight[here, :]).astype(BF16)
        send_other[at, :] = nt(g_low, mixing_weight[there, :]).astype(BF16)
        return 0

    lax.fori_loop(0, half // BLOCK, tile, 0)

    for source, target in (
        (send_other, send_other_out),
        (send_own, send_own_out),
        (output, output_out),
        (after_grad, after_grad_out),
    ):
        mover.start(source, target)
    vectors = [bias_grad[0:1, c : c + width] for c in range(0, hidden, width)]
    vectors += [gain_grads[0:1, :], gain_grads[1:2, :]]
    vectors += [jnp.zeros_like(vectors[0])] * (16 - len(vectors))
    vectors = jnp.concatenate(vectors, axis=0).astype(BF16)
    for grads, target, mixed, which in (
        (grads_other, grads_other_out, mixed_other, 1 - head),
        (grads_own, grads_own_out, mixed_own, head),
    ):

        def weights(step, _, grads=grads, which=which):
            cs = pl.ds(pl.multiple_of((2 * which + step) * COLS, COLS), COLS)
            at = pl.multiple_of(step * COLS, COLS)
            grads[pl.ds(at, COLS), :] = tn(active[:, cs], out_grad[...]).astype(BF16)
            grads[pl.ds(2 * COLS + at, COLS), :] = tn(middle[...], pre_grad[:, cs]).astype(BF16)
            return 0

        lax.fori_loop(0, 2, weights, 0)
        last = 4 * COLS + group
        grads[4 * COLS : last, :] = tn(mixed[...], after_low[...]).astype(BF16)
        grads[last : last + 16, :] = vectors
        grads[last + 16 :, :] = jnp.zeros((112, width), BF16)
        mover.start(grads, target)
    mover.wait_all()


def row_part(info, lengths, tokens, mixed_own, mixed_other, cotangent, wo, we, ws, bias, gain, shift):
    half, width = tokens.shape
    hidden = we.shape[1]
    group = mixed_own.shape[1]
    outs = [
        ((half, width), BF16),
        ((half, width), F32),
        ((half, group), BF16),
        ((half, group), BF16),
        ((hidden + group + 128, width), BF16),
        ((hidden + group + 128, width), BF16),
    ]
    args = (tokens, mixed_own, mixed_other, cotangent, wo, we, ws, bias, gain, shift)
    scratch = [
        *[(a.shape, a.dtype) for a in args],
        *outs,
        ((8, hidden), F32),
        ((8, width), F32),
        ((half, hidden), BF16),
        ((BLOCK, hidden), F32),
        ((half, hidden), BF16),
        ((half, width), BF16),
        ((half, width), BF16),
        ((half, width), BF16),
    ]
    return run_kernel(
        rows_kernel, "row_part", (info, lengths), args, outs, scratch, 16, 15 * 10**9
    )


def arrange_gradient(count, head, grad_own, grad_other, mixed, grad, inner):
    half = grad_own.shape[0]
    total = 2 * half

    for rows_ref, which in ((grad_own, head), (grad_other, 1 - head)):

        def arrange(step, _, rows_ref=rows_ref, which=which):
            at = pl.ds(pl.multiple_of(step * BLOCK, BLOCK), BLOCK)
            tile = which * (half // BLOCK) + step
            rows = rows_ref[at, :]

            def put(count_here):
                value = rows
                if count_here > 1:
                    value = nn(sorter(count_here), rows).astype(BF16)
                for pair in range(2):

                    def write(dst, piece, pair=pair):
                        grad[pair, dst, :] = piece

                    store_grouped(
                        write, value[:, pair * 128 : (pair + 1) * 128], tile, total, count_here
                    )

            for option in SLOT_OPTIONS:
                pl.when(count == option)(partial(put, option))
            return 0

        lax.fori_loop(0, half // BLOCK, arrange, 0)

    def inners(block, _):
        at = pl.ds(pl.multiple_of(block * BLOCK, BLOCK), BLOCK)
        for pair in range(2):
            flipped = jnp.transpose(grad[pair, at, :].astype(F32) * mixed[pair, at, :].astype(F32))
            for sub in range(2):
                inner[pair, sub : sub + 1, at] = jnp.sum(
                    flipped[sub * 64 : (sub + 1) * 64], axis=0, keepdims=True
                )
        return 0

    lax.fori_loop(0, total // BLOCK, inners, 0)


def attend_blocks(count, first, last, query, keys, values, grad, logsum, inner, query_total, kept):
    blocks = first + query.shape[1] // BLOCK
    per_slot = blocks // count
    lane = lax.broadcasted_iota(jnp.int32, (1, 128), 1)
    tri = lax.broadcasted_iota(jnp.int32, (BLOCK, BLOCK), 0) <= lax.broadcasted_iota(
        jnp.int32, (BLOCK, BLOCK), 1
    )

    def attend(block, _):
        width = per_slot - block % per_slot

        def run(wide):
            here = pl.multiple_of((block - first) * BLOCK, BLOCK)
            span = pl.ds(here, wide * BLOCK)
            at = out = pl.ds(here, BLOCK)

            def score(h):
                pair, sub = h // 2, h % 2
                pick = (lane < 64) == (sub == 0)
                k, v = keys[pair, at, :], values[pair, at, :]
                k = jnp.where(pick, k, jnp.zeros_like(k))
                v = jnp.where(pick, v, jnp.zeros_like(v))
                return k, nt(k, query[pair, span, :]), nt(v, grad[pair, span, :])

            def finish(h, k, raw, grad_probs):
                pair, sub = h // 2, h % 2
                probs = jnp.exp2(raw * LOG2E - logsum[pair, sub : sub + 1, span])
                diag = jnp.where(tri, probs[:, :BLOCK], 0.0)
                probs = diag if wide == 1 else jnp.concatenate([diag, probs[:, BLOCK:]], axis=1)
                grad_scores = (probs * (grad_probs - inner[pair, sub : sub + 1, span])).astype(BF16)
                grad_value = nn(probs.astype(BF16), grad[pair, span, :])
                grad_key = nn(grad_scores, query[pair, span, :])
                return grad_value, grad_key, tn(grad_scores, k)

            ahead = score(0)
            done = []
            for h in range(4):
                now = ahead
                if h < 3:
                    ahead = score(h + 1)
                done.append(finish(h, *now))
                if h % 2:
                    pair = h // 2
                    one, two = done[h - 1], done[h]
                    kept[out, pair * 128 : (pair + 1) * 128] = jnp.where(
                        lane < 64, one[1], two[1]
                    ).astype(BF16)
                    kept[out, 256 + pair * 128 : 256 + (pair + 1) * 128] = jnp.where(
                        lane < 64, one[0], two[0]
                    ).astype(BF16)
                    query_total[pair, span, :] += one[2] + two[2]

        for wide in range(1, blocks - first + 1):
            pl.when(width == wide)(partial(run, wide))
        return 0

    lax.fori_loop(first, last, attend, 0)


def first_kernel(
    last, info, grad_own_in, grad_other_in, query_in, keys_in, values_in, mixed_in, logsum_in,
    grad_out, inner_out, query_total_out, kept_out,
    grad_own, grad_other, query, keys, values, mixed, logsum, grad, inner, query_total, kept, semaphores,
):
    mover = Mover(semaphores)
    rows = pl.ds(0, last * BLOCK)
    mover.start(grad_own_in, grad_own, "a")
    mover.start(grad_other_in, grad_other, "b")
    mover.start(mixed_in, mixed, "c")
    mover.start(query_in, query, "d")
    mover.start(keys_in.at[:, rows], keys, "e")
    mover.start(values_in.at[:, rows], values, "f")
    mover.start(logsum_in, logsum, "g")
    query_total[...] = jnp.zeros_like(query_total)
    mover.wait("a", "b", "c")
    arrange_gradient(info[0], info[1], grad_own, grad_other, mixed, grad, inner)
    mover.start(grad, grad_out)
    mover.start(inner, inner_out)
    mover.wait("d", "e", "f", "g")
    attend_blocks(info[0], 0, last, query, keys, values, grad, logsum, inner, query_total, kept)
    mover.start(query_total, query_total_out)
    mover.start(kept, kept_out)
    mover.wait_all()


def first_blocks(last, info, grad_own, grad_other, query, keys, values, mixed, logsum):
    total = query.shape[1]
    outs = [
        ((2, total, 128), BF16),
        ((2, 8, total), F32),
        ((2, total, 128), F32),
        ((last * BLOCK, 512), BF16),
    ]
    scratch = [
        (grad_own.shape, BF16),
        (grad_other.shape, BF16),
        (query.shape, BF16),
        ((2, last * BLOCK, 128), BF16),
        ((2, last * BLOCK, 128), BF16),
        (mixed.shape, BF16),
        (logsum.shape, F32),
        *outs,
    ]
    return run_kernel(
        partial(first_kernel, last), "first_blocks", (info,),
        (grad_own, grad_other, query, keys, values, mixed, logsum), outs, scratch, 11, 10**10,
    )


def fetch_blocks(mover, first, last, sources, targets):
    before, query, keys, values, grad, logsum, inner = sources
    total = query.shape[1]
    span, rows = pl.ds(first * BLOCK, total - first * BLOCK), pl.ds(first * BLOCK, (last - first) * BLOCK)
    for source, target in zip(
        (
            keys.at[:, rows], query.at[:, span], values.at[:, rows], grad.at[:, span],
            logsum.at[:, :, span], inner.at[:, :, span], before.at[:, span],
        ),
        targets,
    ):
        mover.start(source, target)


def next_kernel(first, last, info, *refs):
    sources, (query_total_out, kept_out), local, (kept, semaphores) = (
        refs[:7], refs[7:9], refs[9:16], refs[16:]
    )
    mover = Mover(semaphores)
    fetch_blocks(mover, first, last, sources, local)
    mover.wait_all()
    keys, query, values, grad, logsum, inner, query_total = local
    attend_blocks(
        info[0], first, last, query, keys, values, grad, logsum, inner, query_total, kept
    )
    total = sources[1].shape[1]
    span = pl.ds(first * BLOCK, total - first * BLOCK)
    mover.start(query_total, query_total_out.at[:, span])
    mover.start(kept, kept_out)
    mover.wait_all()


def local_blocks(first, last, total):
    rows, span = (last - first) * BLOCK, total - first * BLOCK
    return [
        ((2, rows, 128), BF16),
        ((2, span, 128), BF16),
        ((2, rows, 128), BF16),
        ((2, span, 128), BF16),
        ((2, 8, span), F32),
        ((2, 8, span), F32),
        ((2, span, 128), F32),
    ]


def next_blocks(first, last, info, before, query, keys, values, grad, logsum, inner):
    outs = [(before.shape, F32), (((last - first) * BLOCK, 512), BF16)]
    return run_kernel(
        partial(next_kernel, first, last), f"blocks_{first}", (info,),
        (before, query, keys, values, grad, logsum, inner), outs,
        local_blocks(first, last, query.shape[1]) + [outs[1]], 9, 5 * 10**9, {1: 0},
    )


def last_kernel(first, pieces, info, *refs):
    sources, refs = refs[:7], refs[7:]
    normed_in, gain_in, shift_in, query_in, key_in, value_in = refs[:6]
    kept_in, refs = refs[6 : 6 + pieces], refs[6 + pieces :]
    weight_grad_out, packed_out = refs[:2]
    local, refs = refs[2:9], refs[9:]
    kept, normed, gain, shift, query_weight, key_weight, value_weight, before, weight_grad, packed, semaphores = refs
    keys, query, values, grad, logsum, inner, query_total = local
    total = packed.shape[0]
    head = info[1]
    cols = pl.ds(pl.multiple_of(head * 256, 256), 256)
    fresh_cols = pl.ds(pl.multiple_of(head * 128, 128), 128)
    mover = Mover(semaphores)
    fetch_blocks(mover, first, total // BLOCK, sources, local)
    mover.start(sources[0].at[:, pl.ds(0, first * BLOCK)], before, "before")
    mover.start(normed_in, normed, "normed")
    mover.start(gain_in, gain, "gain")
    mover.start(shift_in, shift, "shift")
    mover.start(query_in.at[:, cols], query_weight, "q")
    mover.start(key_in.at[:, cols], key_weight, "k")
    mover.start(value_in.at[:, fresh_cols], value_weight, "v")
    row = 0
    for n, piece in enumerate(kept_in):
        mover.start(piece, packed.at[pl.ds(row, piece.shape[0]), pl.ds(256, 512)], f"p{n}")
        row += piece.shape[0]
    mover.wait(*range(7))
    attend_blocks(
        info[0], first, total // BLOCK, query, keys, values, grad, logsum, inner, query_total, kept
    )
    mover.wait_all()
    packed[row:, 256:] = kept[...]
    for pair in range(2):
        lanes = slice(pair * 128, (pair + 1) * 128)
        packed[:row, lanes] = (before[pair, :, :] * 0.125).astype(BF16)
        packed[row:, lanes] = (query_total[pair, :, :] * 0.125).astype(BF16)
    mover.start(packed, packed_out)
    ones = jnp.ones((8, total), BF16)
    gain_grad = jnp.zeros((gain.shape[1], 1), F32)
    shift_grad = jnp.zeros((gain.shape[1], 1), F32)
    gain_column = jnp.transpose(jnp.broadcast_to(gain[...], (128, gain.shape[1])))[:, :1]
    shift_column = jnp.transpose(jnp.broadcast_to(shift[...], (128, gain.shape[1])))[:, :1]
    for start, stop, weight in ((0, 256, query_weight), (256, 512, key_weight), (512, 640, value_weight)):
        part = packed[:, start:stop]
        product = tn(normed[...], part)
        sums = nn(ones, part)[0:1, :]
        weight_grad[:, start:stop] = product.astype(BF16)
        weight = weight[...].astype(F32)
        shift_grad += jnp.sum(weight * sums, axis=1, keepdims=True)
        gain_grad += jnp.sum(weight * (product - shift_column * sums), axis=1, keepdims=True)
    lane = lax.broadcasted_iota(jnp.int32, (1, 128), 1)
    edge = jnp.where(lane == 0, gain_grad / gain_column, jnp.where(lane == 1, shift_grad, 0.0))
    weight_grad[:, 640:] = edge.astype(BF16)
    mover.start(weight_grad, weight_grad_out)
    mover.wait_all()


def last_blocks(first, info, before, query, keys, values, grad, logsum, inner, normed, gain, shift, wq, wk, wv, kept):
    total, width = normed.shape
    outs = [((width, 768), BF16), ((total, 768), BF16)]
    scratch = local_blocks(first, total // BLOCK, total) + [
        ((total - first * BLOCK, 512), BF16),
        (normed.shape, BF16),
        (gain.shape, F32),
        (shift.shape, F32),
        ((width, 256), BF16),
        ((width, 256), BF16),
        ((width, 128), BF16),
        ((2, first * BLOCK, 128), F32),
        *outs,
    ]
    return run_kernel(
        partial(last_kernel, first, len(kept)), "last_blocks", (info,),
        (before, query, keys, values, grad, logsum, inner, normed, gain, shift, wq, wk, wv, *kept),
        outs, scratch, 16 + len(kept), 5 * 10**9,
    )


def back_kernel(
    info, packed_in, query_in, key_in, value_in, back_own_out, back_other_out, skip_own_out, skip_other_out,
    packed, query_weight, key_weight, value_weight, back_own, back_other, skip_own, skip_other, back, semaphores,
):
    count, head = info[0], info[1]
    total = packed.shape[0]
    half = total // 2
    cols = pl.ds(pl.multiple_of(head * 256, 256), 256)
    fresh_cols = pl.ds(pl.multiple_of(head * 128, 128), 128)
    mover = Mover(semaphores)
    mover.start(packed_in, packed)
    mover.start(query_in.at[:, cols], query_weight)
    mover.start(key_in.at[:, cols], key_weight)
    mover.start(value_in.at[:, fresh_cols], value_weight)
    mover.wait_all()

    def close(block, _):
        at = pl.ds(pl.multiple_of(block * BLOCK, BLOCK), BLOCK)
        back[at, :] = (
            nt(packed[at, :256], query_weight[...])
            + nt(packed[at, 256:512], key_weight[...])
            + nt(packed[at, 512:640], value_weight[...])
        ).astype(BF16)
        return 0

    lax.fori_loop(0, total // BLOCK, close, 0)

    for back_ref, skip_ref, back_out, skip_out, which in (
        (back_other, skip_other, back_other_out, skip_other_out, 1 - head),
        (back_own, skip_own, back_own_out, skip_own_out, head),
    ):

        def give(step, _, back_ref=back_ref, skip_ref=skip_ref, which=which):
            at = pl.ds(pl.multiple_of(step * BLOCK, BLOCK), BLOCK)
            tile = which * (half // BLOCK) + step

            def put(count_here):
                g = load_grouped(lambda s: back[s, :], tile, total, count_here)
                k = load_grouped(lambda s: packed[s, 640:], tile, total, count_here)
                if count_here > 1:
                    order = sorter(count_here, True)
                    g = nn(order, g).astype(BF16)
                    k = nn(order, k).astype(BF16)
                back_ref[at, :] = g
                skip_ref[at, :] = k

            for option in SLOT_OPTIONS:
                pl.when(count == option)(partial(put, option))
            return 0

        lax.fori_loop(0, half // BLOCK, give, 0)
        mover.start(back_ref, back_out)
        mover.start(skip_ref, skip_out)
    mover.wait_all()


def back_rows(info, packed, wq, wk, wv):
    total, width = packed.shape[0], wq.shape[0]
    half = total // 2
    outs = [((half, width), BF16), ((half, width), BF16), ((half, 128), BF16), ((half, 128), BF16)]
    scratch = [
        (packed.shape, BF16),
        ((width, 256), BF16),
        ((width, 256), BF16),
        ((width, 128), BF16),
        *outs,
        ((total, width), BF16),
    ]
    return run_kernel(
        back_kernel, "back_rows", (info,), (packed, wq, wk, wv), outs, scratch, 8, 2 * 10**9
    )


def close_kernel(
    info, tokens_in, after_grad_in, back_own_in, back_other_in, kept_in, arrived_in, gain_in,
    result_out, skip_out,
    tokens, after_grad, back_own, back_other, gain, result, skip_grad, semaphores,
):
    head = info[1]
    mover = Mover(semaphores)
    mover.start(gain_in, gain)
    mover.start(tokens_in, tokens)
    mover.start(after_grad_in, after_grad)
    mover.start(back_own_in, back_own)
    mover.start(back_other_in, back_other)
    mover.start(kept_in, skip_grad.at[:, pl.ds(pl.multiple_of(head * 128, 128), 128)])
    mover.start(arrived_in, skip_grad.at[:, pl.ds(pl.multiple_of((1 - head) * 128, 128), 128)])
    mover.wait_all()
    mover.start(skip_grad, skip_out)

    def tile(step, _):
        at = pl.ds(pl.multiple_of(step * BLOCK, BLOCK), BLOCK)
        hat, scale = normalized(tokens[at, :].astype(F32))
        y = (back_own[at, :].astype(F32) + back_other[at, :].astype(F32)) * gain[...]
        result[at, :] = (
            after_grad[at, :]
            + scale
            * (
                y
                - jnp.mean(y, axis=-1, keepdims=True)
                - hat * jnp.mean(y * hat, axis=-1, keepdims=True)
            )
        ).astype(BF16)
        return 0

    lax.fori_loop(0, tokens.shape[0] // BLOCK, tile, 0)
    mover.start(result, result_out)
    mover.wait_all()


def close_rows(info, tokens, after_grad, back_own, back_other, kept, arrived, gain):
    args = (tokens, after_grad, back_own, back_other, kept, arrived, gain)
    outs = [(tokens.shape, BF16), ((tokens.shape[0], 256), BF16)]
    scratch = [(a.shape, a.dtype) for a in args[:4]] + [(gain.shape, F32)] + outs
    return run_kernel(close_kernel, "close_rows", (info,), args, outs, scratch, 9, 10**8)


def unpack_kernel(
    info, mine_in, arrived_in, shrink_out, expand_out, mixing_out, bias_out, gain_out, shift_out,
    mine, arrived, wide, bias, gain, shift, semaphores,
):
    head = info[1]
    width = mine.shape[1]
    mover = Mover(semaphores)
    mover.start(mine_in, mine, "mine")
    mover.start(arrived_in, arrived, "arrived")
    for half, name, slot, which in ((mine, "mine", 0, head), (arrived, "arrived", 1, 1 - head)):
        mover.wait(name)
        for at in range(0, 2 * COLS, COLS):
            wide[slot, at : at + COLS, :] = half[at : at + COLS, :].astype(F32)
            row = pl.multiple_of(which * 2 * COLS + at, COLS)
            mover.start(wide.at[slot, pl.ds(at, COLS)], shrink_out.at[pl.ds(row, COLS)])
        for at in range(2 * COLS, 4 * COLS, COLS):
            wide[slot, at : at + COLS, :] = half[at : at + COLS, :].astype(F32)
            col = pl.multiple_of(which * 2 * COLS + at - 2 * COLS, COLS)
            mover.start(wide.at[slot, pl.ds(at, COLS)], expand_out.at[:, pl.ds(col, COLS)])
        top = 4 * COLS + mixing_out.shape[0] // 2
        wide[slot, 4 * COLS : top + 16, :] = half[4 * COLS : top + 16, :].astype(F32)
        row = pl.multiple_of(which * (top - 4 * COLS), 256)
        mover.start(wide.at[slot, pl.ds(4 * COLS, top - 4 * COLS)], mixing_out.at[pl.ds(row, top - 4 * COLS)])
    vectors = wide[head, top : top + 8, :]
    for n in range(4):
        bias[:, n * width : (n + 1) * width] = vectors[n : n + 1]
    gain[...] = vectors[4:5]
    shift[...] = vectors[5:6]
    for source, target in ((bias, bias_out), (gain, gain_out), (shift, shift_out)):
        mover.start(source, target)
    mover.wait_all()


def unpack_grads(info, mine, arrived):
    rows, width = mine.shape
    hidden = 4 * COLS
    outs = [((hidden, width), F32), ((width, hidden), F32), ((width, width), F32)]
    small = [((1, hidden), F32), ((1, width), F32), ((1, width), F32)]
    outs += small
    scratch = [(mine.shape, BF16), (mine.shape, BF16), ((2, rows, width), F32)] + small
    return run_kernel(unpack_kernel, "unpack_grads", (info,), (mine, arrived), outs, scratch, 15, 10**8)


def split_kernel(
    info, mine_in, arrived_in, query_out, key_out, value_out, gain_out, shift_out,
    mine, arrived, query, key, value, gain, shift, semaphores,
):
    head = info[1]
    mover = Mover(semaphores)
    mover.start(mine_in, mine)
    mover.start(arrived_in, arrived)
    mover.wait_all()
    for half, which in ((mine, head), (arrived, 1 - head)):
        for target, wide, at in ((query, 256, 0), (key, 256, 256), (value, 128, 512)):
            cols = pl.ds(pl.multiple_of(which * wide, 128), wide)
            target[:, cols] = half[:, at : at + wide].astype(F32)
    for source, target in ((query, query_out), (key, key_out), (value, value_out)):
        mover.start(source, target)
    edges = jnp.transpose(mine[:, 640:].astype(F32) + arrived[:, 640:].astype(F32))
    gain[...] = edges[0:1]
    shift[...] = edges[1:2]
    mover.start(gain, gain_out)
    mover.start(shift, shift_out)
    mover.wait_all()


def split_projection(info, mine, arrived):
    width = mine.shape[0]
    outs = [((width, 512), F32), ((width, 512), F32), ((width, 256), F32), ((1, width), F32), ((1, width), F32)]
    scratch = [(mine.shape, BF16), (mine.shape, BF16)] + outs
    return run_kernel(split_kernel, "split_projection", (info,), (mine, arrived), outs, scratch, 7, 10**8)


def swap_cores(array):
    return lax.ppermute(array, "head", [(0, 1), (1, 0)])


def half_of(array, which):
    rows = array.shape[0] // 2
    return lax.dynamic_slice_in_dim(array, which * rows, rows, 0)


def add_low(a, b):
    return (a.astype(F32) + b.astype(F32)).astype(BF16)


def join(mine, theirs, which):
    both = jnp.concatenate([mine, mine], axis=0)
    return lax.dynamic_update_slice_in_dim(both, theirs, (1 - which) * mine.shape[0], 0)


def after_all(first, *rest):
    return lax.optimization_barrier((first, *rest))


class SeqSum:
    def __init__(self, mine, coming, orders):
        self.size = lax.axis_size("seq")
        bits = self.size.bit_length() - 1
        self.orders = [
            [b for b in order if b < bits] + [b for b in range(bits) if b not in order]
            for order in orders
        ]
        self.mine, self.coming, self.stage, self.bits, self.trail = mine, coming, 0, bits, []

    def which(self, stage):
        bit = jnp.where(lax.axis_index("head") == 0, self.orders[0][stage], self.orders[1][stage])
        return (lax.axis_index("seq") >> bit) & 1

    def swap(self, array, stage):
        pairs = []
        for i in range(self.size):
            for core in range(2):
                pairs.append((2 * i + core, 2 * (i ^ (1 << self.orders[core][stage])) + core))
        return lax.ppermute(array, ("seq", "head"), pairs)

    def added(self, which=None):
        parts = [a if which is None else half_of(a, which) for a in (self.mine, self.coming) if a is not None]
        return parts[0] if len(parts) == 1 else add_low(*parts)

    def ready(self):
        if self.stage < self.bits - 1 and self.mine.shape[0] % 32 == 0:
            which = self.which(self.stage)
            self.trail.append(self.stage)
            self.away, self.mine = self.added(1 - which), self.added(which)
        else:
            self.away = self.mine = self.added()

    def send(self):
        self.coming = self.swap(self.away, self.stage)
        self.stage += 1

    def finish(self):
        self.mine, self.coming = self.added(), None

    def call_back(self):
        self.back_stage = self.trail.pop()
        self.coming = self.swap(self.mine, self.back_stage)

    def fit(self):
        self.mine = join(self.mine, self.coming, self.which(self.back_stage))


ORDERS = ((0, 1, 2, 3), (1, 2, 3, 0))
PROJECTION_ORDERS = ((1, 0, 2, 3), (2, 1, 0, 3))
CUTS = (1, 3, 5, 8)


def on_device(
    tokens, first_values, cotangent, slot_count, seq_lengths, query_weight, key_weight, value_weight,
    mixing_weight, expand_weight, shrink_weight, expand_bias, before_gain, before_shift,
    middle_gain, middle_shift,
):
    head = lax.axis_index("head")
    info = jnp.stack([slot_count[0], head.astype(jnp.int32)])
    lengths = seq_lengths[0]
    row = lambda v: v.reshape(1, -1)

    other = swap_cores(tokens)
    skip_other = swap_cores(first_values)
    mixed_own, mixed_away, query, keys, values, mixed, logsum, normed = forward_attention(
        info, tokens, other, first_values, skip_other, query_weight, key_weight, value_weight,
        row(before_gain), row(before_shift),
    )
    mixed_other = swap_cores(mixed_away)
    output, after_grad, grad_own, grad_away, grads_own, grads_away = row_part(
        info, lengths, tokens, mixed_own, mixed_other, cotangent, mixing_weight, expand_weight,
        shrink_weight, row(expand_bias), row(middle_gain), row(middle_shift),
    )
    grad_other = swap_cores(grad_away)
    grad_other, grads_away = after_all(grad_other, grads_away)
    grads_come = swap_cores(grads_away)
    grad, inner, query_total, kept = first_blocks(
        CUTS[0], info, grad_own, grad_other, query, keys, values, mixed, logsum
    )
    pieces = [kept]
    query_total, grads_come = after_all(query_total, grads_come)
    sums = SeqSum(grads_own, grads_come, ORDERS)
    for first, last in zip(CUTS, CUTS[1:-1]):
        sums.ready()
        query_total, sums.away = after_all(query_total, sums.away)
        sums.send()
        query_total, kept = next_blocks(
            first, last, info, query_total, query, keys, values, grad, logsum, inner
        )
        pieces.append(kept)
        query_total, sums.coming = after_all(query_total, sums.coming)
    sums.ready()
    query_total, sums.away = after_all(query_total, sums.away)
    sums.send()
    projection_part, packed = last_blocks(
        CUTS[-2], info, query_total, query, keys, values, grad, logsum, inner, normed,
        row(before_gain), row(before_shift), query_weight, key_weight, value_weight, pieces,
    )
    projection = SeqSum(projection_part, None, PROJECTION_ORDERS)
    packed, sums.coming = after_all(packed, sums.coming)

    def both_ready():
        projection.ready()
        if sums.stage < sums.bits:
            sums.ready()
            return True
        return False

    more = both_ready()
    packed, projection.away, sums.away = after_all(packed, projection.away, sums.away)
    projection.send()
    if more:
        sums.send()
    back_own, back_away, skip_own, skip_away = back_rows(
        info, packed, query_weight, key_weight, value_weight
    )
    while sums.stage < sums.bits or projection.stage < projection.bits - 3:
        back_away, projection.coming, sums.coming = after_all(
            back_away, projection.coming, sums.coming
        )
        more = both_ready()
        projection.send()
        if more:
            sums.send()
    back_away, projection.coming, sums.coming = after_all(back_away, projection.coming, sums.coming)
    back_other, skip_arrived = swap_cores(back_away), swap_cores(skip_away)
    sums.finish()
    projection.ready()
    projection.send()
    sums.call_back()
    back_other, projection.coming, sums.coming = after_all(back_other, projection.coming, sums.coming)
    sums.fit()
    projection.ready()
    projection.send()
    sums.call_back()
    input_grad, skip_grad = close_rows(
        info, tokens, after_grad, back_own, back_other, skip_own, skip_arrived, row(before_gain)
    )
    input_grad, projection.coming, sums.coming = after_all(input_grad, projection.coming, sums.coming)
    sums.fit()
    projection.ready()
    projection.send()
    sums.call_back()
    projection.finish()
    while len(projection.trail) > 1:
        projection.call_back()
        projection.fit()
    projection.call_back()
    projection.coming, sums.coming = after_all(projection.coming, sums.coming)
    while True:
        sums.fit()
        if not sums.trail:
            break
        sums.call_back()
    projection.fit()
    sums_arrived, arrived = swap_cores(sums.mine), swap_cores(projection.mine)
    shrink_grad, expand_grad, mixing_grad, *sums_vectors = unpack_grads(info, sums.mine, sums_arrived)
    query_grad, key_grad, value_grad, *edges = split_projection(info, projection.mine, arrived)
    bias_grad, middle_gain_grad, middle_shift_grad = [v.reshape(-1) for v in sums_vectors]
    before_gain_grad, before_shift_grad = [v.reshape(-1) for v in edges]
    return (
        output, input_grad, skip_grad, query_grad, key_grad, value_grad, mixing_grad, expand_grad,
        shrink_grad, bias_grad, before_gain_grad, before_shift_grad, middle_gain_grad, middle_shift_grad,
    )


def solution(mesh):
    rows = P(("seq", "head"), None)
    return jax.shard_map(
        on_device,
        mesh=mesh,
        in_specs=(rows, rows, rows, P("seq"), P("seq", None)) + (P(),) * 11,
        out_specs=(rows, rows, rows) + (P(),) * 11,
        check_vma=False,
    )
```

```python
from functools import partial
import math
import jax
import jax.numpy as jnp
from jax import lax
from jax.experimental import pallas as pl
from jax.experimental.pallas import tpu as pltpu
from jax.sharding import PartitionSpec as P

BLOCK = 256
SLOT_OPTIONS = (1, 2, 4, 8)
LOG2E = math.log2(math.e)
F32, BF16 = jnp.float32, jnp.bfloat16
MASKED = -1e30
EPS = 1e-05
MIB = 1 << 20
VMEM_MIB, WHOLE_MIB = 52, 62


def nn(a, b):
    return lax.dot_general(a, b, (((1,), (0,)), ((), ())), preferred_element_type=F32)


def nt(a, b):
    return lax.dot_general(a, b, (((1,), (1,)), ((), ())), preferred_element_type=F32)


def tn(a, b):
    return lax.dot_general(a, b, (((0,), (0,)), ((), ())), preferred_element_type=F32)


def sorter(count, transposed=False):
    each = BLOCK // count
    grouped = lax.broadcasted_iota(jnp.int32, (BLOCK, BLOCK), 1 if transposed else 0)
    plain = lax.broadcasted_iota(jnp.int32, (BLOCK, BLOCK), 0 if transposed else 1)
    place = (plain & (count - 1)) * each + (plain >> (count.bit_length() - 1))
    return jnp.where(grouped == place, 1.0, 0.0).astype(BF16)


def store_grouped(write, values, tile, total, count):
    each = BLOCK // count
    for group in range(count):
        start = pl.multiple_of(group * (total // count) + tile * each, each)
        write(pl.ds(start, each), values[group * each : (group + 1) * each])


def load_grouped(read, tile, total, count):
    each = BLOCK // count
    parts = []
    for group in range(count):
        start = pl.multiple_of(group * (total // count) + tile * each, each)
        parts.append(read(pl.ds(start, each)))
    return parts[0] if count == 1 else jnp.concatenate(parts, axis=0)


def normalized(rows):
    average = jnp.mean(rows, axis=-1, keepdims=True)
    centred = rows - average
    spread = jnp.mean(centred * centred, axis=-1, keepdims=True)
    scale = lax.rsqrt(spread + EPS)
    return centred * scale, scale


def as_columns(vectors):
    stack = jnp.concatenate(vectors + [jnp.zeros((128 - len(vectors), vectors[0].shape[1]), F32)], axis=0)
    return jnp.transpose(stack).astype(BF16)


def forward_kernel(
    info, own_in, other_in, skip_own_in, skip_other_in, query_in, key_in, value_in, gain_in, shift_in,
    mixed_own_out, mixed_other_out, query_out, keys_out, saved_out, mixed_out, logsum_out, normed_out,
    own, other, skip_own, skip_other, query_weight, key_weight, value_weight,
    mixed_own, mixed_other, query, keys, saved, mixed, logsum, normed, values, gain, shift, semaphores,
):
    count, head = info[0], info[1]
    half = own.shape[0]
    total = 2 * half
    blocks = total // BLOCK
    cols = pl.ds(pl.multiple_of(head * 256, 256), 256)
    fresh_cols = pl.ds(pl.multiple_of(head * 128, 128), 128)
    mover = Mover(semaphores)
    mover.start(own_in, own, "own")
    mover.start(gain_in, gain, "gain")
    mover.start(shift_in, shift, "shift")
    mover.start(query_in.at[:, cols], query_weight, "q")
    mover.start(key_in.at[:, cols], key_weight, "k")
    mover.start(value_in.at[:, fresh_cols], value_weight, "v")
    mover.start(skip_own_in.at[:, fresh_cols], skip_own, "skip")
    mover.start(other_in, other, "other")
    mover.start(skip_other_in.at[:, fresh_cols], skip_other, "skip_other")
    values[:, :, 128:] = jnp.ones((2, total, 128), BF16)

    for rows_ref, skip_ref, which, needs in (
        (own, skip_own, head, ("own", "gain", "shift", "q", "k", "v", "skip")),
        (other, skip_other, 1 - head, ("other", "skip_other")),
    ):
        mover.wait(*needs)

        def project(step, _, rows_ref=rows_ref, skip_ref=skip_ref, which=which):
            at = pl.ds(pl.multiple_of(step * BLOCK, BLOCK), BLOCK)
            tile = which * (half // BLOCK) + step
            hat, _s = normalized(rows_ref[at, :].astype(F32))
            low = (hat * gain[...] + shift[...]).astype(BF16)
            skip = skip_ref[at, :]

            def put(count_here):
                rows, skipped = low, skip
                if count_here > 1:
                    order = sorter(count_here)
                    rows = nn(order, low).astype(BF16)
                    skipped = nn(order, skip).astype(BF16)
                q = nn(rows, query_weight[...]).astype(BF16)
                q = q * jnp.asarray(0.125, BF16)
                k = nn(rows, key_weight[...]).astype(BF16)
                f = nn(rows, value_weight[...]).astype(BF16)

                def put_in(ref, part, value):
                    def write(dst, piece):
                        if part is None:
                            ref[dst, :] = piece
                        else:
                            ref[part, dst, :128] = piece
                            if ref is values:
                                saved[part, dst, :] = piece

                    store_grouped(write, value, tile, total, count_here)

                put_in(normed, None, rows)
                put_in(query, 0, q[:, :128])
                put_in(query, 1, q[:, 128:])
                put_in(keys, 0, k[:, :128])
                put_in(keys, 1, k[:, 128:])
                put_in(values, 0, f)
                put_in(values, 1, skipped)

            for option in SLOT_OPTIONS:
                pl.when(count == option)(partial(put, option))
            return 0

        lax.fori_loop(0, half // BLOCK, project, 0)

    for source, target in ((query, query_out), (keys, keys_out), (saved, saved_out), (normed, normed_out)):
        mover.start(source, target)

    per_slot = blocks // count
    lane = lax.broadcasted_iota(jnp.int32, (1, 128), 1)
    tri = lax.broadcasted_iota(jnp.int32, (BLOCK, BLOCK), 1) <= lax.broadcasted_iota(
        jnp.int32, (BLOCK, BLOCK), 0
    )

    def attend(block, _):
        width = block % per_slot + 1
        here = pl.multiple_of(block * BLOCK, BLOCK)

        def run(wide):
            first = pl.multiple_of((block - (wide - 1)) * BLOCK, BLOCK)

            def score(h):
                pair, sub = h // 2, h % 2
                q = query[pair, pl.ds(here, BLOCK), :]
                qm = jnp.where((lane < 64) == (sub == 0), q, jnp.zeros_like(q))
                diag = nt(qm, keys[pair, pl.ds(here, BLOCK), :]) * LOG2E
                rest = None
                if wide > 1:
                    rest = nt(qm, keys[pair, pl.ds(first, (wide - 1) * BLOCK), :]) * LOG2E
                return diag, rest

            def finish(h, diag, rest):
                pair, sub = h // 2, h % 2
                diag = jnp.where(tri, diag, MASKED)
                top = jnp.max(diag, axis=1, keepdims=True)
                if wide > 1:
                    top = jnp.maximum(top, jnp.max(rest, axis=1, keepdims=True))
                raised = jnp.exp2(diag - top).astype(BF16)
                acc = nn(raised, values[pair, pl.ds(here, BLOCK), :])
                if wide > 1:
                    raised = jnp.exp2(rest - top).astype(BF16)
                    acc += nn(raised, values[pair, pl.ds(first, (wide - 1) * BLOCK), :])
                sums = acc[:, 128:]
                return acc[:, :128] / sums, jnp.transpose(top + jnp.log2(sums))[0:1, :]

            nxt = score(0)
            outs = []
            for h in range(4):
                cur = nxt
                if h < 3:
                    nxt = score(h + 1)
                outs.append(finish(h, *cur))
            for pair in range(2):
                mixed[pair, pl.ds(here, BLOCK), :] = jnp.where(lane < 64, outs[2*pair][0], outs[2*pair+1][0]).astype(BF16)
                for sub in range(2):
                    logsum[pair, sub : sub + 1, pl.ds(here, BLOCK)] = outs[2*pair+sub][1]

        for wide in range(1, blocks + 1):
            pl.when(width == wide)(partial(run, wide))
        return 0

    lax.fori_loop(0, blocks, attend, 0)
    mover.start(mixed, mixed_out)
    mover.start(logsum, logsum_out)

    for out_ref, target, which in (
        (mixed_other, mixed_other_out, 1 - head),
        (mixed_own, mixed_own_out, head),
    ):

        def give(step, _, out_ref=out_ref, which=which):
            at = pl.ds(pl.multiple_of(step * BLOCK, BLOCK), BLOCK)
            tile = which * (half // BLOCK) + step

            def put(count_here):
                for pair in range(2):
                    part = load_grouped(lambda s: mixed[pair, s, :], tile, total, count_here)
                    if count_here > 1:
                        part = nn(sorter(count_here, True), part).astype(BF16)
                    out_ref[at, pair * 128 : (pair + 1) * 128] = part

            for option in SLOT_OPTIONS:
                pl.when(count == option)(partial(put, option))
            return 0

        lax.fori_loop(0, half // BLOCK, give, 0)
        mover.start(out_ref, target)
    mover.wait_all()


class Mover:
    def __init__(self, semaphores):
        self.semaphores, self.used, self.open = semaphores, 0, {}

    def start(self, source, target, name=None):
        copy = pltpu.make_async_copy(source, target, self.semaphores.at[self.used])
        copy.start()
        self.open[self.used if name is None else name] = copy
        self.used += 1

    def wait(self, *names):
        for name in names:
            self.open.pop(name).wait()

    def wait_all(self):
        self.wait(*list(self.open))


def run_kernel(kernel, name, scalars, args, outs, scratch, moves, flops, aliases=None, limit=VMEM_MIB):
    smem = pl.BlockSpec(memory_space=pltpu.SMEM)
    large = pl.BlockSpec(memory_space=pl.ANY)
    size = lambda shape, dtype: math.prod(shape) * jnp.dtype(dtype).itemsize
    moved = sum(size(a.shape, a.dtype) for a in args) + sum(size(*o) for o in outs)
    return pl.pallas_call(
        kernel,
        in_specs=[smem] * len(scalars) + [large] * len(args),
        out_specs=[large] * len(outs),
        out_shape=[jax.ShapeDtypeStruct(*o) for o in outs],
        scratch_shapes=[pltpu.VMEM(*s) for s in scratch] + [pltpu.SemaphoreType.DMA((moves,))],
        input_output_aliases=aliases or {},
        cost_estimate=pl.CostEstimate(flops=flops, bytes_accessed=moved, transcendentals=0),
        compiler_params=pltpu.CompilerParams(vmem_limit_bytes=limit * MIB),
        name=name,
    )(*scalars, *args)


def forward_attention(info, own, other, skip_own, skip_other, wq, wk, wv, gain, shift):
    half, width = own.shape
    total = 2 * half
    group = wq.shape[1] // 2
    outs = [
        ((half, group), BF16),
        ((half, group), BF16),
        ((2, total, 128), BF16),
        ((2, total, 128), BF16),
        ((2, total, 128), BF16),
        ((2, total, 128), BF16),
        ((2, 8, total), F32),
        ((total, width), BF16),
    ]
    scratch = [
        ((half, width), BF16),
        ((half, width), BF16),
        ((half, 128), BF16),
        ((half, 128), BF16),
        ((width, group), BF16),
        ((width, group), BF16),
        ((width, 128), BF16),
        *outs,
        ((2, total, 256), BF16),
        (gain.shape, F32),
        (shift.shape, F32),
    ]
    return run_kernel(
        forward_kernel, "forward_attention", (info,),
        (own, other, skip_own, skip_other, wq, wk, wv, gain, shift), outs, scratch, 17, 10 * 10**9,
        limit=WHOLE_MIB,
    )


COLS = 512
TILE, PART = 512, 256
GELU_SLOPE = math.sqrt(2.0 / math.pi)
GELU_CUBE = 0.044715


def gelu_pair(v):
    square = v * v
    bend = jnp.tanh(v * (GELU_SLOPE + (GELU_SLOPE * GELU_CUBE) * square))
    front = 0.5 + 0.5 * bend
    slope = front + (0.5 * v) * (1.0 - bend * bend) * (
        GELU_SLOPE + (3.0 * GELU_SLOPE * GELU_CUBE) * square
    )
    return v * front, slope


def rows_kernel(
    info, lengths, tokens_in, mixed_own_in, mixed_other_in, cotangent_in, mixing_in, expand_in,
    shrink_in, bias_in, gain_in, shift_in,
    output_out, after_grad_out, send_own_out, send_other_out,
    own_stay_out, own_away_out, other_stay_out, other_away_out,
    tokens, mixed_own, mixed_other, cotangent, mixing_weight, expand_weight, shrink_weight,
    expand_bias, gain, shift, output, after_grad, send_own, send_other, grads_own, grads_other,
    bias_grad, gain_grads, active, pre_grad, middle, out_grad, after_low, semaphores,
):
    mover = Mover(semaphores)
    for source, target, name in (
        (mixing_in, mixing_weight, "mixing"),
        (tokens_in, tokens, "tokens"),
        (mixed_own_in, mixed_own, "own"),
        (mixed_other_in, mixed_other, "other"),
        (gain_in, gain, "gain"),
        (shift_in, shift, "shift"),
        (bias_in, expand_bias, "bias"),
        (expand_in, expand_weight, "expand"),
        (shrink_in, shrink_weight, "shrink"),
        (cotangent_in, cotangent, "cotangent"),
    ):
        mover.start(source, target, name)
    count, head = info[0], info[1]
    half, width = tokens.shape
    hidden = expand_weight.shape[1]
    group = mixed_own.shape[1]
    shift_by = (
        (count >= 2).astype(jnp.int32)
        + (count >= 4).astype(jnp.int32)
        + (count >= 8).astype(jnp.int32)
    )
    here = pl.ds(pl.multiple_of(head * group, group), group)
    there = pl.ds(pl.multiple_of((1 - head) * group, group), group)
    bias_grad[...] = jnp.zeros_like(bias_grad)
    gain_grads[...] = jnp.zeros_like(gain_grads)
    mover.wait("mixing", "tokens", "own", "other", "gain", "shift", "bias")

    def tile(step, _):
        at = pl.ds(pl.multiple_of(step * TILE, TILE), TILE)
        row = head * half + step * TILE + lax.broadcasted_iota(jnp.int32, (TILE, 1), 0)
        slot = row & (count - 1)
        limit = jnp.zeros_like(row)
        for s in range(lengths.shape[0]):
            limit = jnp.where(slot == s, lengths[s], limit)
        valid = (row >> shift_by) < limit

        def first_wait(*names):
            pl.when(step == 0)(lambda: mover.wait(*names))

        after = (
            tokens[at, :].astype(F32)
            + nn(mixed_own[at, :], mixing_weight[here, :])
            + nn(mixed_other[at, :], mixing_weight[there, :])
        )
        hat, scale = normalized(after)
        low = (hat * gain[...] + shift[...]).astype(BF16)
        middle[at, :] = low
        first_wait("expand", "shrink", "cotangent")
        grad_out = jnp.where(valid, cotangent[at, :].astype(F32), 0.0)
        grad_low = grad_out.astype(BF16)
        out_grad[at, :] = grad_low

        def products(c):
            cs = slice(c, c + PART)
            return nn(low, expand_weight[:, cs]), nt(grad_low, shrink_weight[cs, :])

        ahead = products(0)
        for c in range(0, hidden, PART):
            cs = slice(c, c + PART)
            now = ahead
            if c + PART < hidden:
                ahead = products(c + PART)
            act, slope = gelu_pair(now[0] + expand_bias[:, cs])
            active[at, cs] = act.astype(BF16)
            g = now[1] * slope
            bias_grad[0:1, cs] += jnp.sum(g, axis=0, keepdims=True)
            pre_grad[at, cs] = g.astype(BF16)
        g_middle = nt(pre_grad[at, :], expand_weight[...])
        grown = nn(active[at, :], shrink_weight[...])
        gain_grads[0:1, :] += jnp.sum(g_middle * hat, axis=0, keepdims=True)
        gain_grads[1:2, :] += jnp.sum(g_middle, axis=0, keepdims=True)
        y = g_middle * gain[...]
        g_after = grad_out + scale * (
            y
            - jnp.mean(y, axis=-1, keepdims=True)
            - hat * jnp.mean(y * hat, axis=-1, keepdims=True)
        )
        after_grad[at, :] = g_after
        g_low = g_after.astype(BF16)
        after_low[at, :] = g_low
        output[at, :] = jnp.where(valid, after + grown, 0.0).astype(BF16)
        send_own[at, :] = nt(g_low, mixing_weight[here, :]).astype(BF16)
        send_other[at, :] = nt(g_low, mixing_weight[there, :]).astype(BF16)
        return 0

    lax.fori_loop(0, half // TILE, tile, 0)

    for source, target in (
        (send_other, send_other_out),
        (send_own, send_own_out),
        (output, output_out),
        (after_grad, after_grad_out),
    ):
        mover.start(source, target)
    vectors = [bias_grad[0:1, c : c + width] for c in range(0, hidden, width)]
    vectors += [gain_grads[0:1, :], gain_grads[1:2, :]]
    vectors += [jnp.zeros_like(vectors[0])] * (16 - len(vectors))
    vectors = jnp.concatenate(vectors, axis=0).astype(BF16)
    first_half = grads_own.shape[0] // 2
    for grads, stay_out, away_out, mixed, which, side in (
        (grads_other, other_stay_out, other_away_out, mixed_other, 1 - head, info[4]),
        (grads_own, own_stay_out, own_away_out, mixed_own, head, info[2]),
    ):
        stay = pl.ds(pl.multiple_of(side * first_half, 16), first_half)
        away = pl.ds(pl.multiple_of((1 - side) * first_half, 16), first_half)

        def weights(step, _, grads=grads, which=which):
            cs = pl.ds(pl.multiple_of((2 * which + step) * COLS, COLS), COLS)
            at = pl.multiple_of(step * COLS, COLS)
            grads[pl.ds(at, COLS), :] = tn(active[:, cs], out_grad[...]).astype(BF16)
            grads[pl.ds(2 * COLS + at, COLS), :] = tn(middle[...], pre_grad[:, cs]).astype(BF16)
            return 0

        lax.fori_loop(0, 2, weights, 0)
        last = 4 * COLS + group
        grads[4 * COLS : last, :] = tn(mixed[...], after_low[...]).astype(BF16)
        grads[last : last + 16, :] = vectors
        grads[last + 16 :, :] = jnp.zeros((112, width), BF16)
        mover.start(grads.at[away], away_out)
        mover.start(grads.at[stay], stay_out)
    mover.wait_all()


def row_part(info, lengths, tokens, mixed_own, mixed_other, cotangent, wo, we, ws, bias, gain, shift):
    half, width = tokens.shape
    hidden = we.shape[1]
    group = mixed_own.shape[1]
    outs = [
        ((half, width), BF16),
        ((half, width), F32),
        ((half, group), BF16),
        ((half, group), BF16),
        *[(((hidden + group + 128) // 2, width), BF16)] * 4,
    ]
    args = (tokens, mixed_own, mixed_other, cotangent, wo, we, ws, bias, gain, shift)
    scratch = [
        *[(a.shape, a.dtype) for a in args],
        *outs[:4],
        ((hidden + group + 128, width), BF16),
        ((hidden + group + 128, width), BF16),
        ((8, hidden), F32),
        ((8, width), F32),
        ((half, hidden), BF16),
        ((half, hidden), BF16),
        ((half, width), BF16),
        ((half, width), BF16),
        ((half, width), BF16),
    ]
    return run_kernel(
        rows_kernel, "row_part", (info, lengths), args, outs, scratch, 18, 15 * 10**9,
        limit=WHOLE_MIB,
    )


def arrange_gradient(count, head, grad_own, grad_other, mixed, grad, inner):
    half = grad_own.shape[0]
    total = 2 * half

    for rows_ref, which in ((grad_own, head), (grad_other, 1 - head)):

        def arrange(step, _, rows_ref=rows_ref, which=which):
            at = pl.ds(pl.multiple_of(step * BLOCK, BLOCK), BLOCK)
            tile = which * (half // BLOCK) + step
            rows = rows_ref[at, :]

            def put(count_here):
                value = rows
                if count_here > 1:
                    value = nn(sorter(count_here), rows).astype(BF16)
                for pair in range(2):

                    def write(dst, piece, pair=pair):
                        grad[pair, dst, :] = piece

                    store_grouped(
                        write, value[:, pair * 128 : (pair + 1) * 128], tile, total, count_here
                    )

            for option in SLOT_OPTIONS:
                pl.when(count == option)(partial(put, option))
            return 0

        lax.fori_loop(0, half // BLOCK, arrange, 0)

    def inners(block, _):
        at = pl.ds(pl.multiple_of(block * BLOCK, BLOCK), BLOCK)
        for pair in range(2):
            flipped = jnp.transpose(grad[pair, at, :].astype(F32) * mixed[pair, at, :].astype(F32))
            for sub in range(2):
                inner[pair, sub : sub + 1, at] = jnp.sum(
                    flipped[sub * 64 : (sub + 1) * 64], axis=0, keepdims=True
                )
        return 0

    lax.fori_loop(0, total // BLOCK, inners, 0)


def attend_blocks(
    count, first, last, query, keys, values, grad, logsum, inner, query_total, kept, key_sums, value_sums
):
    blocks = first + query.shape[1] // BLOCK
    per_slot = blocks // count
    lane = lax.broadcasted_iota(jnp.int32, (1, 128), 1)
    tri = lax.broadcasted_iota(jnp.int32, (BLOCK, BLOCK), 0) <= lax.broadcasted_iota(
        jnp.int32, (BLOCK, BLOCK), 1
    )

    def attend(block, _):
        more = per_slot - block % per_slot - 1
        here = pl.multiple_of((block - first) * BLOCK, BLOCK)
        at = pl.ds(here, BLOCK)

        def part(start, size, diagonal):
            span = pl.ds(pl.multiple_of(start, BLOCK), size)

            def score(h):
                pair, sub = h // 2, h % 2
                pick = (lane < 64) == (sub == 0)
                k, v = keys[pair, at, :], values[pair, at, :]
                k = jnp.where(pick, k, jnp.zeros_like(k))
                v = jnp.where(pick, v, jnp.zeros_like(v))
                return k, nt(k, query[pair, span, :]), nt(v, grad[pair, span, :])

            def finish(h, k, raw, grad_probs):
                pair, sub = h // 2, h % 2
                probs = jnp.exp2(raw * LOG2E - logsum[pair, sub : sub + 1, span])
                if diagonal:
                    probs = jnp.where(tri, probs, 0.0)
                grad_scores = (probs * (grad_probs - inner[pair, sub : sub + 1, span])).astype(BF16)
                grad_value = nn(probs.astype(BF16), grad[pair, span, :])
                grad_key = nn(grad_scores, query[pair, span, :])
                if diagonal:
                    value_sums[h], key_sums[h] = grad_value, grad_key
                else:
                    value_sums[h] += grad_value
                    key_sums[h] += grad_key
                return tn(grad_scores, k)

            ahead = score(0)
            done = []
            for h in range(4):
                now = ahead
                if h < 3:
                    ahead = score(h + 1)
                done.append(finish(h, *now))
                if h % 2:
                    query_total[h // 2, span, :] += done[h - 1] + done[h]

        part(here, BLOCK, True)

        def two(n, _):
            part(here + BLOCK + n * (2 * BLOCK), 2 * BLOCK, False)
            return 0

        lax.fori_loop(0, more // 2, two, 0)

        @pl.when(more % 2 == 1)
        def _():
            part(here + more * BLOCK, BLOCK, False)

        for pair in range(2):
            for start, sums in ((0, key_sums), (256, value_sums)):
                kept[at, start + pair * 128 : start + (pair + 1) * 128] = jnp.where(
                    lane < 64, sums[2 * pair], sums[2 * pair + 1]
                ).astype(BF16)
        return 0

    lax.fori_loop(first, last, attend, 0)


def arrange_kernel(
    info, grad_own_in, grad_other_in, mixed_in, grad_out, inner_out,
    grad_own, grad_other, mixed, grad, inner, semaphores,
):
    mover = Mover(semaphores)
    for source, target in ((grad_own_in, grad_own), (grad_other_in, grad_other), (mixed_in, mixed)):
        mover.start(source, target)
    mover.wait_all()
    arrange_gradient(info[0], info[1], grad_own, grad_other, mixed, grad, inner)
    mover.start(grad, grad_out)
    mover.start(inner, inner_out)
    mover.wait_all()


def arrange_rows(info, grad_own, grad_other, mixed):
    total = mixed.shape[1]
    outs = [((2, total, 128), BF16), ((2, 8, total), F32)]
    args = (grad_own, grad_other, mixed)
    scratch = [(a.shape, BF16) for a in args] + outs
    return run_kernel(arrange_kernel, "arrange_rows", (info,), args, outs, scratch, 5, 10**8)


def fetch_blocks(mover, first, last, sources, targets):
    query, keys, values, grad, logsum, inner, *before = sources
    total = query.shape[1]
    span, rows = pl.ds(first * BLOCK, total - first * BLOCK), pl.ds(first * BLOCK, (last - first) * BLOCK)
    for source, target in zip(
        (
            keys.at[:, rows], query.at[:, span], values.at[:, rows], grad.at[:, span],
            logsum.at[:, :, span], inner.at[:, :, span], *[b.at[:, span] for b in before],
        ),
        targets,
    ):
        mover.start(source, target)


def next_kernel(first, last, info, *refs):
    count = 7 if first else 6
    sources, (query_total_out, kept_out), local, (key_sums, value_sums, kept, semaphores) = (
        refs[:count], refs[count : count + 2], refs[count + 2 : count + 9], refs[count + 9 :]
    )
    mover = Mover(semaphores)
    fetch_blocks(mover, first, last, sources, local)
    keys, query, values, grad, logsum, inner, query_total = local
    if not first:
        query_total[...] = jnp.zeros_like(query_total)
    mover.wait_all()
    attend_blocks(
        info[0], first, last, query, keys, values, grad, logsum, inner, query_total, kept,
        key_sums, value_sums,
    )
    total = sources[0].shape[1]
    span = pl.ds(first * BLOCK, total - first * BLOCK)
    mover.start(query_total, query_total_out.at[:, span])
    mover.start(kept, kept_out)
    mover.wait_all()


def local_blocks(first, last, total):
    rows, span = (last - first) * BLOCK, total - first * BLOCK
    return [
        ((2, rows, 128), BF16),
        ((2, span, 128), BF16),
        ((2, rows, 128), BF16),
        ((2, span, 128), BF16),
        ((2, 8, span), F32),
        ((2, 8, span), F32),
        ((2, span, 128), F32),
        ((4, BLOCK, 128), F32),
        ((4, BLOCK, 128), F32),
    ]


def next_blocks(first, last, info, before, query, keys, values, grad, logsum, inner):
    outs = [(query.shape, F32), (((last - first) * BLOCK, 512), BF16)]
    args = (query, keys, values, grad, logsum, inner) + ((before,) if first else ())
    return run_kernel(
        partial(next_kernel, first, last), f"blocks_{first}", (info,), args, outs,
        local_blocks(first, last, query.shape[1]) + [outs[1]], 9, 5 * 10**9, {7: 0} if first else {},
    )


def last_kernel(first, pieces, info, *refs):
    sources, refs = refs[:7], refs[7:]
    normed_in, gain_in, shift_in, query_in, key_in, value_in = refs[:6]
    kept_in, refs = refs[6 : 6 + pieces], refs[6 + pieces :]
    stay_out, away_out, packed_out = refs[:3]
    local, (key_sums, value_sums, *refs) = refs[3:10], refs[10:]
    kept, normed, gain, shift, query_weight, key_weight, value_weight, before, weight_grad, packed, semaphores = refs
    keys, query, values, grad, logsum, inner, query_total = local
    total = packed.shape[0]
    head = info[1]
    cols = pl.ds(pl.multiple_of(head * 256, 256), 256)
    fresh_cols = pl.ds(pl.multiple_of(head * 128, 128), 128)
    mover = Mover(semaphores)
    fetch_blocks(mover, first, total // BLOCK, sources, local)
    mover.start(sources[6].at[:, pl.ds(0, first * BLOCK)], before, "before")
    mover.start(normed_in, normed, "normed")
    mover.start(gain_in, gain, "gain")
    mover.start(shift_in, shift, "shift")
    mover.start(query_in.at[:, cols], query_weight, "q")
    mover.start(key_in.at[:, cols], key_weight, "k")
    mover.start(value_in.at[:, fresh_cols], value_weight, "v")
    row = 0
    for n, piece in enumerate(kept_in):
        mover.start(piece, packed.at[pl.ds(row, piece.shape[0]), pl.ds(256, 512)], f"p{n}")
        row += piece.shape[0]
    mover.wait(*range(7))
    attend_blocks(
        info[0], first, total // BLOCK, query, keys, values, grad, logsum, inner, query_total, kept,
        key_sums, value_sums,
    )
    mover.wait_all()
    packed[row:, 256:] = kept[...]
    for pair in range(2):
        lanes = slice(pair * 128, (pair + 1) * 128)
        packed[:row, lanes] = (before[pair, :, :] * 0.125).astype(BF16)
        packed[row:, lanes] = (query_total[pair, :, :] * 0.125).astype(BF16)
    mover.start(packed, packed_out)
    ones = jnp.ones((8, total), BF16)
    gain_grad = jnp.zeros((gain.shape[1], 1), F32)
    shift_grad = jnp.zeros((gain.shape[1], 1), F32)
    gain_column = jnp.transpose(jnp.broadcast_to(gain[...], (128, gain.shape[1])))[:, :1]
    shift_column = jnp.transpose(jnp.broadcast_to(shift[...], (128, gain.shape[1])))[:, :1]
    for start, stop, weight in ((0, 256, query_weight), (256, 512, key_weight), (512, 640, value_weight)):
        part = packed[:, start:stop]
        product = tn(normed[...], part)
        sums = nn(ones, part)[0:1, :]
        weight_grad[:, start:stop] = product.astype(BF16)
        weight = weight[...].astype(F32)
        shift_grad += jnp.sum(weight * sums, axis=1, keepdims=True)
        gain_grad += jnp.sum(weight * (product - shift_column * sums), axis=1, keepdims=True)
    lane = lax.broadcasted_iota(jnp.int32, (1, 128), 1)
    edge = jnp.where(lane == 0, gain_grad / gain_column, jnp.where(lane == 1, shift_grad, 0.0))
    weight_grad[:, 640:] = edge.astype(BF16)
    rows = weight_grad.shape[0] // 2
    mover.start(weight_grad.at[pl.ds(pl.multiple_of((1 - info[3]) * rows, 16), rows)], away_out)
    mover.start(weight_grad.at[pl.ds(pl.multiple_of(info[3] * rows, 16), rows)], stay_out)
    mover.wait_all()


def last_blocks(first, info, before, query, keys, values, grad, logsum, inner, normed, gain, shift, wq, wk, wv, kept):
    total, width = normed.shape
    outs = [((width // 2, 768), BF16), ((width // 2, 768), BF16), ((total, 768), BF16)]
    scratch = local_blocks(first, total // BLOCK, total) + [
        ((total - first * BLOCK, 512), BF16),
        (normed.shape, BF16),
        (gain.shape, F32),
        (shift.shape, F32),
        ((width, 256), BF16),
        ((width, 256), BF16),
        ((width, 128), BF16),
        ((2, first * BLOCK, 128), F32),
        ((width, 768), BF16),
        outs[2],
    ]
    return run_kernel(
        partial(last_kernel, first, len(kept)), "last_blocks", (info,),
        (query, keys, values, grad, logsum, inner, before, normed, gain, shift, wq, wk, wv, *kept),
        outs, scratch, 17 + len(kept), 5 * 10**9,
    )


def back_kernel(
    info, packed_in, query_in, key_in, value_in, back_own_out, back_other_out, skip_own_out, skip_other_out,
    packed, query_weight, key_weight, value_weight, back_own, back_other, skip_own, skip_other, back, semaphores,
):
    count, head = info[0], info[1]
    total = packed.shape[0]
    half = total // 2
    cols = pl.ds(pl.multiple_of(head * 256, 256), 256)
    fresh_cols = pl.ds(pl.multiple_of(head * 128, 128), 128)
    mover = Mover(semaphores)
    mover.start(packed_in, packed)
    mover.start(query_in.at[:, cols], query_weight)
    mover.start(key_in.at[:, cols], key_weight)
    mover.start(value_in.at[:, fresh_cols], value_weight)
    mover.wait_all()

    def close(block, _):
        at = pl.ds(pl.multiple_of(block * BLOCK, BLOCK), BLOCK)
        back[at, :] = (
            nt(packed[at, :256], query_weight[...])
            + nt(packed[at, 256:512], key_weight[...])
            + nt(packed[at, 512:640], value_weight[...])
        ).astype(BF16)
        return 0

    lax.fori_loop(0, total // BLOCK, close, 0)

    for back_ref, skip_ref, back_out, skip_out, which in (
        (back_other, skip_other, back_other_out, skip_other_out, 1 - head),
        (back_own, skip_own, back_own_out, skip_own_out, head),
    ):

        def give(step, _, back_ref=back_ref, skip_ref=skip_ref, which=which):
            at = pl.ds(pl.multiple_of(step * BLOCK, BLOCK), BLOCK)
            tile = which * (half // BLOCK) + step

            def put(count_here):
                g = load_grouped(lambda s: back[s, :], tile, total, count_here)
                k = load_grouped(lambda s: packed[s, 640:], tile, total, count_here)
                if count_here > 1:
                    order = sorter(count_here, True)
                    g = nn(order, g).astype(BF16)
                    k = nn(order, k).astype(BF16)
                back_ref[at, :] = g
                skip_ref[at, :] = k

            for option in SLOT_OPTIONS:
                pl.when(count == option)(partial(put, option))
            return 0

        lax.fori_loop(0, half // BLOCK, give, 0)
        mover.start(back_ref, back_out)
        mover.start(skip_ref, skip_out)
    mover.wait_all()


def back_rows(info, packed, wq, wk, wv):
    total, width = packed.shape[0], wq.shape[0]
    half = total // 2
    outs = [((half, width), BF16), ((half, width), BF16), ((half, 128), BF16), ((half, 128), BF16)]
    scratch = [
        (packed.shape, BF16),
        ((width, 256), BF16),
        ((width, 256), BF16),
        ((width, 128), BF16),
        *outs,
        ((total, width), BF16),
    ]
    return run_kernel(
        back_kernel, "back_rows", (info,), (packed, wq, wk, wv), outs, scratch, 8, 2 * 10**9
    )


def close_kernel(
    info, tokens_in, after_grad_in, back_own_in, back_other_in, kept_in, arrived_in, gain_in,
    result_out, skip_out,
    tokens, after_grad, back_own, back_other, gain, result, skip_grad, semaphores,
):
    head = info[1]
    mover = Mover(semaphores)
    mover.start(gain_in, gain)
    mover.start(tokens_in, tokens)
    mover.start(after_grad_in, after_grad)
    mover.start(back_own_in, back_own)
    mover.start(back_other_in, back_other)
    mover.start(kept_in, skip_grad.at[:, pl.ds(pl.multiple_of(head * 128, 128), 128)])
    mover.start(arrived_in, skip_grad.at[:, pl.ds(pl.multiple_of((1 - head) * 128, 128), 128)])
    mover.wait_all()
    mover.start(skip_grad, skip_out)

    def tile(step, _):
        at = pl.ds(pl.multiple_of(step * BLOCK, BLOCK), BLOCK)
        hat, scale = normalized(tokens[at, :].astype(F32))
        y = (back_own[at, :].astype(F32) + back_other[at, :].astype(F32)) * gain[...]
        result[at, :] = (
            after_grad[at, :]
            + scale
            * (
                y
                - jnp.mean(y, axis=-1, keepdims=True)
                - hat * jnp.mean(y * hat, axis=-1, keepdims=True)
            )
        ).astype(BF16)
        return 0

    lax.fori_loop(0, tokens.shape[0] // BLOCK, tile, 0)
    mover.start(result, result_out)
    mover.wait_all()


def close_rows(info, tokens, after_grad, back_own, back_other, kept, arrived, gain):
    args = (tokens, after_grad, back_own, back_other, kept, arrived, gain)
    outs = [(tokens.shape, BF16), ((tokens.shape[0], 256), BF16)]
    scratch = [(a.shape, a.dtype) for a in args[:4]] + [(gain.shape, F32)] + outs
    return run_kernel(close_kernel, "close_rows", (info,), args, outs, scratch, 9, 10**8)


def unpack_kernel(late, info, *refs):
    half_in, refs = refs[0], refs[1 + (6 if late else 0) :]
    shrink_out, expand_out, mixing_out, bias_out, gain_out, shift_out, half, wide, bias, gain, shift, semaphores = refs
    which = 1 - info[1] if late else info[1]
    width = half.shape[1]
    top = 4 * COLS + mixing_out.shape[0] // 2
    mover = Mover(semaphores)
    for at in range(0, 4 * COLS, COLS):
        mover.start(half_in.at[pl.ds(at, COLS)], half.at[pl.ds(at, COLS)], at)
    mover.start(half_in.at[pl.ds(4 * COLS, half.shape[0] - 4 * COLS)], half.at[pl.ds(4 * COLS, half.shape[0] - 4 * COLS)], "rest")
    for at in range(0, 4 * COLS, COLS):
        mover.wait(at)
        wide[at : at + COLS, :] = half[at : at + COLS, :].astype(F32)
        if at < 2 * COLS:
            row = pl.multiple_of(which * 2 * COLS + at, COLS)
            mover.start(wide.at[pl.ds(at, COLS)], shrink_out.at[pl.ds(row, COLS)])
        else:
            col = pl.multiple_of(which * 2 * COLS + at - 2 * COLS, COLS)
            mover.start(wide.at[pl.ds(at, COLS)], expand_out.at[:, pl.ds(col, COLS)])
    mover.wait("rest")
    wide[4 * COLS : top + 16, :] = half[4 * COLS : top + 16, :].astype(F32)
    row = pl.multiple_of(which * (top - 4 * COLS), 256)
    mover.start(wide.at[pl.ds(4 * COLS, top - 4 * COLS)], mixing_out.at[pl.ds(row, top - 4 * COLS)])
    mover.wait_all()

    @pl.when(which == 0)
    def _():
        vectors = wide[top : top + 8, :]
        for n in range(4):
            bias[:, n * width : (n + 1) * width] = vectors[n : n + 1]
        gain[...] = vectors[4:5]
        shift[...] = vectors[5:6]
        small = Mover(semaphores)
        for source, target in ((bias, bias_out), (gain, gain_out), (shift, shift_out)):
            small.start(source, target)
        small.wait_all()


def unpack_half(info, half, before=()):
    rows, width = half.shape
    hidden = 4 * COLS
    outs = [((hidden, width), F32), ((width, hidden), F32), ((width, width), F32)]
    small = [((1, hidden), F32), ((1, width), F32), ((1, width), F32)]
    scratch = [(half.shape, BF16), ((rows, width), F32)] + small
    return run_kernel(
        partial(unpack_kernel, bool(before)), "unpack_late" if before else "unpack_half", (info,),
        (half, *before), outs + small, scratch, 10, 10**8, {2 + n: n for n in range(6)} if before else {},
        limit=20,
    )


def split_kernel(
    info, mine_in, arrived_in, query_out, key_out, value_out, gain_out, shift_out,
    mine, arrived, query, key, value, gain, shift, semaphores,
):
    head = info[1]
    mover = Mover(semaphores)
    mover.start(mine_in, mine)
    mover.start(arrived_in, arrived)
    mover.wait_all()
    for half, which in ((mine, head), (arrived, 1 - head)):
        for target, wide, at in ((query, 256, 0), (key, 256, 256), (value, 128, 512)):
            cols = pl.ds(pl.multiple_of(which * wide, 128), wide)
            target[:, cols] = half[:, at : at + wide].astype(F32)
    for source, target in ((query, query_out), (key, key_out), (value, value_out)):
        mover.start(source, target)
    edges = jnp.transpose(mine[:, 640:].astype(F32) + arrived[:, 640:].astype(F32))
    gain[...] = edges[0:1]
    shift[...] = edges[1:2]
    mover.start(gain, gain_out)
    mover.start(shift, shift_out)
    mover.wait_all()


def split_projection(info, mine, arrived):
    width = mine.shape[0]
    outs = [((width, 512), F32), ((width, 512), F32), ((width, 256), F32), ((1, width), F32), ((1, width), F32)]
    scratch = [(mine.shape, BF16), (mine.shape, BF16)] + outs
    return run_kernel(split_kernel, "split_projection", (info,), (mine, arrived), outs, scratch, 7, 10**8, limit=20)


def swap_cores(array):
    return lax.ppermute(array, "head", [(0, 1), (1, 0)])


def half_of(array, which):
    rows = array.shape[0] // 2
    return lax.dynamic_slice_in_dim(array, which * rows, rows, 0)


def add_low(a, b):
    return (a.astype(F32) + b.astype(F32)).astype(BF16)


def join(mine, theirs, which):
    both = jnp.concatenate([mine, mine], axis=0)
    return lax.dynamic_update_slice_in_dim(both, theirs, (1 - which) * mine.shape[0], 0)


def after_all(first, *rest):
    return lax.optimization_barrier((first, *rest))


class SeqSum:
    def __init__(self, orders):
        self.size = lax.axis_size("seq")
        bits = self.size.bit_length() - 1
        self.orders = [
            [b for b in order if b < bits] + [b for b in range(bits) if b not in order]
            for order in orders
        ]
        self.stage, self.bits = 0, bits
        self.fitting, self.whole, self.kept = False, False, None

    def begin(self, stay, stay_come, away, away_come):
        self.mine, self.coming, self.half = stay, stay_come, None if stay_come is None else -1
        self.sent = away if away_come is None else add_low(away, away_come)
        self.next, self.stage, self.trail = 0, 1, [0]

    def which(self, stage, other=0):
        bit = jnp.where(lax.axis_index("head") == other, self.orders[0][stage], self.orders[1][stage])
        return (lax.axis_index("seq") >> bit) & 1

    def swap(self, array, stage):
        pairs = []
        for i in range(self.size):
            for core in range(2):
                pairs.append((2 * i + core, 2 * (i ^ (1 << self.orders[core][stage])) + core))
        return lax.ppermute(array, ("seq", "head"), pairs)

    def added(self, which=None):
        parts = [a if which is None else half_of(a, which) for a in (self.mine, self.coming) if a is not None]
        return parts[0] if len(parts) == 1 else add_low(*parts)

    def prepare(self):
        if self.stage < self.bits:
            self.settle()
            if self.stage < self.bits - 1 and self.mine.shape[0] % 32 == 0:
                which = self.which(self.stage)
                self.trail.append(self.stage)
                self.sent, self.half = self.added(1 - which), which
            else:
                self.sent = self.mine = self.added()
                self.coming = None
            self.next = self.stage
            self.stage += 1
            return True
        self.settle()
        if self.fitting:
            self.mine = join(self.mine, self.coming, self.which(self.next))
        else:
            self.mine, self.fitting = self.added(), True
        if not self.trail:
            return False
        self.next, self.sent = self.trail.pop(), self.mine
        return True

    def launch(self):
        self.kept = self.coming
        self.coming = self.swap(self.sent, self.next)

    def settle(self):
        if self.half is not None:
            parts = [a for a in (self.mine, self.kept) if a is not None]
            if not isinstance(self.half, int):
                parts = [half_of(a, self.half) for a in parts]
            self.mine = parts[0] if len(parts) == 1 else add_low(*parts)
            self.half = None

    def flow(self, cuts, ready=False):
        while ready or self.prepare():
            ready = False
            rows = self.sent.shape[0]
            parts = cuts if self.fitting and not self.trail else 1
            edges = [rows // 16 * n // parts * 16 for n in range(parts)] + [rows]
            came = []
            for start, stop in zip(edges, edges[1:]):
                came.append((yield lambda a: self.swap(a, self.next), self.sent[start:stop]))
            self.kept = self.coming
            self.coming = came[0] if parts == 1 else jnp.concatenate(came, axis=0)
        self.whole = True
        self.other = yield swap_cores, self.mine


ORDERS = ((0, 1, 2, 3), (1, 2, 3, 0))
PROJECTION_ORDERS = ((0, 1, 2, 3), (1, 0, 2, 3))
CUTS = (0, 2, 4, 6, 8)


def on_device(
    tokens, first_values, cotangent, slot_count, seq_lengths, query_weight, key_weight, value_weight,
    mixing_weight, expand_weight, shrink_weight, expand_bias, before_gain, before_shift,
    middle_gain, middle_shift,
):
    head = lax.axis_index("head")
    sums, projection = SeqSum(ORDERS), SeqSum(PROJECTION_ORDERS)
    info = jnp.stack([slot_count[0], head, sums.which(0), projection.which(0), sums.which(0, 1)])
    info = info.astype(jnp.int32)
    lengths = seq_lengths[0]
    row = lambda v: v.reshape(1, -1)

    other = swap_cores(tokens)
    skip_other = swap_cores(first_values)
    mixed_own, mixed_away, query, keys, values, mixed, logsum, normed = forward_attention(
        info, tokens, other, first_values, skip_other, query_weight, key_weight, value_weight,
        row(before_gain), row(before_shift),
    )
    mixed_other = swap_cores(mixed_away)
    output, after_grad, grad_own, grad_away, own_stay, own_away, other_stay, other_away = row_part(
        info, lengths, tokens, mixed_own, mixed_other, cotangent, mixing_weight, expand_weight,
        shrink_weight, row(expand_bias), row(middle_gain), row(middle_shift),
    )
    grad_other = swap_cores(grad_away)
    grad_other, other_away = after_all(grad_other, other_away)
    away_come = swap_cores(other_away)
    grad, inner = arrange_rows(info, grad_own, grad_other, mixed)
    grad, away_come = after_all(grad, away_come)
    sums.begin(own_stay, swap_cores(other_stay), own_away, away_come)
    attention = (query, keys, values, grad, logsum, inner)
    query_total, pieces = None, []
    for first, last in zip(CUTS, CUTS[1:]):
        if first > 0:
            sums.prepare()
        *attention, sums.sent = after_all(*attention, sums.sent)
        sums.launch()
        if last < CUTS[-1]:
            query_total, kept = next_blocks(first, last, info, query_total, *attention)
            pieces.append(kept)
            query_total, sums.coming, sums.mine, sums.kept = after_all(
                query_total, sums.coming, sums.mine, sums.kept
            )
        else:
            projection_stay, projection_away, packed = last_blocks(
                first, info, query_total, *attention, normed, row(before_gain), row(before_shift),
                query_weight, key_weight, value_weight, pieces,
            )
            packed, sums.coming, sums.mine, sums.kept = after_all(packed, sums.coming, sums.mine, sums.kept)
    projection.begin(projection_stay, None, projection_away, None)

    lanes = [projection.flow(1, True), sums.flow(3)]
    pending = [next(lane) for lane in lanes]
    work, made, extra, finished = 0, None, (), False
    while pending:
        inputs = ()
        if work == 0:
            inputs, kernel = (packed,), lambda p: back_rows(info, p, query_weight, key_weight, value_weight)
        elif work == 1:
            extra = (back_away, skip_away)
        elif work == 2:
            inputs, kernel = (back_other, skip_arrived), lambda b, k: close_rows(
                info, tokens, after_grad, back_own, b, skip_own, k, row(before_gain)
            )
        elif sums.whole and made is None:
            inputs, kernel = (sums.mine,), lambda m: unpack_half(info, m)
        elif made is not None and not finished:
            inputs, kernel, finished = (sums.other, *made), lambda o, *m: unpack_half(info, o, tuple(m)), True
        tied = after_all(*[array for _, array in pending], *extra, *inputs)
        count = len(pending)
        came = [swap(a) for (swap, _), a in zip(pending, tied)]
        came += [swap_cores(a) for a in tied[count : count + len(extra)]]
        results = kernel(*tied[count + len(extra) :]) if inputs else ()
        tied = after_all(*came, *results)
        came, results = tied[: len(came)], tied[len(came) :]
        if work == 0:
            back_own, back_away, skip_own, skip_away = results
        elif work == 1:
            back_other, skip_arrived = came[count:]
        elif work == 2:
            input_grad, skip_grad = results
        elif results:
            made = results
        work, extra = work + 1, ()
        later = []
        for lane, array in zip(lanes, came):
            try:
                later.append((lane, lane.send(array)))
            except StopIteration:
                pass
        lanes, pending = [lane for lane, _ in later], [p for _, p in later]
    if made is None:
        made = unpack_half(info, sums.mine)
    if not finished:
        made = unpack_half(info, sums.other, tuple(made))
    shrink_grad, expand_grad, mixing_grad, *sums_vectors = made
    query_grad, key_grad, value_grad, *edges = split_projection(info, projection.mine, projection.other)
    bias_grad, middle_gain_grad, middle_shift_grad = [v.reshape(-1) for v in sums_vectors]
    before_gain_grad, before_shift_grad = [v.reshape(-1) for v in edges]
    return (
        output, input_grad, skip_grad, query_grad, key_grad, value_grad, mixing_grad, expand_grad,
        shrink_grad, bias_grad, before_gain_grad, before_shift_grad, middle_gain_grad, middle_shift_grad,
    )


def solution(mesh):
    rows = P(("seq", "head"), None)
    return jax.shard_map(
        on_device,
        mesh=mesh,
        in_specs=(rows, rows, rows, P("seq"), P("seq", None)) + (P(),) * 11,
        out_specs=(rows, rows, rows) + (P(),) * 11,
        check_vma=False,
    )
```

```python
from functools import partial
import math
import jax
import jax.numpy as jnp
from jax import lax
from jax.experimental import pallas as pl
from jax.experimental.pallas import tpu as pltpu
from jax.sharding import PartitionSpec as P

BLOCK = 256
SLOT_OPTIONS = (1, 2, 4, 8)
LOG2E = math.log2(math.e)
F32, BF16 = jnp.float32, jnp.bfloat16
MASKED = -1e30
EPS = 1e-05
MIB = 1 << 20
VMEM_MIB, WHOLE_MIB = 56, 62


def nn(a, b):
    return lax.dot_general(a, b, (((1,), (0,)), ((), ())), preferred_element_type=F32)


def nt(a, b):
    return lax.dot_general(a, b, (((1,), (1,)), ((), ())), preferred_element_type=F32)


def tn(a, b):
    return lax.dot_general(a, b, (((0,), (0,)), ((), ())), preferred_element_type=F32)


def sorter(count, transposed=False):
    each = BLOCK // count
    grouped = lax.broadcasted_iota(jnp.int32, (BLOCK, BLOCK), 1 if transposed else 0)
    plain = lax.broadcasted_iota(jnp.int32, (BLOCK, BLOCK), 0 if transposed else 1)
    place = (plain & (count - 1)) * each + (plain >> (count.bit_length() - 1))
    return jnp.where(grouped == place, 1.0, 0.0).astype(BF16)


def store_grouped(write, values, tile, total, count):
    each = BLOCK // count
    for group in range(count):
        start = pl.multiple_of(group * (total // count) + tile * each, each)
        write(pl.ds(start, each), values[group * each : (group + 1) * each])


def load_grouped(read, tile, total, count):
    each = BLOCK // count
    parts = []
    for group in range(count):
        start = pl.multiple_of(group * (total // count) + tile * each, each)
        parts.append(read(pl.ds(start, each)))
    return parts[0] if count == 1 else jnp.concatenate(parts, axis=0)


def normalized(rows):
    average = jnp.mean(rows, axis=-1, keepdims=True)
    centred = rows - average
    spread = jnp.mean(centred * centred, axis=-1, keepdims=True)
    scale = lax.rsqrt(spread + EPS)
    return centred * scale, scale


def as_columns(vectors):
    stack = jnp.concatenate(vectors + [jnp.zeros((128 - len(vectors), vectors[0].shape[1]), F32)], axis=0)
    return jnp.transpose(stack).astype(BF16)


def forward_kernel(
    info, own_in, other_in, skip_own_in, skip_other_in, query_in, key_in, value_in, gain_in, shift_in,
    mixed_own_out, mixed_other_out, query_out, keys_out, saved_out, mixed_out, logsum_out, normed_out,
    own, other, skip_own, skip_other, query_weight, key_weight, value_weight,
    mixed_own, mixed_other, query, keys, saved, mixed, logsum, normed, values, gain, shift, semaphores,
):
    count, head = info[0], info[1]
    half = own.shape[0]
    total = 2 * half
    blocks = total // BLOCK
    cols = pl.ds(pl.multiple_of(head * 256, 256), 256)
    fresh_cols = pl.ds(pl.multiple_of(head * 128, 128), 128)
    mover = Mover(semaphores)
    mover.start(own_in, own, "own")
    mover.start(gain_in, gain, "gain")
    mover.start(shift_in, shift, "shift")
    mover.start(query_in.at[:, cols], query_weight, "q")
    mover.start(key_in.at[:, cols], key_weight, "k")
    mover.start(value_in.at[:, fresh_cols], value_weight, "v")
    mover.start(skip_own_in.at[:, fresh_cols], skip_own, "skip")
    values[:, :, 128:] = jnp.ones((2, total, 128), BF16)

    for rows_ref, skip_ref, which, needs in (
        (own, skip_own, head, ("own", "gain", "shift", "q", "k", "v", "skip")),
        (other, skip_other, 1 - head, ("other", "skip_other")),
    ):
        mover.wait(*needs)
        if needs[0] == "own":
            mover.start(other_in, other, "other")
            mover.start(skip_other_in.at[:, fresh_cols], skip_other, "skip_other")

        def project(step, _, rows_ref=rows_ref, skip_ref=skip_ref, which=which):
            at = pl.ds(pl.multiple_of(step * BLOCK, BLOCK), BLOCK)
            tile = which * (half // BLOCK) + step
            hat, _s = normalized(rows_ref[at, :].astype(F32))
            low = (hat * gain[...] + shift[...]).astype(BF16)
            skip = skip_ref[at, :]

            def put(count_here):
                rows, skipped = low, skip
                if count_here > 1:
                    order = sorter(count_here)
                    rows = nn(order, low).astype(BF16)
                    skipped = nn(order, skip).astype(BF16)
                q = nn(rows, query_weight[...]).astype(BF16)
                q = (q.astype(F32) * (0.125 * LOG2E)).astype(BF16)
                k = nn(rows, key_weight[...]).astype(BF16)
                f = nn(rows, value_weight[...]).astype(BF16)

                def put_in(ref, part, value):
                    def write(dst, piece):
                        if part is None:
                            ref[dst, :] = piece
                        else:
                            ref[part, dst, :128] = piece
                            if ref is values:
                                saved[part, dst, :] = piece

                    store_grouped(write, value, tile, total, count_here)

                put_in(normed, None, rows)
                put_in(query, 0, q[:, :128])
                put_in(query, 1, q[:, 128:])
                put_in(keys, 0, k[:, :128])
                put_in(keys, 1, k[:, 128:])
                put_in(values, 0, f)
                put_in(values, 1, skipped)

            for option in SLOT_OPTIONS:
                pl.when(count == option)(partial(put, option))
            return 0

        lax.fori_loop(0, half // BLOCK, project, 0)

    for source, target in ((query, query_out), (keys, keys_out), (saved, saved_out), (normed, normed_out)):
        mover.start(source, target)

    per_slot = blocks // count
    lane = lax.broadcasted_iota(jnp.int32, (1, 128), 1)
    tri = lax.broadcasted_iota(jnp.int32, (BLOCK, BLOCK), 1) <= lax.broadcasted_iota(
        jnp.int32, (BLOCK, BLOCK), 0
    )

    def attend(block, _):
        width = block % per_slot + 1
        here = pl.multiple_of(block * BLOCK, BLOCK)

        def run(wide):
            first = pl.multiple_of((block - (wide - 1)) * BLOCK, BLOCK)

            def score(h):
                pair, sub = h // 2, h % 2
                q = query[pair, pl.ds(here, BLOCK), :]
                qm = jnp.where((lane < 64) == (sub == 0), q, jnp.zeros_like(q))
                diag = nt(qm, keys[pair, pl.ds(here, BLOCK), :])
                rest = None
                if wide > 1:
                    rest = nt(qm, keys[pair, pl.ds(first, (wide - 1) * BLOCK), :])
                return diag, rest

            def soften(diag, rest):
                diag = jnp.where(tri, diag, MASKED)
                top = jnp.max(diag, axis=1, keepdims=True)
                if wide > 1:
                    top = jnp.maximum(top, jnp.max(rest, axis=1, keepdims=True))
                raised = [jnp.exp2(diag - top).astype(BF16)]
                if wide > 1:
                    raised.append(jnp.exp2(rest - top).astype(BF16))
                return top, raised

            def finish(h, top, raised):
                acc = nn(raised[0], values[h // 2, pl.ds(here, BLOCK), :])
                if wide > 1:
                    acc += nn(raised[1], values[h // 2, pl.ds(first, (wide - 1) * BLOCK), :])
                sums = acc[:, 128:]
                return acc[:, :128] / sums, jnp.transpose(top + jnp.log2(sums))[0:1, :]

            scores = [score(h) for h in range(4)]
            softened = [soften(*scores[h]) for h in range(4)]
            outs = [finish(h, *softened[h]) for h in range(4)]
            for pair in range(2):
                mixed[pair, pl.ds(here, BLOCK), :] = jnp.where(lane < 64, outs[2*pair][0], outs[2*pair+1][0]).astype(BF16)
                for sub in range(2):
                    logsum[pair, sub : sub + 1, pl.ds(here, BLOCK)] = outs[2*pair+sub][1]

        for wide in range(1, blocks + 1):
            pl.when(width == wide)(partial(run, wide))
        return 0

    lax.fori_loop(0, blocks, attend, 0)
    mover.start(mixed, mixed_out)
    mover.start(logsum, logsum_out)

    for out_ref, target, which in (
        (mixed_other, mixed_other_out, 1 - head),
        (mixed_own, mixed_own_out, head),
    ):

        def give(step, _, out_ref=out_ref, which=which):
            at = pl.ds(pl.multiple_of(step * BLOCK, BLOCK), BLOCK)
            tile = which * (half // BLOCK) + step

            def put(count_here):
                for pair in range(2):
                    part = load_grouped(lambda s: mixed[pair, s, :], tile, total, count_here)
                    if count_here > 1:
                        part = nn(sorter(count_here, True), part).astype(BF16)
                    out_ref[at, pair * 128 : (pair + 1) * 128] = part

            for option in SLOT_OPTIONS:
                pl.when(count == option)(partial(put, option))
            return 0

        lax.fori_loop(0, half // BLOCK, give, 0)
        mover.start(out_ref, target)
    mover.wait_all()


class Mover:
    def __init__(self, semaphores):
        self.semaphores, self.used, self.open = semaphores, 0, {}

    def start(self, source, target, name=None):
        copy = pltpu.make_async_copy(source, target, self.semaphores.at[self.used])
        copy.start()
        self.open[self.used if name is None else name] = copy
        self.used += 1

    def wait(self, *names):
        for name in names:
            self.open.pop(name).wait()

    def wait_all(self):
        self.wait(*list(self.open))


def run_kernel(kernel, name, scalars, args, outs, scratch, moves, flops, aliases=None, limit=VMEM_MIB):
    smem = pl.BlockSpec(memory_space=pltpu.SMEM)
    large = pl.BlockSpec(memory_space=pl.ANY)
    size = lambda shape, dtype: math.prod(shape) * jnp.dtype(dtype).itemsize
    moved = sum(size(a.shape, a.dtype) for a in args) + sum(size(*o) for o in outs)
    return pl.pallas_call(
        kernel,
        in_specs=[smem] * len(scalars) + [large] * len(args),
        out_specs=[large] * len(outs),
        out_shape=[jax.ShapeDtypeStruct(*o) for o in outs],
        scratch_shapes=[pltpu.VMEM(*s) for s in scratch] + [pltpu.SemaphoreType.DMA((moves,))],
        input_output_aliases=aliases or {},
        cost_estimate=pl.CostEstimate(flops=flops, bytes_accessed=moved, transcendentals=0),
        compiler_params=pltpu.CompilerParams(vmem_limit_bytes=limit * MIB),
        name=name,
    )(*scalars, *args)


def forward_attention(info, own, other, skip_own, skip_other, wq, wk, wv, gain, shift):
    half, width = own.shape
    total = 2 * half
    group = wq.shape[1] // 2
    outs = [
        ((half, group), BF16),
        ((half, group), BF16),
        ((2, total, 128), BF16),
        ((2, total, 128), BF16),
        ((2, total, 128), BF16),
        ((2, total, 128), BF16),
        ((2, 8, total), F32),
        ((total, width), BF16),
    ]
    scratch = [
        ((half, width), BF16),
        ((half, width), BF16),
        ((half, 128), BF16),
        ((half, 128), BF16),
        ((width, group), BF16),
        ((width, group), BF16),
        ((width, 128), BF16),
        *outs,
        ((2, total, 256), BF16),
        (gain.shape, F32),
        (shift.shape, F32),
    ]
    return run_kernel(
        forward_kernel, "forward_attention", (info,),
        (own, other, skip_own, skip_other, wq, wk, wv, gain, shift), outs, scratch, 17, 10 * 10**9,
        limit=WHOLE_MIB,
    )


COLS = 512
TILE, PART = 512, 256
GELU_SLOPE = math.sqrt(2.0 / math.pi)
GELU_CUBE = 0.044715


def gelu_pair(v):
    square = v * v
    bend = jnp.tanh(v * (GELU_SLOPE + (GELU_SLOPE * GELU_CUBE) * square))
    front = 0.5 + 0.5 * bend
    steep = v * (2.0 * GELU_SLOPE + (6.0 * GELU_SLOPE * GELU_CUBE) * square)
    return v * front, front + steep * (front * (1.0 - front))


def rows_kernel(
    info, lengths, tokens_in, mixed_own_in, mixed_other_in, cotangent_in, mixing_in, expand_in,
    shrink_in, bias_in, gain_in, shift_in,
    output_out, after_grad_out, send_own_out, send_other_out,
    own_stay_out, own_away_out, other_stay_out, other_away_out, vectors_out,
    tokens, mixed_own, mixed_other, cotangent, mixing_weight, expand_weight, shrink_weight,
    expand_bias, gain, shift, output, after_grad, send_own, send_other, grads_own, grads_other,
    vectors, bias_grad, gain_grads, active, pre_grad, middle, out_grad, after_low, semaphores,
):
    mover = Mover(semaphores)
    for source, target, name in (
        (mixing_in, mixing_weight, "mixing"),
        (tokens_in, tokens, "tokens"),
        (mixed_own_in, mixed_own, "own"),
        (mixed_other_in, mixed_other, "other"),
        (gain_in, gain, "gain"),
        (shift_in, shift, "shift"),
        (bias_in, expand_bias, "bias"),
        (expand_in, expand_weight, "expand"),
        (shrink_in, shrink_weight, "shrink"),
        (cotangent_in, cotangent, "cotangent"),
    ):
        mover.start(source, target, name)
    count, head = info[0], info[1]
    half, width = tokens.shape
    hidden = expand_weight.shape[1]
    group = mixed_own.shape[1]
    shift_by = (
        (count >= 2).astype(jnp.int32)
        + (count >= 4).astype(jnp.int32)
        + (count >= 8).astype(jnp.int32)
    )
    here = pl.ds(pl.multiple_of(head * group, group), group)
    there = pl.ds(pl.multiple_of((1 - head) * group, group), group)
    bias_grad[...] = jnp.zeros_like(bias_grad)
    gain_grads[...] = jnp.zeros_like(gain_grads)
    mover.wait("mixing", "tokens", "own", "other", "gain", "shift", "bias")

    def tile(step, _):
        at = pl.ds(pl.multiple_of(step * TILE, TILE), TILE)
        row = head * half + step * TILE + lax.broadcasted_iota(jnp.int32, (TILE, 1), 0)
        slot = row & (count - 1)
        limit = jnp.zeros_like(row)
        for s in range(lengths.shape[0]):
            limit = jnp.where(slot == s, lengths[s], limit)
        valid = (row >> shift_by) < limit

        def first_wait(*names):
            pl.when(step == 0)(lambda: mover.wait(*names))

        after = (
            tokens[at, :].astype(F32)
            + nn(mixed_own[at, :], mixing_weight[here, :])
            + nn(mixed_other[at, :], mixing_weight[there, :])
        )
        hat, scale = normalized(after)
        low = (hat * gain[...] + shift[...]).astype(BF16)
        middle[at, :] = low
        first_wait("expand", "shrink", "cotangent")
        grad_out = jnp.where(valid, cotangent[at, :].astype(F32), 0.0)
        grad_low = grad_out.astype(BF16)
        out_grad[at, :] = grad_low

        def products(c):
            cs = slice(c, c + PART)
            return nn(low, expand_weight[:, cs]), nt(grad_low, shrink_weight[cs, :])

        ahead = products(0)
        for c in range(0, hidden, PART):
            cs = slice(c, c + PART)
            now = ahead
            if c + PART < hidden:
                ahead = products(c + PART)
            act, slope = gelu_pair(now[0] + expand_bias[:, cs])
            active[at, cs] = act.astype(BF16)
            g = now[1] * slope
            bias_grad[0:1, cs] += jnp.sum(g, axis=0, keepdims=True)
            pre_grad[at, cs] = g.astype(BF16)
        g_middle = nt(pre_grad[at, :], expand_weight[...])
        grown = nn(active[at, :], shrink_weight[...])
        gain_grads[0:1, :] += jnp.sum(g_middle * hat, axis=0, keepdims=True)
        gain_grads[1:2, :] += jnp.sum(g_middle, axis=0, keepdims=True)
        y = g_middle * gain[...]
        g_after = grad_out + scale * (
            y
            - jnp.mean(y, axis=-1, keepdims=True)
            - hat * jnp.mean(y * hat, axis=-1, keepdims=True)
        )
        after_grad[at, :] = g_after
        g_low = g_after.astype(BF16)
        after_low[at, :] = g_low
        output[at, :] = jnp.where(valid, after + grown, 0.0).astype(BF16)
        send_own[at, :] = nt(g_low, mixing_weight[here, :]).astype(BF16)
        send_other[at, :] = nt(g_low, mixing_weight[there, :]).astype(BF16)
        return 0

    lax.fori_loop(0, half // TILE, tile, 0)

    for source, target in (
        (send_other, send_other_out),
        (send_own, send_own_out),
        (output, output_out),
        (after_grad, after_grad_out),
    ):
        mover.start(source, target)
    vectors[...] = jnp.zeros_like(vectors)
    for n, c in enumerate(range(0, hidden, width)):
        vectors[n : n + 1, :] = bias_grad[0:1, c : c + width]
    vectors[4:6, :] = gain_grads[0:2, :]
    mover.start(vectors, vectors_out)
    first_half = grads_own.shape[0] // 2
    for grads, stay_out, away_out, mixed, which, side in (
        (grads_other, other_stay_out, other_away_out, mixed_other, 1 - head, info[4]),
        (grads_own, own_stay_out, own_away_out, mixed_own, head, info[2]),
    ):
        stay = pl.ds(pl.multiple_of(side * first_half, 16), first_half)
        away = pl.ds(pl.multiple_of((1 - side) * first_half, 16), first_half)

        def weights(step, _, grads=grads, which=which):
            cs = pl.ds(pl.multiple_of((2 * which + step) * COLS, COLS), COLS)
            at = pl.multiple_of(step * COLS, COLS)
            grads[pl.ds(at, COLS), :] = tn(active[:, cs], out_grad[...]).astype(BF16)
            grads[pl.ds(2 * COLS + at, COLS), :] = tn(middle[...], pre_grad[:, cs]).astype(BF16)
            return 0

        lax.fori_loop(0, 2, weights, 0)
        grads[4 * COLS :, :] = tn(mixed[...], after_low[...]).astype(BF16)
        mover.start(grads.at[away], away_out)
        mover.start(grads.at[stay], stay_out)
    mover.wait_all()


def row_part(info, lengths, tokens, mixed_own, mixed_other, cotangent, wo, we, ws, bias, gain, shift):
    half, width = tokens.shape
    hidden = we.shape[1]
    group = mixed_own.shape[1]
    outs = [
        ((half, width), BF16),
        ((half, width), F32),
        ((half, group), BF16),
        ((half, group), BF16),
        *[(((hidden + group) // 2, width), BF16)] * 4,
        ((8, width), F32),
    ]
    args = (tokens, mixed_own, mixed_other, cotangent, wo, we, ws, bias, gain, shift)
    scratch = [
        *[(a.shape, a.dtype) for a in args],
        *outs[:4],
        ((hidden + group, width), BF16),
        ((hidden + group, width), BF16),
        outs[8],
        ((8, hidden), F32),
        ((8, width), F32),
        ((half, hidden), BF16),
        ((half, hidden), BF16),
        ((half, width), BF16),
        ((half, width), BF16),
        ((half, width), BF16),
    ]
    return run_kernel(
        rows_kernel, "row_part", (info, lengths), args, outs, scratch, 19, 15 * 10**9,
        limit=WHOLE_MIB,
    )


def arrange_gradient(count, head, grad_own, grad_other, mixed, grad, inner):
    half = grad_own.shape[0]
    total = 2 * half

    for rows_ref, which in ((grad_own, head), (grad_other, 1 - head)):

        def arrange(step, _, rows_ref=rows_ref, which=which):
            at = pl.ds(pl.multiple_of(step * BLOCK, BLOCK), BLOCK)
            tile = which * (half // BLOCK) + step
            rows = rows_ref[at, :]

            def put(count_here):
                value = rows
                if count_here > 1:
                    value = nn(sorter(count_here), rows).astype(BF16)
                for pair in range(2):

                    def write(dst, piece, pair=pair):
                        grad[pair, dst, :] = piece

                    store_grouped(
                        write, value[:, pair * 128 : (pair + 1) * 128], tile, total, count_here
                    )

            for option in SLOT_OPTIONS:
                pl.when(count == option)(partial(put, option))
            return 0

        lax.fori_loop(0, half // BLOCK, arrange, 0)

    def inners(block, _):
        at = pl.ds(pl.multiple_of(block * BLOCK, BLOCK), BLOCK)
        for pair in range(2):
            flipped = jnp.transpose(grad[pair, at, :].astype(F32) * mixed[pair, at, :].astype(F32))
            for sub in range(2):
                inner[pair, sub : sub + 1, at] = jnp.sum(
                    flipped[sub * 64 : (sub + 1) * 64], axis=0, keepdims=True
                )
        return 0

    lax.fori_loop(0, total // BLOCK, inners, 0)


def attend_blocks(
    count, first, last, query, keys, values, grad, logsum, inner, query_total, kept, key_sums, value_sums
):
    blocks = first + query.shape[1] // BLOCK
    per_slot = blocks // count
    lane = lax.broadcasted_iota(jnp.int32, (1, 128), 1)
    tri = lax.broadcasted_iota(jnp.int32, (BLOCK, BLOCK), 0) <= lax.broadcasted_iota(
        jnp.int32, (BLOCK, BLOCK), 1
    )

    def attend(block, _):
        more = per_slot - block % per_slot - 1
        here = pl.multiple_of((block - first) * BLOCK, BLOCK)
        at = pl.ds(here, BLOCK)

        def part(start, size, diagonal):
            span = pl.ds(pl.multiple_of(start, BLOCK), size)

            def score(h):
                pair, sub = h // 2, h % 2
                pick = (lane < 64) == (sub == 0)
                k, v = keys[pair, at, :], values[pair, at, :]
                k = jnp.where(pick, k, jnp.zeros_like(k))
                v = jnp.where(pick, v, jnp.zeros_like(v))
                return k, nt(k, query[pair, span, :]), nt(v, grad[pair, span, :])

            def finish(h, k, raw, grad_probs):
                pair, sub = h // 2, h % 2
                probs = jnp.exp2(raw - logsum[pair, sub : sub + 1, span])
                if diagonal:
                    probs = jnp.where(tri, probs, 0.0)
                grad_scores = (probs * (grad_probs - inner[pair, sub : sub + 1, span])).astype(BF16)
                grad_value = nn(probs.astype(BF16), grad[pair, span, :])
                grad_key = nn(grad_scores, query[pair, span, :])
                if diagonal:
                    value_sums[h], key_sums[h] = grad_value, grad_key
                else:
                    value_sums[h] += grad_value
                    key_sums[h] += grad_key
                return tn(grad_scores, k)

            ahead = score(0)
            done = []
            for h in range(4):
                now = ahead
                if h < 3:
                    ahead = score(h + 1)
                done.append(finish(h, *now))
                if h % 2:
                    query_total[h // 2, span, :] += done[h - 1] + done[h]

        part(here, BLOCK, True)

        def two(n, _):
            part(here + BLOCK + n * (2 * BLOCK), 2 * BLOCK, False)
            return 0

        lax.fori_loop(0, more // 2, two, 0)

        @pl.when(more % 2 == 1)
        def _():
            part(here + more * BLOCK, BLOCK, False)

        for pair in range(2):
            for start, sums, scale in ((0, key_sums, 1.0 / LOG2E), (256, value_sums, 1.0)):
                picked = jnp.where(lane < 64, sums[2 * pair], sums[2 * pair + 1])
                kept[at, start + pair * 128 : start + (pair + 1) * 128] = (picked * scale).astype(BF16)
        return 0

    lax.fori_loop(first, last, attend, 0)


def arrange_kernel(
    info, grad_own_in, grad_other_in, mixed_in, grad_out, inner_out,
    grad_own, grad_other, mixed, grad, inner, semaphores,
):
    mover = Mover(semaphores)
    for source, target in ((grad_own_in, grad_own), (grad_other_in, grad_other), (mixed_in, mixed)):
        mover.start(source, target)
    mover.wait_all()
    arrange_gradient(info[0], info[1], grad_own, grad_other, mixed, grad, inner)
    mover.start(grad, grad_out)
    mover.start(inner, inner_out)
    mover.wait_all()


def arrange_rows(info, grad_own, grad_other, mixed):
    total = mixed.shape[1]
    outs = [((2, total, 128), BF16), ((2, 8, total), F32)]
    args = (grad_own, grad_other, mixed)
    scratch = [(a.shape, BF16) for a in args] + outs
    return run_kernel(arrange_kernel, "arrange_rows", (info,), args, outs, scratch, 5, 10**8, limit=WHOLE_MIB)


def fetch_blocks(mover, first, last, sources, targets):
    query, keys, values, grad, logsum, inner, *before = sources
    total = query.shape[1]
    span, rows = pl.ds(first * BLOCK, total - first * BLOCK), pl.ds(first * BLOCK, (last - first) * BLOCK)
    for source, target in zip(
        (
            keys.at[:, rows], query.at[:, span], values.at[:, rows], grad.at[:, span],
            logsum.at[:, :, span], inner.at[:, :, span], *[b.at[:, span] for b in before],
        ),
        targets,
    ):
        mover.start(source, target)


def next_kernel(first, last, info, *refs):
    count = 7 if first else 6
    sources, (query_total_out, kept_out), local, (key_sums, value_sums, kept, semaphores) = (
        refs[:count], refs[count : count + 2], refs[count + 2 : count + 9], refs[count + 9 :]
    )
    mover = Mover(semaphores)
    fetch_blocks(mover, first, last, sources, local)
    keys, query, values, grad, logsum, inner, query_total = local
    if not first:
        query_total[...] = jnp.zeros_like(query_total)
    mover.wait_all()
    attend_blocks(
        info[0], first, last, query, keys, values, grad, logsum, inner, query_total, kept,
        key_sums, value_sums,
    )
    total = sources[0].shape[1]
    span = pl.ds(first * BLOCK, total - first * BLOCK)
    mover.start(query_total, query_total_out.at[:, span])
    mover.start(kept, kept_out)
    mover.wait_all()


def local_blocks(first, last, total):
    rows, span = (last - first) * BLOCK, total - first * BLOCK
    return [
        ((2, rows, 128), BF16),
        ((2, span, 128), BF16),
        ((2, rows, 128), BF16),
        ((2, span, 128), BF16),
        ((2, 8, span), F32),
        ((2, 8, span), F32),
        ((2, span, 128), F32),
        ((4, BLOCK, 128), F32),
        ((4, BLOCK, 128), F32),
    ]


def next_blocks(first, last, info, before, query, keys, values, grad, logsum, inner):
    outs = [(query.shape, F32), (((last - first) * BLOCK, 512), BF16)]
    args = (query, keys, values, grad, logsum, inner) + ((before,) if first else ())
    return run_kernel(
        partial(next_kernel, first, last), f"blocks_{first}", (info,), args, outs,
        local_blocks(first, last, query.shape[1]) + [outs[1]], 9, 5 * 10**9, {7: 0} if first else {},
    )


def last_kernel(first, pieces, info, *refs):
    sources, refs = refs[:7], refs[7:]
    normed_in, gain_in, shift_in, vectors_in, query_in, key_in, value_in = refs[:7]
    kept_in, refs = refs[7 : 7 + pieces], refs[7 + pieces :]
    stay_out, away_out, packed_out = refs[:3]
    local, (key_sums, value_sums, *refs) = refs[3:10], refs[10:]
    kept, normed, gain, shift, vectors, query_weight, key_weight, value_weight, before, weight_grad, packed, semaphores = refs
    keys, query, values, grad, logsum, inner, query_total = local
    total = packed.shape[0]
    head = info[1]
    cols = pl.ds(pl.multiple_of(head * 256, 256), 256)
    fresh_cols = pl.ds(pl.multiple_of(head * 128, 128), 128)
    mover = Mover(semaphores)
    fetch_blocks(mover, first, total // BLOCK, sources, local)
    mover.start(sources[6].at[:, pl.ds(0, first * BLOCK)], before, "before")
    mover.start(normed_in, normed, "normed")
    mover.start(vectors_in, vectors, "vectors")
    mover.start(gain_in, gain, "gain")
    mover.start(shift_in, shift, "shift")
    mover.start(query_in.at[:, cols], query_weight, "q")
    mover.start(key_in.at[:, cols], key_weight, "k")
    mover.start(value_in.at[:, fresh_cols], value_weight, "v")
    row = 0
    for n, piece in enumerate(kept_in):
        mover.start(piece, packed.at[pl.ds(row, piece.shape[0]), pl.ds(256, 512)], f"p{n}")
        row += piece.shape[0]
    mover.wait(*range(7))
    attend_blocks(
        info[0], first, total // BLOCK, query, keys, values, grad, logsum, inner, query_total, kept,
        key_sums, value_sums,
    )
    mover.wait_all()
    packed[row:, 256:] = kept[...]
    for pair in range(2):
        lanes = slice(pair * 128, (pair + 1) * 128)
        packed[:row, lanes] = (before[pair, :, :] * 0.125).astype(BF16)
        packed[row:, lanes] = (query_total[pair, :, :] * 0.125).astype(BF16)
    mover.start(packed, packed_out)
    ones = jnp.ones((8, total), BF16)
    gain_grad = jnp.zeros((gain.shape[1], 1), F32)
    shift_grad = jnp.zeros((gain.shape[1], 1), F32)
    gain_column = jnp.transpose(jnp.broadcast_to(gain[...], (128, gain.shape[1])))[:, :1]
    shift_column = jnp.transpose(jnp.broadcast_to(shift[...], (128, gain.shape[1])))[:, :1]
    for start, stop, weight in ((0, 256, query_weight), (256, 512, key_weight), (512, 640, value_weight)):
        part = packed[:, start:stop]
        product = tn(normed[...], part)
        sums = nn(ones, part)[0:1, :]
        weight_grad[:, start:stop] = product.astype(BF16)
        weight = weight[...].astype(F32)
        shift_grad += jnp.sum(weight * sums, axis=1, keepdims=True)
        gain_grad += jnp.sum(weight * (product - shift_column * sums), axis=1, keepdims=True)
    lane = lax.broadcasted_iota(jnp.int32, (1, 128), 1)
    edge = jnp.where(lane == 0, gain_grad / gain_column, jnp.where(lane == 1, shift_grad, 0.0))
    stack = jnp.concatenate([vectors[...], jnp.zeros((120, vectors.shape[1]), F32)], axis=0)
    edge += jnp.where(lane >= 8, pltpu.roll(jnp.transpose(stack), 8, 1), 0.0)
    weight_grad[:, 640:] = edge.astype(BF16)
    rows = weight_grad.shape[0] // 2
    mover.start(weight_grad.at[pl.ds(pl.multiple_of((1 - info[3]) * rows, 16), rows)], away_out)
    mover.start(weight_grad.at[pl.ds(pl.multiple_of(info[3] * rows, 16), rows)], stay_out)
    mover.wait_all()


def last_blocks(first, info, before, query, keys, values, grad, logsum, inner, normed, gain, shift, vectors, wq, wk, wv, kept):
    total, width = normed.shape
    outs = [((width // 2, 768), BF16), ((width // 2, 768), BF16), ((total, 768), BF16)]
    scratch = local_blocks(first, total // BLOCK, total) + [
        ((total - first * BLOCK, 512), BF16),
        (normed.shape, BF16),
        (gain.shape, F32),
        (shift.shape, F32),
        (vectors.shape, F32),
        ((width, 256), BF16),
        ((width, 256), BF16),
        ((width, 128), BF16),
        ((2, first * BLOCK, 128), F32),
        ((width, 768), BF16),
        outs[2],
    ]
    return run_kernel(
        partial(last_kernel, first, len(kept)), "last_blocks", (info,),
        (query, keys, values, grad, logsum, inner, before, normed, gain, shift, vectors, wq, wk, wv, *kept),
        outs, scratch, 18 + len(kept), 5 * 10**9,
    )


def back_kernel(
    info, packed_in, query_in, key_in, value_in, back_own_out, back_other_out, skip_own_out, skip_other_out,
    packed, query_weight, key_weight, value_weight, back_own, back_other, skip_own, skip_other, back, semaphores,
):
    count, head = info[0], info[1]
    total = packed.shape[0]
    half = total // 2
    cols = pl.ds(pl.multiple_of(head * 256, 256), 256)
    fresh_cols = pl.ds(pl.multiple_of(head * 128, 128), 128)
    mover = Mover(semaphores)
    mover.start(packed_in, packed)
    mover.start(query_in.at[:, cols], query_weight)
    mover.start(key_in.at[:, cols], key_weight)
    mover.start(value_in.at[:, fresh_cols], value_weight)
    mover.wait_all()

    def close(block, _):
        at = pl.ds(pl.multiple_of(block * BLOCK, BLOCK), BLOCK)
        back[at, :] = (
            nt(packed[at, :256], query_weight[...])
            + nt(packed[at, 256:512], key_weight[...])
            + nt(packed[at, 512:640], value_weight[...])
        ).astype(BF16)
        return 0

    lax.fori_loop(0, total // BLOCK, close, 0)

    for back_ref, skip_ref, back_out, skip_out, which in (
        (back_other, skip_other, back_other_out, skip_other_out, 1 - head),
        (back_own, skip_own, back_own_out, skip_own_out, head),
    ):

        def give(step, _, back_ref=back_ref, skip_ref=skip_ref, which=which):
            at = pl.ds(pl.multiple_of(step * BLOCK, BLOCK), BLOCK)
            tile = which * (half // BLOCK) + step

            def put(count_here):
                g = load_grouped(lambda s: back[s, :], tile, total, count_here)
                k = load_grouped(lambda s: packed[s, 640:], tile, total, count_here)
                if count_here > 1:
                    order = sorter(count_here, True)
                    g = nn(order, g).astype(BF16)
                    k = nn(order, k).astype(BF16)
                back_ref[at, :] = g
                skip_ref[at, :] = k

            for option in SLOT_OPTIONS:
                pl.when(count == option)(partial(put, option))
            return 0

        lax.fori_loop(0, half // BLOCK, give, 0)
        mover.start(back_ref, back_out)
        mover.start(skip_ref, skip_out)
    mover.wait_all()


def back_rows(info, packed, wq, wk, wv):
    total, width = packed.shape[0], wq.shape[0]
    half = total // 2
    outs = [((half, width), BF16), ((half, width), BF16), ((half, 128), BF16), ((half, 128), BF16)]
    scratch = [
        (packed.shape, BF16),
        ((width, 256), BF16),
        ((width, 256), BF16),
        ((width, 128), BF16),
        *outs,
        ((total, width), BF16),
    ]
    return run_kernel(
        back_kernel, "back_rows", (info,), (packed, wq, wk, wv), outs, scratch, 8, 2 * 10**9
    )


def close_kernel(
    info, tokens_in, after_grad_in, back_own_in, back_other_in, kept_in, arrived_in, gain_in,
    result_out, skip_out,
    tokens, after_grad, back_own, back_other, gain, result, skip_grad, semaphores,
):
    head = info[1]
    mover = Mover(semaphores)
    mover.start(gain_in, gain)
    mover.start(tokens_in, tokens)
    mover.start(after_grad_in, after_grad)
    mover.start(back_own_in, back_own)
    mover.start(back_other_in, back_other)
    mover.start(kept_in, skip_grad.at[:, pl.ds(pl.multiple_of(head * 128, 128), 128)])
    mover.start(arrived_in, skip_grad.at[:, pl.ds(pl.multiple_of((1 - head) * 128, 128), 128)])
    mover.wait_all()
    mover.start(skip_grad, skip_out)

    def tile(step, _):
        at = pl.ds(pl.multiple_of(step * BLOCK, BLOCK), BLOCK)
        hat, scale = normalized(tokens[at, :].astype(F32))
        y = (back_own[at, :].astype(F32) + back_other[at, :].astype(F32)) * gain[...]
        result[at, :] = (
            after_grad[at, :]
            + scale
            * (
                y
                - jnp.mean(y, axis=-1, keepdims=True)
                - hat * jnp.mean(y * hat, axis=-1, keepdims=True)
            )
        ).astype(BF16)
        return 0

    lax.fori_loop(0, tokens.shape[0] // BLOCK, tile, 0)
    mover.start(result, result_out)
    mover.wait_all()


def close_rows(info, tokens, after_grad, back_own, back_other, kept, arrived, gain):
    args = (tokens, after_grad, back_own, back_other, kept, arrived, gain)
    outs = [(tokens.shape, BF16), ((tokens.shape[0], 256), BF16)]
    scratch = [(a.shape, a.dtype) for a in args[:4]] + [(gain.shape, F32)] + outs
    return run_kernel(close_kernel, "close_rows", (info,), args, outs, scratch, 9, 10**8)


def unpack_kernel(late, info, *refs):
    half_in, refs = refs[0], refs[1 + (3 if late else 0) :]
    shrink_out, expand_out, mixing_out, half, wide, semaphores = refs
    which = 1 - info[1] if late else info[1]
    width = half.shape[1]
    top = 4 * COLS + mixing_out.shape[0] // 2
    mover = Mover(semaphores)
    for at in range(0, 4 * COLS, COLS):
        mover.start(half_in.at[pl.ds(at, COLS)], half.at[pl.ds(at, COLS)], at)
    mover.start(half_in.at[pl.ds(4 * COLS, half.shape[0] - 4 * COLS)], half.at[pl.ds(4 * COLS, half.shape[0] - 4 * COLS)], "rest")
    for at in range(0, 4 * COLS, COLS):
        mover.wait(at)
        wide[at : at + COLS, :] = half[at : at + COLS, :].astype(F32)
        if at < 2 * COLS:
            row = pl.multiple_of(which * 2 * COLS + at, COLS)
            mover.start(wide.at[pl.ds(at, COLS)], shrink_out.at[pl.ds(row, COLS)])
        else:
            col = pl.multiple_of(which * 2 * COLS + at - 2 * COLS, COLS)
            mover.start(wide.at[pl.ds(at, COLS)], expand_out.at[:, pl.ds(col, COLS)])
    mover.wait("rest")
    wide[4 * COLS :, :] = half[4 * COLS :, :].astype(F32)
    row = pl.multiple_of(which * (top - 4 * COLS), 256)
    mover.start(wide.at[pl.ds(4 * COLS, top - 4 * COLS)], mixing_out.at[pl.ds(row, top - 4 * COLS)])
    mover.wait_all()


def unpack_half(info, half, before=()):
    rows, width = half.shape
    hidden = 4 * COLS
    outs = [((hidden, width), F32), ((width, hidden), F32), ((width, width), F32)]
    scratch = [(half.shape, BF16), ((rows, width), F32)]
    return run_kernel(
        partial(unpack_kernel, bool(before)), "unpack_late" if before else "unpack_half", (info,),
        (half, *before), outs, scratch, 10, 10**8, {2 + n: n for n in range(3)} if before else {},
        limit=20,
    )


def split_kernel(
    info, mine_in, arrived_in, query_out, key_out, value_out, *refs
):
    vectors_out, (mine, arrived, query, key, value), vectors, semaphores = refs[:5], refs[5:10], refs[10:15], refs[15]
    head = info[1]
    mover = Mover(semaphores)
    mover.start(mine_in, mine)
    mover.start(arrived_in, arrived)
    mover.wait_all()
    for half, which in ((mine, head), (arrived, 1 - head)):
        for target, wide, at in ((query, 256, 0), (key, 256, 256), (value, 128, 512)):
            cols = pl.ds(pl.multiple_of(which * wide, 128), wide)
            target[:, cols] = half[:, at : at + wide].astype(F32)
    for source, target in ((query, query_out), (key, key_out), (value, value_out)):
        mover.start(source, target)
    edges = jnp.transpose(mine[:, 640:].astype(F32) + arrived[:, 640:].astype(F32))
    gain, shift, bias, middle_gain, middle_shift = vectors
    width = gain.shape[1]
    for target, at in ((gain, 0), (shift, 1), (middle_gain, 12), (middle_shift, 13)):
        target[...] = edges[at : at + 1]
    for n in range(bias.shape[1] // width):
        bias[:, n * width : (n + 1) * width] = edges[8 + n : 9 + n]
    for source, target in zip(vectors, vectors_out):
        mover.start(source, target)
    mover.wait_all()


def split_projection(info, mine, arrived):
    width = mine.shape[0]
    outs = [((width, 512), F32), ((width, 512), F32), ((width, 256), F32)]
    outs += [((1, n * width), F32) for n in (1, 1, 4, 1, 1)]
    scratch = [(mine.shape, BF16), (mine.shape, BF16)] + outs
    return run_kernel(split_kernel, "split_projection", (info,), (mine, arrived), outs, scratch, 10, 10**8, limit=20)


def swap_cores(array):
    return lax.ppermute(array, "head", [(0, 1), (1, 0)])


def half_of(array, which):
    rows = array.shape[0] // 2
    return lax.dynamic_slice_in_dim(array, which * rows, rows, 0)


def add_low(a, b):
    return (a.astype(F32) + b.astype(F32)).astype(BF16)


def join(mine, theirs, which):
    both = jnp.concatenate([mine, mine], axis=0)
    return lax.dynamic_update_slice_in_dim(both, theirs, (1 - which) * mine.shape[0], 0)


def after_all(first, *rest):
    return lax.optimization_barrier((first, *rest))


class SeqSum:
    def __init__(self, orders):
        self.size = lax.axis_size("seq")
        bits = self.size.bit_length() - 1
        self.orders = [
            [b for b in order if b < bits] + [b for b in range(bits) if b not in order]
            for order in orders
        ]
        self.stage, self.bits = 0, bits
        self.fitting, self.whole, self.kept = False, False, None

    def begin(self, stay, stay_come, away, away_come):
        self.mine, self.coming, self.half = stay, stay_come, None if stay_come is None else -1
        self.sent = away if away_come is None else add_low(away, away_come)
        self.next, self.stage, self.trail = 0, 1, [0]

    def which(self, stage, other=0):
        bit = jnp.where(lax.axis_index("head") == other, self.orders[0][stage], self.orders[1][stage])
        return (lax.axis_index("seq") >> bit) & 1

    def swap(self, array, stage):
        pairs = []
        for i in range(self.size):
            for core in range(2):
                pairs.append((2 * i + core, 2 * (i ^ (1 << self.orders[core][stage])) + core))
        return lax.ppermute(array, ("seq", "head"), pairs)

    def added(self, which=None):
        parts = [a if which is None else half_of(a, which) for a in (self.mine, self.coming) if a is not None]
        return parts[0] if len(parts) == 1 else add_low(*parts)

    def prepare(self):
        if self.stage < self.bits:
            self.settle()
            if self.stage < self.bits - 1 and self.mine.shape[0] % 32 == 0:
                which = self.which(self.stage)
                self.trail.append(self.stage)
                self.sent, self.half = self.added(1 - which), which
            else:
                self.sent = self.mine = self.added()
                self.coming = None
            self.next = self.stage
            self.stage += 1
            return True
        self.settle()
        if self.fitting:
            self.mine = join(self.mine, self.coming, self.which(self.next))
        else:
            self.mine, self.fitting = self.added(), True
        if not self.trail:
            return False
        self.next, self.sent = self.trail.pop(), self.mine
        return True

    def launch(self):
        self.kept = self.coming
        self.coming = self.swap(self.sent, self.next)

    def settle(self):
        if self.half is not None:
            parts = [a for a in (self.mine, self.kept) if a is not None]
            if not isinstance(self.half, int):
                parts = [half_of(a, self.half) for a in parts]
            self.mine = parts[0] if len(parts) == 1 else add_low(*parts)
            self.half = None

    def via(self, stage):
        return lambda array: self.swap(array, stage)

    def flow(self, ready, small):
        while ready or self.stage < self.bits or len(self.trail) > 3:
            if not ready:
                self.prepare()
            ready = False
            (came,) = yield [(self.via(self.next), self.sent)]
            self.kept, self.coming = self.coming, came
        self.settle()
        piece = join(self.mine, self.coming, self.which(self.next)) if self.fitting else self.added()
        far, mid, near = self.trail
        rows = piece.shape[0]
        came_near, got_own = yield [(self.via(near), piece), (self.via(far), piece)]
        both = join(piece, came_near, self.which(near))
        if small:
            came_mid, got_near = yield [(self.via(mid), both), (self.via(far), came_near)]
            self.mine = join(both, came_mid, self.which(mid))
            got_mid, other_mine = yield [(self.via(far), came_mid), (swap_cores, self.mine)]
        else:
            (came_mid,) = yield [(self.via(mid), both)]
            cut = rows // 32 * 16
            (first,) = yield [(self.via(far), jnp.concatenate([came_near, came_mid[:cut]], axis=0))]
            (second,) = yield [(self.via(far), came_mid[cut:])]
            got_near, got_mid = first[:rows], jnp.concatenate([first[rows:], second], axis=0)
            self.mine = join(both, came_mid, self.which(mid))
        theirs = join(join(got_own, got_near, self.which(near)), got_mid, self.which(mid))
        self.mine = join(self.mine, theirs, self.which(far))
        self.whole = True
        if small:
            (other_theirs,) = yield [(swap_cores, theirs)]
            self.other = join(other_mine, other_theirs, self.which(far, 1))
        else:
            (self.other,) = yield [(swap_cores, self.mine)]


ORDERS = ((0, 1, 2, 3), (1, 2, 3, 0))
PROJECTION_ORDERS = ((0, 1, 2, 3), (1, 0, 2, 3))
CUTS = (0, 2, 4, 6, 8)


def on_device(
    tokens, first_values, cotangent, slot_count, seq_lengths, query_weight, key_weight, value_weight,
    mixing_weight, expand_weight, shrink_weight, expand_bias, before_gain, before_shift,
    middle_gain, middle_shift,
):
    head = lax.axis_index("head")
    sums, projection = SeqSum(ORDERS), SeqSum(PROJECTION_ORDERS)
    info = jnp.stack([slot_count[0], head, sums.which(0), projection.which(0), sums.which(0, 1)])
    info = info.astype(jnp.int32)
    lengths = seq_lengths[0]
    row = lambda v: v.reshape(1, -1)

    other = swap_cores(tokens)
    skip_other = swap_cores(first_values)
    mixed_own, mixed_away, query, keys, values, mixed, logsum, normed = forward_attention(
        info, tokens, other, first_values, skip_other, query_weight, key_weight, value_weight,
        row(before_gain), row(before_shift),
    )
    mixed_other = swap_cores(mixed_away)
    output, after_grad, grad_own, grad_away, own_stay, own_away, other_stay, other_away, row_vectors = row_part(
        info, lengths, tokens, mixed_own, mixed_other, cotangent, mixing_weight, expand_weight,
        shrink_weight, row(expand_bias), row(middle_gain), row(middle_shift),
    )
    grad_other = swap_cores(grad_away)
    grad_other, other_away = after_all(grad_other, other_away)
    away_come = swap_cores(other_away)
    grad, inner = arrange_rows(info, grad_own, grad_other, mixed)
    grad, away_come = after_all(grad, away_come)
    sums.begin(own_stay, swap_cores(other_stay), own_away, away_come)
    attention = (query, keys, values, grad, logsum, inner)
    query_total, pieces = None, []
    for first, last in zip(CUTS, CUTS[1:]):
        if first > 0:
            sums.prepare()
        *attention, sums.sent = after_all(*attention, sums.sent)
        sums.launch()
        if last < CUTS[-1]:
            query_total, kept = next_blocks(first, last, info, query_total, *attention)
            pieces.append(kept)
            query_total, sums.coming, sums.mine, sums.kept = after_all(
                query_total, sums.coming, sums.mine, sums.kept
            )
        else:
            projection_stay, projection_away, packed = last_blocks(
                first, info, query_total, *attention, normed, row(before_gain), row(before_shift),
                row_vectors, query_weight, key_weight, value_weight, pieces,
            )
            packed, sums.coming, sums.mine, sums.kept = after_all(packed, sums.coming, sums.mine, sums.kept)
    projection.begin(projection_stay, None, projection_away, None)

    lanes = [projection.flow(True, True), sums.flow(False, False)]
    pending = [next(lane) for lane in lanes]
    work, made, extra, finished = 0, None, (), False
    while pending:
        inputs = ()
        if work == 0:
            inputs, kernel = (packed,), lambda p: back_rows(info, p, query_weight, key_weight, value_weight)
        elif work == 1:
            extra = (back_away, skip_away)
        elif work == 2:
            inputs, kernel = (back_other, skip_arrived), lambda b, k: close_rows(
                info, tokens, after_grad, back_own, b, skip_own, k, row(before_gain)
            )
        elif sums.whole and made is None:
            inputs, kernel = (sums.mine,), lambda m: unpack_half(info, m)
        elif made is not None and not finished:
            inputs, kernel, finished = (sums.other, *made), lambda o, *m: unpack_half(info, o, tuple(m)), True
        moves = [move for group in pending for move in group]
        tied = after_all(*[array for _, array in moves], *extra, *inputs)
        count = len(moves)
        came = [swap(a) for (swap, _), a in zip(moves, tied)]
        came += [swap_cores(a) for a in tied[count : count + len(extra)]]
        results = kernel(*tied[count + len(extra) :]) if inputs else ()
        tied = after_all(*came, *results)
        came, results = tied[: len(came)], tied[len(came) :]
        if work == 0:
            back_own, back_away, skip_own, skip_away = results
        elif work == 1:
            back_other, skip_arrived = came[count:]
        elif work == 2:
            input_grad, skip_grad = results
        elif results:
            made = results
        work, extra = work + 1, ()
        later = []
        came = list(came)
        for lane, group in zip(lanes, pending):
            mine, came = came[: len(group)], came[len(group) :]
            try:
                later.append((lane, lane.send(mine)))
            except StopIteration:
                pass
        lanes, pending = [lane for lane, _ in later], [p for _, p in later]
    if made is None:
        made = unpack_half(info, sums.mine)
    if not finished:
        made = unpack_half(info, sums.other, tuple(made))
    shrink_grad, expand_grad, mixing_grad = made
    query_grad, key_grad, value_grad, *edges = split_projection(info, projection.mine, projection.other)
    before_gain_grad, before_shift_grad, bias_grad, middle_gain_grad, middle_shift_grad = [
        v.reshape(-1) for v in edges
    ]
    return (
        output, input_grad, skip_grad, query_grad, key_grad, value_grad, mixing_grad, expand_grad,
        shrink_grad, bias_grad, before_gain_grad, before_shift_grad, middle_gain_grad, middle_shift_grad,
    )


def solution(mesh):
    rows = P(("seq", "head"), None)
    return jax.shard_map(
        on_device,
        mesh=mesh,
        in_specs=(rows, rows, rows, P("seq"), P("seq", None)) + (P(),) * 11,
        out_specs=(rows, rows, rows) + (P(),) * 11,
        check_vma=False,
    )
```

```python
from functools import partial
import math
import jax
import jax.numpy as jnp
from jax import lax
from jax.experimental import pallas as pl
from jax.experimental.pallas import tpu as pltpu
from jax.sharding import PartitionSpec as P

BLOCK = 256
SLOT_OPTIONS = (1, 2, 4, 8)
LOG2E = math.log2(math.e)
F32, BF16 = jnp.float32, jnp.bfloat16
MASKED = -1e30
EPS = 1e-05
MIB = 1 << 20
VMEM_MIB, WHOLE_MIB = 56, 58


def nn(a, b):
    return lax.dot_general(a, b, (((1,), (0,)), ((), ())), preferred_element_type=F32)


def nt(a, b):
    return lax.dot_general(a, b, (((1,), (1,)), ((), ())), preferred_element_type=F32)


def tn(a, b):
    return lax.dot_general(a, b, (((0,), (0,)), ((), ())), preferred_element_type=F32)


def sorter(count, transposed=False):
    each = BLOCK // count
    grouped = lax.broadcasted_iota(jnp.int32, (BLOCK, BLOCK), 1 if transposed else 0)
    plain = lax.broadcasted_iota(jnp.int32, (BLOCK, BLOCK), 0 if transposed else 1)
    place = (plain & (count - 1)) * each + (plain >> (count.bit_length() - 1))
    return jnp.where(grouped == place, 1.0, 0.0).astype(BF16)


def store_grouped(write, values, tile, total, count):
    each = BLOCK // count
    for group in range(count):
        start = pl.multiple_of(group * (total // count) + tile * each, each)
        write(pl.ds(start, each), values[group * each : (group + 1) * each])


def load_grouped(read, tile, total, count):
    each = BLOCK // count
    parts = []
    for group in range(count):
        start = pl.multiple_of(group * (total // count) + tile * each, each)
        parts.append(read(pl.ds(start, each)))
    return parts[0] if count == 1 else jnp.concatenate(parts, axis=0)


def normalized(rows):
    average = jnp.mean(rows, axis=-1, keepdims=True)
    centred = rows - average
    spread = jnp.mean(centred * centred, axis=-1, keepdims=True)
    scale = lax.rsqrt(spread + EPS)
    return centred * scale, scale


def as_columns(vectors):
    stack = jnp.concatenate(vectors + [jnp.zeros((128 - len(vectors), vectors[0].shape[1]), F32)], axis=0)
    return jnp.transpose(stack).astype(BF16)


def forward_kernel(
    info, own_in, other_in, skip_own_in, skip_other_in, query_in, key_in, value_in, gain_in, shift_in,
    mixed_own_out, mixed_other_out, query_out, keys_out, saved_out, mixed_out, logsum_out, normed_out,
    own, other, skip_own, skip_other, query_weight, key_weight, value_weight,
    mixed_own, mixed_other, query, keys, saved, mixed, logsum, normed, values, gain, shift, semaphores,
):
    count, head = info[0], info[1]
    half = own.shape[0]
    total = 2 * half
    blocks = total // BLOCK
    cols = pl.ds(pl.multiple_of(head * 256, 256), 256)
    fresh_cols = pl.ds(pl.multiple_of(head * 128, 128), 128)
    mover = Mover(semaphores)
    mover.start(own_in, own, "own")
    mover.start(gain_in, gain, "gain")
    mover.start(shift_in, shift, "shift")
    mover.start(query_in.at[:, cols], query_weight, "q")
    mover.start(key_in.at[:, cols], key_weight, "k")
    mover.start(value_in.at[:, fresh_cols], value_weight, "v")
    mover.start(skip_own_in.at[:, fresh_cols], skip_own, "skip")
    values[:, :, 128:] = jnp.ones((2, total, 128), BF16)

    for rows_ref, skip_ref, which, needs in (
        (own, skip_own, head, ("own", "gain", "shift", "q", "k", "v", "skip")),
        (other, skip_other, 1 - head, ("other", "skip_other")),
    ):
        mover.wait(*needs)
        if needs[0] == "own":
            mover.start(other_in, other, "other")
            mover.start(skip_other_in.at[:, fresh_cols], skip_other, "skip_other")

        def project(step, _, rows_ref=rows_ref, skip_ref=skip_ref, which=which):
            at = pl.ds(pl.multiple_of(step * BLOCK, BLOCK), BLOCK)
            tile = which * (half // BLOCK) + step
            hat, _s = normalized(rows_ref[at, :].astype(F32))
            low = (hat * gain[...] + shift[...]).astype(BF16)
            skip = skip_ref[at, :]

            def put(count_here):
                rows, skipped = low, skip
                if count_here > 1:
                    order = sorter(count_here)
                    rows = nn(order, low).astype(BF16)
                    skipped = nn(order, skip).astype(BF16)
                q = nn(rows, query_weight[...]).astype(BF16)
                q = (q.astype(F32) * (0.125 * LOG2E)).astype(BF16)
                k = nn(rows, key_weight[...]).astype(BF16)
                f = nn(rows, value_weight[...]).astype(BF16)

                def put_in(ref, part, value):
                    def write(dst, piece):
                        if part is None:
                            ref[dst, :] = piece
                        else:
                            ref[part, dst, :128] = piece
                            if ref is values:
                                saved[part, dst, :] = piece

                    store_grouped(write, value, tile, total, count_here)

                put_in(normed, None, rows)
                put_in(query, 0, q[:, :128])
                put_in(query, 1, q[:, 128:])
                put_in(keys, 0, k[:, :128])
                put_in(keys, 1, k[:, 128:])
                put_in(values, 0, f)
                put_in(values, 1, skipped)

            for option in SLOT_OPTIONS:
                pl.when(count == option)(partial(put, option))
            return 0

        lax.fori_loop(0, half // BLOCK, project, 0)

    for source, target in ((query, query_out), (keys, keys_out), (saved, saved_out), (normed, normed_out)):
        mover.start(source, target)

    per_slot = blocks // count
    lane = lax.broadcasted_iota(jnp.int32, (1, 128), 1)
    tri = lax.broadcasted_iota(jnp.int32, (BLOCK, BLOCK), 1) <= lax.broadcasted_iota(
        jnp.int32, (BLOCK, BLOCK), 0
    )

    def attend(block, _):
        width = block % per_slot + 1
        here = pl.multiple_of(block * BLOCK, BLOCK)

        def run(wide):
            first = pl.multiple_of((block - (wide - 1)) * BLOCK, BLOCK)

            def score(h):
                pair, sub = h // 2, h % 2
                q = query[pair, pl.ds(here, BLOCK), :]
                qm = jnp.where((lane < 64) == (sub == 0), q, jnp.zeros_like(q))
                diag = nt(qm, keys[pair, pl.ds(here, BLOCK), :])
                rest = None
                if wide > 1:
                    rest = nt(qm, keys[pair, pl.ds(first, (wide - 1) * BLOCK), :])
                return diag, rest

            def soften(diag, rest):
                diag = jnp.where(tri, diag, MASKED)
                top = jnp.max(diag, axis=1, keepdims=True)
                if wide > 1:
                    top = jnp.maximum(top, jnp.max(rest, axis=1, keepdims=True))
                raised = [jnp.exp2(diag - top).astype(BF16)]
                if wide > 1:
                    raised.append(jnp.exp2(rest - top).astype(BF16))
                return top, raised

            def finish(h, top, raised):
                acc = nn(raised[0], values[h // 2, pl.ds(here, BLOCK), :])
                if wide > 1:
                    acc += nn(raised[1], values[h // 2, pl.ds(first, (wide - 1) * BLOCK), :])
                sums = acc[:, 128:]
                return acc[:, :128] / sums, jnp.transpose(top + jnp.log2(sums))[0:1, :]

            scores = [score(h) for h in range(4)]
            softened = [soften(*scores[h]) for h in range(4)]
            outs = [finish(h, *softened[h]) for h in range(4)]
            for pair in range(2):
                mixed[pair, pl.ds(here, BLOCK), :] = jnp.where(lane < 64, outs[2*pair][0], outs[2*pair+1][0]).astype(BF16)
                for sub in range(2):
                    logsum[pair, sub : sub + 1, pl.ds(here, BLOCK)] = outs[2*pair+sub][1]

        for wide in range(1, blocks + 1):
            pl.when(width == wide)(partial(run, wide))
        return 0

    lax.fori_loop(0, blocks, attend, 0)
    mover.start(mixed, mixed_out)
    mover.start(logsum, logsum_out)

    for out_ref, target, which in (
        (mixed_other, mixed_other_out, 1 - head),
        (mixed_own, mixed_own_out, head),
    ):

        def give(step, _, out_ref=out_ref, which=which):
            at = pl.ds(pl.multiple_of(step * BLOCK, BLOCK), BLOCK)
            tile = which * (half // BLOCK) + step

            def put(count_here):
                for pair in range(2):
                    part = load_grouped(lambda s: mixed[pair, s, :], tile, total, count_here)
                    if count_here > 1:
                        part = nn(sorter(count_here, True), part).astype(BF16)
                    out_ref[at, pair * 128 : (pair + 1) * 128] = part

            for option in SLOT_OPTIONS:
                pl.when(count == option)(partial(put, option))
            return 0

        lax.fori_loop(0, half // BLOCK, give, 0)
        mover.start(out_ref, target)
    mover.wait_all()


class Mover:
    def __init__(self, semaphores):
        self.semaphores, self.used, self.open = semaphores, 0, {}

    def start(self, source, target, name=None):
        copy = pltpu.make_async_copy(source, target, self.semaphores.at[self.used])
        copy.start()
        self.open[self.used if name is None else name] = copy
        self.used += 1

    def wait(self, *names):
        for name in names:
            self.open.pop(name).wait()

    def wait_all(self):
        self.wait(*list(self.open))


def run_kernel(kernel, name, scalars, args, outs, scratch, moves, flops, aliases=None, limit=VMEM_MIB):
    smem = pl.BlockSpec(memory_space=pltpu.SMEM)
    large = pl.BlockSpec(memory_space=pl.ANY)
    size = lambda shape, dtype: math.prod(shape) * jnp.dtype(dtype).itemsize
    moved = sum(size(a.shape, a.dtype) for a in args) + sum(size(*o) for o in outs)
    return pl.pallas_call(
        kernel,
        in_specs=[smem] * len(scalars) + [large] * len(args),
        out_specs=[large] * len(outs),
        out_shape=[jax.ShapeDtypeStruct(*o) for o in outs],
        scratch_shapes=[pltpu.VMEM(*s) for s in scratch] + [pltpu.SemaphoreType.DMA((moves,))],
        input_output_aliases=aliases or {},
        cost_estimate=pl.CostEstimate(flops=flops, bytes_accessed=moved, transcendentals=0),
        compiler_params=pltpu.CompilerParams(vmem_limit_bytes=limit * MIB),
        name=name,
    )(*scalars, *args)


def forward_attention(info, own, other, skip_own, skip_other, wq, wk, wv, gain, shift):
    half, width = own.shape
    total = 2 * half
    group = wq.shape[1] // 2
    outs = [
        ((half, group), BF16),
        ((half, group), BF16),
        ((2, total, 128), BF16),
        ((2, total, 128), BF16),
        ((2, total, 128), BF16),
        ((2, total, 128), BF16),
        ((2, 8, total), F32),
        ((total, width), BF16),
    ]
    scratch = [
        ((half, width), BF16),
        ((half, width), BF16),
        ((half, 128), BF16),
        ((half, 128), BF16),
        ((width, group), BF16),
        ((width, group), BF16),
        ((width, 128), BF16),
        *outs,
        ((2, total, 256), BF16),
        (gain.shape, F32),
        (shift.shape, F32),
    ]
    return run_kernel(
        forward_kernel, "forward_attention", (info,),
        (own, other, skip_own, skip_other, wq, wk, wv, gain, shift), outs, scratch, 17, 10 * 10**9,
        limit=WHOLE_MIB,
    )


COLS = 512
TILE, PART = 512, 256
GELU_SLOPE = math.sqrt(2.0 / math.pi)
GELU_CUBE = 0.044715


def gelu_pair(v):
    square = v * v
    bend = jnp.tanh(v * (GELU_SLOPE + (GELU_SLOPE * GELU_CUBE) * square))
    front = 0.5 + 0.5 * bend
    steep = v * (2.0 * GELU_SLOPE + (6.0 * GELU_SLOPE * GELU_CUBE) * square)
    return v * front, front + steep * (front * (1.0 - front))


def rows_kernel(
    info, lengths, tokens_in, mixed_own_in, mixed_other_in, cotangent_in, mixing_in, expand_in,
    shrink_in, bias_in, gain_in, shift_in,
    output_out, after_grad_out, send_own_out, send_other_out,
    own_stay_out, own_away_out, other_stay_out, other_away_out, vectors_out,
    tokens, mixed_own, mixed_other, cotangent, mixing_weight, expand_weight, shrink_weight,
    expand_bias, gain, shift, output, after_grad, send_own, send_other, grads_own, grads_other,
    vectors, bias_grad, gain_grads, active, pre_grad, middle, out_grad, after_low, semaphores,
):
    mover = Mover(semaphores)
    for source, target, name in (
        (mixing_in, mixing_weight, "mixing"),
        (tokens_in, tokens, "tokens"),
        (mixed_own_in, mixed_own, "own"),
        (mixed_other_in, mixed_other, "other"),
        (gain_in, gain, "gain"),
        (shift_in, shift, "shift"),
        (bias_in, expand_bias, "bias"),
        (expand_in, expand_weight, "expand"),
        (shrink_in, shrink_weight, "shrink"),
        (cotangent_in, cotangent, "cotangent"),
    ):
        mover.start(source, target, name)
    count, head = info[0], info[1]
    half, width = tokens.shape
    hidden = expand_weight.shape[1]
    group = mixed_own.shape[1]
    shift_by = (
        (count >= 2).astype(jnp.int32)
        + (count >= 4).astype(jnp.int32)
        + (count >= 8).astype(jnp.int32)
    )
    here = pl.ds(pl.multiple_of(head * group, group), group)
    there = pl.ds(pl.multiple_of((1 - head) * group, group), group)
    bias_grad[...] = jnp.zeros_like(bias_grad)
    gain_grads[...] = jnp.zeros_like(gain_grads)
    mover.wait("mixing", "tokens", "own", "other", "gain", "shift", "bias")

    def tile(step, _):
        at = pl.ds(pl.multiple_of(step * TILE, TILE), TILE)
        row = head * half + step * TILE + lax.broadcasted_iota(jnp.int32, (TILE, 1), 0)
        slot = row & (count - 1)
        limit = jnp.zeros_like(row)
        for s in range(lengths.shape[0]):
            limit = jnp.where(slot == s, lengths[s], limit)
        valid = (row >> shift_by) < limit

        def first_wait(*names):
            pl.when(step == 0)(lambda: mover.wait(*names))

        after = (
            tokens[at, :].astype(F32)
            + nn(mixed_own[at, :], mixing_weight[here, :])
            + nn(mixed_other[at, :], mixing_weight[there, :])
        )
        hat, scale = normalized(after)
        low = (hat * gain[...] + shift[...]).astype(BF16)
        middle[at, :] = low
        first_wait("expand", "shrink", "cotangent")
        grad_out = jnp.where(valid, cotangent[at, :].astype(F32), 0.0)
        grad_low = grad_out.astype(BF16)
        out_grad[at, :] = grad_low

        def products(c):
            cs = slice(c, c + PART)
            return nn(low, expand_weight[:, cs]), nt(grad_low, shrink_weight[cs, :])

        ahead = products(0)
        for c in range(0, hidden, PART):
            cs = slice(c, c + PART)
            now = ahead
            if c + PART < hidden:
                ahead = products(c + PART)
            act, slope = gelu_pair(now[0] + expand_bias[:, cs])
            active[at, cs] = act.astype(BF16)
            g = now[1] * slope
            bias_grad[0:1, cs] += jnp.sum(g, axis=0, keepdims=True)
            pre_grad[at, cs] = g.astype(BF16)
        g_middle = nt(pre_grad[at, :], expand_weight[...])
        grown = nn(active[at, :], shrink_weight[...])
        gain_grads[0:1, :] += jnp.sum(g_middle * hat, axis=0, keepdims=True)
        gain_grads[1:2, :] += jnp.sum(g_middle, axis=0, keepdims=True)
        y = g_middle * gain[...]
        g_after = grad_out + scale * (
            y
            - jnp.mean(y, axis=-1, keepdims=True)
            - hat * jnp.mean(y * hat, axis=-1, keepdims=True)
        )
        after_grad[at, :] = g_after
        g_low = g_after.astype(BF16)
        after_low[at, :] = g_low
        output[at, :] = jnp.where(valid, after + grown, 0.0).astype(BF16)
        send_own[at, :] = nt(g_low, mixing_weight[here, :]).astype(BF16)
        send_other[at, :] = nt(g_low, mixing_weight[there, :]).astype(BF16)
        return 0

    lax.fori_loop(0, half // TILE, tile, 0)

    for source, target in (
        (send_other, send_other_out),
        (send_own, send_own_out),
        (output, output_out),
        (after_grad, after_grad_out),
    ):
        mover.start(source, target)
    vectors[...] = jnp.zeros_like(vectors)
    for n, c in enumerate(range(0, hidden, width)):
        vectors[n : n + 1, :] = bias_grad[0:1, c : c + width]
    vectors[4:6, :] = gain_grads[0:2, :]
    mover.start(vectors, vectors_out)
    first_half = grads_own.shape[0] // 2
    for grads, stay_out, away_out, mixed, which, side in (
        (grads_other, other_stay_out, other_away_out, mixed_other, 1 - head, info[4]),
        (grads_own, own_stay_out, own_away_out, mixed_own, head, info[2]),
    ):
        stay = pl.ds(pl.multiple_of(side * first_half, 16), first_half)
        away = pl.ds(pl.multiple_of((1 - side) * first_half, 16), first_half)

        def weights(step, _, grads=grads, which=which):
            cs = pl.ds(pl.multiple_of((2 * which + step) * COLS, COLS), COLS)
            at = pl.multiple_of(step * COLS, COLS)
            grads[pl.ds(at, COLS), :] = tn(active[:, cs], out_grad[...]).astype(BF16)
            grads[pl.ds(2 * COLS + at, COLS), :] = tn(middle[...], pre_grad[:, cs]).astype(BF16)
            return 0

        lax.fori_loop(0, 2, weights, 0)
        grads[4 * COLS :, :] = tn(mixed[...], after_low[...]).astype(BF16)
        mover.start(grads.at[away], away_out)
        mover.start(grads.at[stay], stay_out)
    mover.wait_all()


def row_part(info, lengths, tokens, mixed_own, mixed_other, cotangent, wo, we, ws, bias, gain, shift):
    half, width = tokens.shape
    hidden = we.shape[1]
    group = mixed_own.shape[1]
    outs = [
        ((half, width), BF16),
        ((half, width), F32),
        ((half, group), BF16),
        ((half, group), BF16),
        *[(((hidden + group) // 2, width), BF16)] * 4,
        ((8, width), F32),
    ]
    args = (tokens, mixed_own, mixed_other, cotangent, wo, we, ws, bias, gain, shift)
    scratch = [
        *[(a.shape, a.dtype) for a in args],
        *outs[:4],
        ((hidden + group, width), BF16),
        ((hidden + group, width), BF16),
        outs[8],
        ((8, hidden), F32),
        ((8, width), F32),
        ((half, hidden), BF16),
        ((half, hidden), BF16),
        ((half, width), BF16),
        ((half, width), BF16),
        ((half, width), BF16),
    ]
    return run_kernel(
        rows_kernel, "row_part", (info, lengths), args, outs, scratch, 19, 15 * 10**9,
        limit=WHOLE_MIB,
    )


def arrange_gradient(count, head, grad_own, grad_other, mixed, grad, inner):
    half = grad_own.shape[0]
    total = 2 * half

    for rows_ref, which in ((grad_own, head), (grad_other, 1 - head)):

        def arrange(step, _, rows_ref=rows_ref, which=which):
            at = pl.ds(pl.multiple_of(step * BLOCK, BLOCK), BLOCK)
            tile = which * (half // BLOCK) + step
            rows = rows_ref[at, :]

            def put(count_here):
                value = rows
                if count_here > 1:
                    value = nn(sorter(count_here), rows).astype(BF16)
                for pair in range(2):

                    def write(dst, piece, pair=pair):
                        grad[pair, dst, :] = piece

                    store_grouped(
                        write, value[:, pair * 128 : (pair + 1) * 128], tile, total, count_here
                    )

            for option in SLOT_OPTIONS:
                pl.when(count == option)(partial(put, option))
            return 0

        lax.fori_loop(0, half // BLOCK, arrange, 0)

    def inners(block, _):
        at = pl.ds(pl.multiple_of(block * BLOCK, BLOCK), BLOCK)
        for pair in range(2):
            flipped = jnp.transpose(grad[pair, at, :].astype(F32) * mixed[pair, at, :].astype(F32))
            for sub in range(2):
                inner[pair, sub : sub + 1, at] = jnp.sum(
                    flipped[sub * 64 : (sub + 1) * 64], axis=0, keepdims=True
                )
        return 0

    lax.fori_loop(0, total // BLOCK, inners, 0)


def attend_blocks(
    count, first, last, query, keys, values, grad, logsum, inner, query_total, kept, key_sums, value_sums
):
    blocks = first + query.shape[1] // BLOCK
    per_slot = blocks // count
    lane = lax.broadcasted_iota(jnp.int32, (1, 128), 1)
    tri = lax.broadcasted_iota(jnp.int32, (BLOCK, BLOCK), 0) <= lax.broadcasted_iota(
        jnp.int32, (BLOCK, BLOCK), 1
    )

    def attend(block, _):
        more = per_slot - block % per_slot - 1
        here = pl.multiple_of((block - first) * BLOCK, BLOCK)
        at = pl.ds(here, BLOCK)

        def part(start, size, diagonal):
            span = pl.ds(pl.multiple_of(start, BLOCK), size)

            def score(h):
                pair, sub = h // 2, h % 2
                pick = (lane < 64) == (sub == 0)
                k, v = keys[pair, at, :], values[pair, at, :]
                k = jnp.where(pick, k, jnp.zeros_like(k))
                v = jnp.where(pick, v, jnp.zeros_like(v))
                return k, nt(k, query[pair, span, :]), nt(v, grad[pair, span, :])

            def finish(h, k, raw, grad_probs):
                pair, sub = h // 2, h % 2
                probs = jnp.exp2(raw - logsum[pair, sub : sub + 1, span])
                if diagonal:
                    probs = jnp.where(tri, probs, 0.0)
                grad_scores = (probs * (grad_probs - inner[pair, sub : sub + 1, span])).astype(BF16)
                grad_value = nn(probs.astype(BF16), grad[pair, span, :])
                grad_key = nn(grad_scores, query[pair, span, :])
                if diagonal:
                    value_sums[h], key_sums[h] = grad_value, grad_key
                else:
                    value_sums[h] += grad_value
                    key_sums[h] += grad_key
                return tn(grad_scores, k)

            ahead = score(0)
            done = []
            for h in range(4):
                now = ahead
                if h < 3:
                    ahead = score(h + 1)
                done.append(finish(h, *now))
                if h % 2:
                    query_total[h // 2, span, :] += done[h - 1] + done[h]

        part(here, BLOCK, True)

        def two(n, _):
            part(here + BLOCK + n * (2 * BLOCK), 2 * BLOCK, False)
            return 0

        lax.fori_loop(0, more // 2, two, 0)

        @pl.when(more % 2 == 1)
        def _():
            part(here + more * BLOCK, BLOCK, False)

        for pair in range(2):
            for start, sums, scale in ((0, key_sums, 1.0 / LOG2E), (256, value_sums, 1.0)):
                picked = jnp.where(lane < 64, sums[2 * pair], sums[2 * pair + 1])
                kept[at, start + pair * 128 : start + (pair + 1) * 128] = (picked * scale).astype(BF16)
        return 0

    lax.fori_loop(first, last, attend, 0)


def arrange_kernel(
    info, grad_own_in, grad_other_in, mixed_in, grad_out, inner_out,
    grad_own, grad_other, mixed, grad, inner, semaphores,
):
    mover = Mover(semaphores)
    for source, target in ((grad_own_in, grad_own), (grad_other_in, grad_other), (mixed_in, mixed)):
        mover.start(source, target)
    mover.wait_all()
    arrange_gradient(info[0], info[1], grad_own, grad_other, mixed, grad, inner)
    mover.start(grad, grad_out)
    mover.start(inner, inner_out)
    mover.wait_all()


def arrange_rows(info, grad_own, grad_other, mixed):
    total = mixed.shape[1]
    outs = [((2, total, 128), BF16), ((2, 8, total), F32)]
    args = (grad_own, grad_other, mixed)
    scratch = [(a.shape, BF16) for a in args] + outs
    return run_kernel(arrange_kernel, "arrange_rows", (info,), args, outs, scratch, 5, 10**8, limit=WHOLE_MIB)


def fetch_blocks(mover, first, last, sources, targets):
    query, keys, values, grad, logsum, inner, *before = sources
    total = query.shape[1]
    span, rows = pl.ds(first * BLOCK, total - first * BLOCK), pl.ds(first * BLOCK, (last - first) * BLOCK)
    for source, target in zip(
        (
            keys.at[:, rows], query.at[:, span], values.at[:, rows], grad.at[:, span],
            logsum.at[:, :, span], inner.at[:, :, span], *[b.at[:, span] for b in before],
        ),
        targets,
    ):
        mover.start(source, target)


def next_kernel(first, last, info, *refs):
    count = 7 if first else 6
    sources, (query_total_out, kept_out), local, (key_sums, value_sums, kept, semaphores) = (
        refs[:count], refs[count : count + 2], refs[count + 2 : count + 9], refs[count + 9 :]
    )
    mover = Mover(semaphores)
    fetch_blocks(mover, first, last, sources, local)
    keys, query, values, grad, logsum, inner, query_total = local
    if not first:
        query_total[...] = jnp.zeros_like(query_total)
    mover.wait_all()
    attend_blocks(
        info[0], first, last, query, keys, values, grad, logsum, inner, query_total, kept,
        key_sums, value_sums,
    )
    total = sources[0].shape[1]
    span = pl.ds(first * BLOCK, total - first * BLOCK)
    mover.start(query_total, query_total_out.at[:, span])
    mover.start(kept, kept_out)
    mover.wait_all()


def local_blocks(first, last, total):
    rows, span = (last - first) * BLOCK, total - first * BLOCK
    return [
        ((2, rows, 128), BF16),
        ((2, span, 128), BF16),
        ((2, rows, 128), BF16),
        ((2, span, 128), BF16),
        ((2, 8, span), F32),
        ((2, 8, span), F32),
        ((2, span, 128), F32),
        ((4, BLOCK, 128), F32),
        ((4, BLOCK, 128), F32),
    ]


def next_blocks(first, last, info, before, query, keys, values, grad, logsum, inner):
    outs = [(query.shape, F32), (((last - first) * BLOCK, 512), BF16)]
    args = (query, keys, values, grad, logsum, inner) + ((before,) if first else ())
    return run_kernel(
        partial(next_kernel, first, last), f"blocks_{first}", (info,), args, outs,
        local_blocks(first, last, query.shape[1]) + [outs[1]], 9, 5 * 10**9, {7: 0} if first else {},
    )


def last_kernel(first, pieces, info, *refs):
    sources, refs = refs[:7], refs[7:]
    normed_in, gain_in, shift_in, vectors_in, query_in, key_in, value_in = refs[:7]
    kept_in, refs = refs[7 : 7 + pieces], refs[7 + pieces :]
    stay_out, away_out, packed_out = refs[:3]
    local, (key_sums, value_sums, *refs) = refs[3:10], refs[10:]
    kept, normed, gain, shift, vectors, query_weight, key_weight, value_weight, before, weight_grad, packed, semaphores = refs
    keys, query, values, grad, logsum, inner, query_total = local
    total = packed.shape[0]
    head = info[1]
    cols = pl.ds(pl.multiple_of(head * 256, 256), 256)
    fresh_cols = pl.ds(pl.multiple_of(head * 128, 128), 128)
    mover = Mover(semaphores)
    fetch_blocks(mover, first, total // BLOCK, sources, local)
    mover.start(sources[6].at[:, pl.ds(0, first * BLOCK)], before, "before")
    mover.start(normed_in, normed, "normed")
    mover.start(vectors_in, vectors, "vectors")
    mover.start(gain_in, gain, "gain")
    mover.start(shift_in, shift, "shift")
    mover.start(query_in.at[:, cols], query_weight, "q")
    mover.start(key_in.at[:, cols], key_weight, "k")
    mover.start(value_in.at[:, fresh_cols], value_weight, "v")
    row = 0
    for n, piece in enumerate(kept_in):
        mover.start(piece, packed.at[pl.ds(row, piece.shape[0]), pl.ds(256, 512)], f"p{n}")
        row += piece.shape[0]
    mover.wait(*range(7))
    attend_blocks(
        info[0], first, total // BLOCK, query, keys, values, grad, logsum, inner, query_total, kept,
        key_sums, value_sums,
    )
    mover.wait_all()
    packed[row:, 256:] = kept[...]
    for pair in range(2):
        lanes = slice(pair * 128, (pair + 1) * 128)
        packed[:row, lanes] = (before[pair, :, :] * 0.125).astype(BF16)
        packed[row:, lanes] = (query_total[pair, :, :] * 0.125).astype(BF16)
    mover.start(packed, packed_out)
    ones = jnp.ones((8, total), BF16)
    gain_grad = jnp.zeros((gain.shape[1], 1), F32)
    shift_grad = jnp.zeros((gain.shape[1], 1), F32)
    gain_column = jnp.transpose(jnp.broadcast_to(gain[...], (128, gain.shape[1])))[:, :1]
    shift_column = jnp.transpose(jnp.broadcast_to(shift[...], (128, gain.shape[1])))[:, :1]
    for start, stop, weight in ((0, 256, query_weight), (256, 512, key_weight), (512, 640, value_weight)):
        part = packed[:, start:stop]
        product = tn(normed[...], part)
        sums = nn(ones, part)[0:1, :]
        weight_grad[:, start:stop] = product.astype(BF16)
        weight = weight[...].astype(F32)
        shift_grad += jnp.sum(weight * sums, axis=1, keepdims=True)
        gain_grad += jnp.sum(weight * (product - shift_column * sums), axis=1, keepdims=True)
    lane = lax.broadcasted_iota(jnp.int32, (1, 128), 1)
    edge = jnp.where(lane == 0, gain_grad / gain_column, jnp.where(lane == 1, shift_grad, 0.0))
    stack = jnp.concatenate([vectors[...], jnp.zeros((120, vectors.shape[1]), F32)], axis=0)
    edge += jnp.where(lane >= 8, pltpu.roll(jnp.transpose(stack), 8, 1), 0.0)
    weight_grad[:, 640:] = edge.astype(BF16)
    rows = weight_grad.shape[0] // 2
    mover.start(weight_grad.at[pl.ds(pl.multiple_of((1 - info[3]) * rows, 16), rows)], away_out)
    mover.start(weight_grad.at[pl.ds(pl.multiple_of(info[3] * rows, 16), rows)], stay_out)
    mover.wait_all()


def last_blocks(first, info, before, query, keys, values, grad, logsum, inner, normed, gain, shift, vectors, wq, wk, wv, kept):
    total, width = normed.shape
    outs = [((width // 2, 768), BF16), ((width // 2, 768), BF16), ((total, 768), BF16)]
    scratch = local_blocks(first, total // BLOCK, total) + [
        ((total - first * BLOCK, 512), BF16),
        (normed.shape, BF16),
        (gain.shape, F32),
        (shift.shape, F32),
        (vectors.shape, F32),
        ((width, 256), BF16),
        ((width, 256), BF16),
        ((width, 128), BF16),
        ((2, first * BLOCK, 128), F32),
        ((width, 768), BF16),
        outs[2],
    ]
    return run_kernel(
        partial(last_kernel, first, len(kept)), "last_blocks", (info,),
        (query, keys, values, grad, logsum, inner, before, normed, gain, shift, vectors, wq, wk, wv, *kept),
        outs, scratch, 18 + len(kept), 5 * 10**9,
    )


def back_kernel(
    info, packed_in, query_in, key_in, value_in, back_own_out, back_other_out, skip_own_out, skip_other_out,
    packed, query_weight, key_weight, value_weight, back_own, back_other, skip_own, skip_other, back, semaphores,
):
    count, head = info[0], info[1]
    total = packed.shape[0]
    half = total // 2
    cols = pl.ds(pl.multiple_of(head * 256, 256), 256)
    fresh_cols = pl.ds(pl.multiple_of(head * 128, 128), 128)
    mover = Mover(semaphores)
    mover.start(packed_in, packed)
    mover.start(query_in.at[:, cols], query_weight)
    mover.start(key_in.at[:, cols], key_weight)
    mover.start(value_in.at[:, fresh_cols], value_weight)
    mover.wait_all()

    def close(block, _):
        at = pl.ds(pl.multiple_of(block * BLOCK, BLOCK), BLOCK)
        back[at, :] = (
            nt(packed[at, :256], query_weight[...])
            + nt(packed[at, 256:512], key_weight[...])
            + nt(packed[at, 512:640], value_weight[...])
        ).astype(BF16)
        return 0

    lax.fori_loop(0, total // BLOCK, close, 0)

    for back_ref, skip_ref, back_out, skip_out, which in (
        (back_other, skip_other, back_other_out, skip_other_out, 1 - head),
        (back_own, skip_own, back_own_out, skip_own_out, head),
    ):

        def give(step, _, back_ref=back_ref, skip_ref=skip_ref, which=which):
            at = pl.ds(pl.multiple_of(step * BLOCK, BLOCK), BLOCK)
            tile = which * (half // BLOCK) + step

            def put(count_here):
                g = load_grouped(lambda s: back[s, :], tile, total, count_here)
                k = load_grouped(lambda s: packed[s, 640:], tile, total, count_here)
                if count_here > 1:
                    order = sorter(count_here, True)
                    g = nn(order, g).astype(BF16)
                    k = nn(order, k).astype(BF16)
                back_ref[at, :] = g
                skip_ref[at, :] = k

            for option in SLOT_OPTIONS:
                pl.when(count == option)(partial(put, option))
            return 0

        lax.fori_loop(0, half // BLOCK, give, 0)
        mover.start(back_ref, back_out)
        mover.start(skip_ref, skip_out)
    mover.wait_all()


def back_rows(info, packed, wq, wk, wv):
    total, width = packed.shape[0], wq.shape[0]
    half = total // 2
    outs = [((half, width), BF16), ((half, width), BF16), ((half, 128), BF16), ((half, 128), BF16)]
    scratch = [
        (packed.shape, BF16),
        ((width, 256), BF16),
        ((width, 256), BF16),
        ((width, 128), BF16),
        *outs,
        ((total, width), BF16),
    ]
    return run_kernel(
        back_kernel, "back_rows", (info,), (packed, wq, wk, wv), outs, scratch, 8, 2 * 10**9
    )


def close_kernel(
    info, tokens_in, after_grad_in, back_own_in, back_other_in, kept_in, arrived_in, gain_in,
    result_out, skip_out,
    tokens, after_grad, back_own, back_other, gain, result, skip_grad, semaphores,
):
    head = info[1]
    mover = Mover(semaphores)
    mover.start(gain_in, gain)
    mover.start(tokens_in, tokens)
    mover.start(after_grad_in, after_grad)
    mover.start(back_own_in, back_own)
    mover.start(back_other_in, back_other)
    mover.start(kept_in, skip_grad.at[:, pl.ds(pl.multiple_of(head * 128, 128), 128)])
    mover.start(arrived_in, skip_grad.at[:, pl.ds(pl.multiple_of((1 - head) * 128, 128), 128)])
    mover.wait_all()
    mover.start(skip_grad, skip_out)

    def tile(step, _):
        at = pl.ds(pl.multiple_of(step * BLOCK, BLOCK), BLOCK)
        hat, scale = normalized(tokens[at, :].astype(F32))
        y = (back_own[at, :].astype(F32) + back_other[at, :].astype(F32)) * gain[...]
        result[at, :] = (
            after_grad[at, :]
            + scale
            * (
                y
                - jnp.mean(y, axis=-1, keepdims=True)
                - hat * jnp.mean(y * hat, axis=-1, keepdims=True)
            )
        ).astype(BF16)
        return 0

    lax.fori_loop(0, tokens.shape[0] // BLOCK, tile, 0)
    mover.start(result, result_out)
    mover.wait_all()


def close_rows(info, tokens, after_grad, back_own, back_other, kept, arrived, gain):
    args = (tokens, after_grad, back_own, back_other, kept, arrived, gain)
    outs = [(tokens.shape, BF16), ((tokens.shape[0], 256), BF16)]
    scratch = [(a.shape, a.dtype) for a in args[:4]] + [(gain.shape, F32)] + outs
    return run_kernel(close_kernel, "close_rows", (info,), args, outs, scratch, 9, 10**8)


def unpack_kernel(late, info, *refs):
    half_in, refs = refs[0], refs[1 + (3 if late else 0) :]
    shrink_out, expand_out, mixing_out, half, wide, semaphores = refs
    which = 1 - info[1] if late else info[1]
    width = half.shape[1]
    top = 4 * COLS + mixing_out.shape[0] // 2
    mover = Mover(semaphores)
    for at in range(0, 4 * COLS, COLS):
        mover.start(half_in.at[pl.ds(at, COLS)], half.at[pl.ds(at, COLS)], at)
    mover.start(half_in.at[pl.ds(4 * COLS, half.shape[0] - 4 * COLS)], half.at[pl.ds(4 * COLS, half.shape[0] - 4 * COLS)], "rest")
    for at in range(0, 4 * COLS, COLS):
        mover.wait(at)
        wide[at : at + COLS, :] = half[at : at + COLS, :].astype(F32)
        if at < 2 * COLS:
            row = pl.multiple_of(which * 2 * COLS + at, COLS)
            mover.start(wide.at[pl.ds(at, COLS)], shrink_out.at[pl.ds(row, COLS)])
        else:
            col = pl.multiple_of(which * 2 * COLS + at - 2 * COLS, COLS)
            mover.start(wide.at[pl.ds(at, COLS)], expand_out.at[:, pl.ds(col, COLS)])
    mover.wait("rest")
    wide[4 * COLS :, :] = half[4 * COLS :, :].astype(F32)
    row = pl.multiple_of(which * (top - 4 * COLS), 256)
    mover.start(wide.at[pl.ds(4 * COLS, top - 4 * COLS)], mixing_out.at[pl.ds(row, top - 4 * COLS)])
    mover.wait_all()


def unpack_half(info, half, before=()):
    rows, width = half.shape
    hidden = 4 * COLS
    outs = [((hidden, width), F32), ((width, hidden), F32), ((width, width), F32)]
    scratch = [(half.shape, BF16), ((rows, width), F32)]
    return run_kernel(
        partial(unpack_kernel, bool(before)), "unpack_late" if before else "unpack_half", (info,),
        (half, *before), outs, scratch, 10, 10**8, {2 + n: n for n in range(3)} if before else {},
        limit=20,
    )


def split_kernel(
    info, mine_in, arrived_in, query_out, key_out, value_out, *refs
):
    vectors_out, (mine, arrived, query, key, value), vectors, semaphores = refs[:5], refs[5:10], refs[10:15], refs[15]
    head = info[1]
    mover = Mover(semaphores)
    mover.start(mine_in, mine)
    mover.start(arrived_in, arrived)
    mover.wait_all()
    for half, which in ((mine, head), (arrived, 1 - head)):
        for target, wide, at in ((query, 256, 0), (key, 256, 256), (value, 128, 512)):
            cols = pl.ds(pl.multiple_of(which * wide, 128), wide)
            target[:, cols] = half[:, at : at + wide].astype(F32)
    for source, target in ((query, query_out), (key, key_out), (value, value_out)):
        mover.start(source, target)
    edges = jnp.transpose(mine[:, 640:].astype(F32) + arrived[:, 640:].astype(F32))
    gain, shift, bias, middle_gain, middle_shift = vectors
    width = gain.shape[1]
    for target, at in ((gain, 0), (shift, 1), (middle_gain, 12), (middle_shift, 13)):
        target[...] = edges[at : at + 1]
    for n in range(bias.shape[1] // width):
        bias[:, n * width : (n + 1) * width] = edges[8 + n : 9 + n]
    for source, target in zip(vectors, vectors_out):
        mover.start(source, target)
    mover.wait_all()


def split_projection(info, mine, arrived):
    width = mine.shape[0]
    outs = [((width, 512), F32), ((width, 512), F32), ((width, 256), F32)]
    outs += [((1, n * width), F32) for n in (1, 1, 4, 1, 1)]
    scratch = [(mine.shape, BF16), (mine.shape, BF16)] + outs
    return run_kernel(split_kernel, "split_projection", (info,), (mine, arrived), outs, scratch, 10, 10**8, limit=20)


def swap_cores(array):
    return lax.ppermute(array, "head", [(0, 1), (1, 0)])


def half_of(array, which):
    rows = array.shape[0] // 2
    return lax.dynamic_slice_in_dim(array, which * rows, rows, 0)


def add_low(a, b):
    return (a.astype(F32) + b.astype(F32)).astype(BF16)


def join(mine, theirs, which):
    both = jnp.concatenate([mine, mine], axis=0)
    return lax.dynamic_update_slice_in_dim(both, theirs, (1 - which) * mine.shape[0], 0)


def after_all(first, *rest):
    return lax.optimization_barrier((first, *rest))


class SeqSum:
    def __init__(self, orders):
        self.size = lax.axis_size("seq")
        bits = self.size.bit_length() - 1
        self.orders = [
            [b for b in order if b < bits] + [b for b in range(bits) if b not in order]
            for order in orders
        ]
        self.stage, self.bits = 0, bits
        self.fitting, self.whole, self.kept = False, False, None

    def begin(self, stay, stay_come, away, away_come):
        self.mine, self.coming, self.half = stay, stay_come, None if stay_come is None else -1
        self.sent = away if away_come is None else add_low(away, away_come)
        self.next, self.stage, self.trail = 0, 1, [0]

    def which(self, stage, other=0):
        bit = jnp.where(lax.axis_index("head") == other, self.orders[0][stage], self.orders[1][stage])
        return (lax.axis_index("seq") >> bit) & 1

    def swap(self, array, stage):
        pairs = []
        for i in range(self.size):
            for core in range(2):
                pairs.append((2 * i + core, 2 * (i ^ (1 << self.orders[core][stage])) + core))
        return lax.ppermute(array, ("seq", "head"), pairs)

    def added(self, which=None):
        parts = [a if which is None else half_of(a, which) for a in (self.mine, self.coming) if a is not None]
        return parts[0] if len(parts) == 1 else add_low(*parts)

    def prepare(self):
        if self.stage < self.bits:
            self.settle()
            if self.stage < self.bits - 1 and self.mine.shape[0] % 32 == 0:
                which = self.which(self.stage)
                self.trail.append(self.stage)
                self.sent, self.half = self.added(1 - which), which
            else:
                self.sent = self.mine = self.added()
                self.coming = None
            self.next = self.stage
            self.stage += 1
            return True
        self.settle()
        if self.fitting:
            self.mine = join(self.mine, self.coming, self.which(self.next))
        else:
            self.mine, self.fitting = self.added(), True
        if not self.trail:
            return False
        self.next, self.sent = self.trail.pop(), self.mine
        return True

    def launch(self):
        self.kept = self.coming
        self.coming = self.swap(self.sent, self.next)

    def settle(self):
        if self.half is not None:
            parts = [a for a in (self.mine, self.kept) if a is not None]
            if not isinstance(self.half, int):
                parts = [half_of(a, self.half) for a in parts]
            self.mine = parts[0] if len(parts) == 1 else add_low(*parts)
            self.half = None

    def via(self, stage):
        return lambda array: self.swap(array, stage)

    def flow(self, ready, small):
        while ready or self.stage < self.bits or len(self.trail) > 3:
            if not ready:
                self.prepare()
            ready = False
            (came,) = yield [(self.via(self.next), self.sent)]
            self.kept, self.coming = self.coming, came
        self.settle()
        piece = join(self.mine, self.coming, self.which(self.next)) if self.fitting else self.added()
        far, mid, near = self.trail
        rows = piece.shape[0]
        if small:
            (came_near,) = yield [(self.via(near), piece)]
        else:
            came_near, got_own = yield [(self.via(near), piece), (self.via(far), piece)]
        both = join(piece, came_near, self.which(near))
        if small:
            came_mid, got = yield [(self.via(mid), both), (self.via(far), both)]
            self.mine = join(both, came_mid, self.which(mid))
            got_mid, other_mine = yield [(self.via(far), came_mid), (swap_cores, self.mine)]
        else:
            (came_mid,) = yield [(self.via(mid), both)]
            cut = rows // 32 * 16
            (first,) = yield [(self.via(far), jnp.concatenate([came_near, came_mid[:cut]], axis=0))]
            (second,) = yield [(self.via(far), came_mid[cut:])]
            got = join(got_own, first[:rows], self.which(near))
            got_mid = jnp.concatenate([first[rows:], second], axis=0)
            self.mine = join(both, came_mid, self.which(mid))
        theirs = join(got, got_mid, self.which(mid))
        self.mine = join(self.mine, theirs, self.which(far))
        self.whole = True
        if small:
            (other_theirs,) = yield [(swap_cores, theirs)]
            self.other = join(other_mine, other_theirs, self.which(far, 1))
        else:
            (self.other,) = yield [(swap_cores, self.mine)]


ORDERS = ((0, 1, 2, 3), (1, 2, 3, 0))
PROJECTION_ORDERS = ((0, 1, 2, 3), (1, 0, 2, 3))
CUTS = (0, 2, 5, 8)


def on_device(
    tokens, first_values, cotangent, slot_count, seq_lengths, query_weight, key_weight, value_weight,
    mixing_weight, expand_weight, shrink_weight, expand_bias, before_gain, before_shift,
    middle_gain, middle_shift,
):
    head = lax.axis_index("head")
    sums, projection = SeqSum(ORDERS), SeqSum(PROJECTION_ORDERS)
    info = jnp.stack([slot_count[0], head, sums.which(0), projection.which(0), sums.which(0, 1)])
    info = info.astype(jnp.int32)
    lengths = seq_lengths[0]
    row = lambda v: v.reshape(1, -1)

    other = swap_cores(tokens)
    skip_other = swap_cores(first_values)
    mixed_own, mixed_away, query, keys, values, mixed, logsum, normed = forward_attention(
        info, tokens, other, first_values, skip_other, query_weight, key_weight, value_weight,
        row(before_gain), row(before_shift),
    )
    mixed_other = swap_cores(mixed_away)
    output, after_grad, grad_own, grad_away, own_stay, own_away, other_stay, other_away, row_vectors = row_part(
        info, lengths, tokens, mixed_own, mixed_other, cotangent, mixing_weight, expand_weight,
        shrink_weight, row(expand_bias), row(middle_gain), row(middle_shift),
    )
    grad_other = swap_cores(grad_away)
    grad_other, other_away = after_all(grad_other, other_away)
    away_come = swap_cores(other_away)
    grad, inner = arrange_rows(info, grad_own, grad_other, mixed)
    grad, away_come = after_all(grad, away_come)
    sums.begin(own_stay, swap_cores(other_stay), own_away, away_come)
    attention = (query, keys, values, grad, logsum, inner)
    query_total, pieces = None, []
    for first, last in zip(CUTS, CUTS[1:]):
        if first > 0:
            sums.prepare()
        *attention, sums.sent = after_all(*attention, sums.sent)
        sums.launch()
        if last < CUTS[-1]:
            query_total, kept = next_blocks(first, last, info, query_total, *attention)
            pieces.append(kept)
            query_total, sums.coming, sums.mine, sums.kept = after_all(
                query_total, sums.coming, sums.mine, sums.kept
            )
        else:
            projection_stay, projection_away, packed = last_blocks(
                first, info, query_total, *attention, normed, row(before_gain), row(before_shift),
                row_vectors, query_weight, key_weight, value_weight, pieces,
            )
            packed, sums.coming, sums.mine, sums.kept = after_all(packed, sums.coming, sums.mine, sums.kept)
    projection.begin(projection_stay, None, projection_away, None)

    lanes = [projection.flow(True, True), sums.flow(False, False)]
    pending = [next(lane) for lane in lanes]
    work, made, extra, finished = 0, None, (), False
    while pending:
        inputs = ()
        if work == 0:
            inputs, kernel = (packed,), lambda p: back_rows(info, p, query_weight, key_weight, value_weight)
        elif work == 1:
            extra = (back_away, skip_away)
        elif work == 2:
            inputs, kernel = (back_other, skip_arrived), lambda b, k: close_rows(
                info, tokens, after_grad, back_own, b, skip_own, k, row(before_gain)
            )
        elif sums.whole and made is None:
            inputs, kernel = (sums.mine,), lambda m: unpack_half(info, m)
        elif made is not None and not finished:
            inputs, kernel, finished = (sums.other, *made), lambda o, *m: unpack_half(info, o, tuple(m)), True
        moves = [move for group in pending for move in group]
        tied = after_all(*[array for _, array in moves], *extra, *inputs)
        count = len(moves)
        came = [swap(a) for (swap, _), a in zip(moves, tied)]
        came += [swap_cores(a) for a in tied[count : count + len(extra)]]
        results = kernel(*tied[count + len(extra) :]) if inputs else ()
        tied = after_all(*came, *results)
        came, results = tied[: len(came)], tied[len(came) :]
        if work == 0:
            back_own, back_away, skip_own, skip_away = results
        elif work == 1:
            back_other, skip_arrived = came[count:]
        elif work == 2:
            input_grad, skip_grad = results
        elif results:
            made = results
        work, extra = work + 1, ()
        later = []
        came = list(came)
        for lane, group in zip(lanes, pending):
            mine, came = came[: len(group)], came[len(group) :]
            try:
                later.append((lane, lane.send(mine)))
            except StopIteration:
                pass
        lanes, pending = [lane for lane, _ in later], [p for _, p in later]
    if made is None:
        made = unpack_half(info, sums.mine)
    if not finished:
        made = unpack_half(info, sums.other, tuple(made))
    shrink_grad, expand_grad, mixing_grad = made
    query_grad, key_grad, value_grad, *edges = split_projection(info, projection.mine, projection.other)
    before_gain_grad, before_shift_grad, bias_grad, middle_gain_grad, middle_shift_grad = [
        v.reshape(-1) for v in edges
    ]
    return (
        output, input_grad, skip_grad, query_grad, key_grad, value_grad, mixing_grad, expand_grad,
        shrink_grad, bias_grad, before_gain_grad, before_shift_grad, middle_gain_grad, middle_shift_grad,
    )


def solution(mesh):
    rows = P(("seq", "head"), None)
    return jax.shard_map(
        on_device,
        mesh=mesh,
        in_specs=(rows, rows, rows, P("seq"), P("seq", None)) + (P(),) * 11,
        out_specs=(rows, rows, rows) + (P(),) * 11,
        check_vma=False,
    )
```

```python
from functools import partial
import math
import jax
import jax.numpy as jnp
from jax import lax
from jax.experimental import pallas as pl
from jax.experimental.pallas import tpu as pltpu
from jax.sharding import PartitionSpec as P

BLOCK = 256
SLOT_OPTIONS = (1, 2, 4, 8)
LOG2E = math.log2(math.e)
F32, BF16 = jnp.float32, jnp.bfloat16
MASKED = -1e30
EPS = 1e-05
MIB = 1 << 20
VMEM_MIB, WHOLE_MIB = 56, 58


def nn(a, b):
    return lax.dot_general(a, b, (((1,), (0,)), ((), ())), preferred_element_type=F32)


def nt(a, b):
    return lax.dot_general(a, b, (((1,), (1,)), ((), ())), preferred_element_type=F32)


def tn(a, b):
    return lax.dot_general(a, b, (((0,), (0,)), ((), ())), preferred_element_type=F32)


def sorter(count, transposed=False):
    each = BLOCK // count
    grouped = lax.broadcasted_iota(jnp.int32, (BLOCK, BLOCK), 1 if transposed else 0)
    plain = lax.broadcasted_iota(jnp.int32, (BLOCK, BLOCK), 0 if transposed else 1)
    place = (plain & (count - 1)) * each + (plain >> (count.bit_length() - 1))
    return jnp.where(grouped == place, 1.0, 0.0).astype(BF16)


def store_grouped(write, values, tile, total, count):
    each = BLOCK // count
    for group in range(count):
        start = pl.multiple_of(group * (total // count) + tile * each, each)
        write(pl.ds(start, each), values[group * each : (group + 1) * each])


def load_grouped(read, tile, total, count):
    each = BLOCK // count
    parts = []
    for group in range(count):
        start = pl.multiple_of(group * (total // count) + tile * each, each)
        parts.append(read(pl.ds(start, each)))
    return parts[0] if count == 1 else jnp.concatenate(parts, axis=0)


def normalized(rows):
    average = jnp.mean(rows, axis=-1, keepdims=True)
    centred = rows - average
    spread = jnp.mean(centred * centred, axis=-1, keepdims=True)
    scale = lax.rsqrt(spread + EPS)
    return centred * scale, scale


def as_columns(vectors):
    stack = jnp.concatenate(vectors + [jnp.zeros((128 - len(vectors), vectors[0].shape[1]), F32)], axis=0)
    return jnp.transpose(stack).astype(BF16)


def forward_kernel(
    info, own_in, other_in, skip_own_in, skip_other_in, query_in, key_in, value_in, gain_in, shift_in,
    mixed_own_out, mixed_other_out, query_out, keys_out, saved_out, mixed_out, logsum_out, normed_out,
    own, other, skip_own, skip_other, query_weight, key_weight, value_weight,
    mixed_own, mixed_other, query, keys, saved, mixed, logsum, normed, values, gain, shift, semaphores,
):
    count, head = info[0], info[1]
    half = own.shape[0]
    total = 2 * half
    blocks = total // BLOCK
    cols = pl.ds(pl.multiple_of(head * 256, 256), 256)
    fresh_cols = pl.ds(pl.multiple_of(head * 128, 128), 128)
    mover = Mover(semaphores)
    mover.start(own_in, own, "own")
    mover.start(gain_in, gain, "gain")
    mover.start(shift_in, shift, "shift")
    mover.start(query_in.at[:, cols], query_weight, "q")
    mover.start(key_in.at[:, cols], key_weight, "k")
    mover.start(value_in.at[:, fresh_cols], value_weight, "v")
    mover.start(skip_own_in.at[:, fresh_cols], skip_own, "skip")
    values[:, :, 128:] = jnp.ones((2, total, 128), BF16)

    for rows_ref, skip_ref, which, needs in (
        (own, skip_own, head, ("own", "gain", "shift", "q", "k", "v", "skip")),
        (other, skip_other, 1 - head, ("other", "skip_other")),
    ):
        mover.wait(*needs)
        if needs[0] == "own":
            mover.start(other_in, other, "other")
            mover.start(skip_other_in.at[:, fresh_cols], skip_other, "skip_other")

        def project(step, _, rows_ref=rows_ref, skip_ref=skip_ref, which=which):
            at = pl.ds(pl.multiple_of(step * BLOCK, BLOCK), BLOCK)
            tile = which * (half // BLOCK) + step
            hat, _s = normalized(rows_ref[at, :].astype(F32))
            low = (hat * gain[...] + shift[...]).astype(BF16)
            skip = skip_ref[at, :]

            def put(count_here):
                rows, skipped = low, skip
                if count_here > 1:
                    order = sorter(count_here)
                    rows = nn(order, low).astype(BF16)
                    skipped = nn(order, skip).astype(BF16)
                q = nn(rows, query_weight[...]).astype(BF16)
                q = (q.astype(F32) * (0.125 * LOG2E)).astype(BF16)
                k = nn(rows, key_weight[...]).astype(BF16)
                f = nn(rows, value_weight[...]).astype(BF16)

                def put_in(ref, part, value):
                    def write(dst, piece):
                        if part is None:
                            ref[dst, :] = piece
                        else:
                            ref[part, dst, :128] = piece
                            if ref is values:
                                saved[part, dst, :] = piece

                    store_grouped(write, value, tile, total, count_here)

                put_in(normed, None, rows)
                put_in(query, 0, q[:, :128])
                put_in(query, 1, q[:, 128:])
                put_in(keys, 0, k[:, :128])
                put_in(keys, 1, k[:, 128:])
                put_in(values, 0, f)
                put_in(values, 1, skipped)

            for option in SLOT_OPTIONS:
                pl.when(count == option)(partial(put, option))
            return 0

        lax.fori_loop(0, half // BLOCK, project, 0)

    for source, target in ((query, query_out), (keys, keys_out), (saved, saved_out), (normed, normed_out)):
        mover.start(source, target)

    per_slot = blocks // count
    lane = lax.broadcasted_iota(jnp.int32, (1, 128), 1)
    tri = lax.broadcasted_iota(jnp.int32, (BLOCK, BLOCK), 1) <= lax.broadcasted_iota(
        jnp.int32, (BLOCK, BLOCK), 0
    )

    def attend(block, _):
        width = block % per_slot + 1
        here = pl.multiple_of(block * BLOCK, BLOCK)

        def run(wide):
            first = pl.multiple_of((block - (wide - 1)) * BLOCK, BLOCK)

            def score(h):
                pair, sub = h // 2, h % 2
                q = query[pair, pl.ds(here, BLOCK), :]
                qm = jnp.where((lane < 64) == (sub == 0), q, jnp.zeros_like(q))
                diag = nt(qm, keys[pair, pl.ds(here, BLOCK), :])
                rest = None
                if wide > 1:
                    rest = nt(qm, keys[pair, pl.ds(first, (wide - 1) * BLOCK), :])
                return diag, rest

            def soften(diag, rest):
                diag = jnp.where(tri, diag, MASKED)
                top = jnp.max(diag, axis=1, keepdims=True)
                if wide > 1:
                    top = jnp.maximum(top, jnp.max(rest, axis=1, keepdims=True))
                raised = [jnp.exp2(diag - top).astype(BF16)]
                if wide > 1:
                    raised.append(jnp.exp2(rest - top).astype(BF16))
                return top, raised

            def finish(h, top, raised):
                acc = nn(raised[0], values[h // 2, pl.ds(here, BLOCK), :])
                if wide > 1:
                    acc += nn(raised[1], values[h // 2, pl.ds(first, (wide - 1) * BLOCK), :])
                sums = acc[:, 128:]
                return acc[:, :128] / sums, jnp.transpose(top + jnp.log2(sums))[0:1, :]

            scores = [score(h) for h in range(4)]
            softened = [soften(*scores[h]) for h in range(4)]
            outs = [finish(h, *softened[h]) for h in range(4)]
            for pair in range(2):
                mixed[pair, pl.ds(here, BLOCK), :] = jnp.where(lane < 64, outs[2*pair][0], outs[2*pair+1][0]).astype(BF16)
                for sub in range(2):
                    logsum[pair, sub : sub + 1, pl.ds(here, BLOCK)] = outs[2*pair+sub][1]

        for wide in range(1, blocks + 1):
            pl.when(width == wide)(partial(run, wide))
        return 0

    lax.fori_loop(0, blocks, attend, 0)
    mover.start(mixed, mixed_out)
    mover.start(logsum, logsum_out)

    for out_ref, target, which in (
        (mixed_other, mixed_other_out, 1 - head),
        (mixed_own, mixed_own_out, head),
    ):

        def give(step, _, out_ref=out_ref, which=which):
            at = pl.ds(pl.multiple_of(step * BLOCK, BLOCK), BLOCK)
            tile = which * (half // BLOCK) + step

            def put(count_here):
                for pair in range(2):
                    part = load_grouped(lambda s: mixed[pair, s, :], tile, total, count_here)
                    if count_here > 1:
                        part = nn(sorter(count_here, True), part).astype(BF16)
                    out_ref[at, pair * 128 : (pair + 1) * 128] = part

            for option in SLOT_OPTIONS:
                pl.when(count == option)(partial(put, option))
            return 0

        lax.fori_loop(0, half // BLOCK, give, 0)
        mover.start(out_ref, target)
    mover.wait_all()


class Mover:
    def __init__(self, semaphores):
        self.semaphores, self.used, self.open = semaphores, 0, {}

    def start(self, source, target, name=None):
        copy = pltpu.make_async_copy(source, target, self.semaphores.at[self.used])
        copy.start()
        self.open[self.used if name is None else name] = copy
        self.used += 1

    def wait(self, *names):
        for name in names:
            self.open.pop(name).wait()

    def wait_all(self):
        self.wait(*list(self.open))


def run_kernel(kernel, name, scalars, args, outs, scratch, moves, flops, aliases=None, limit=VMEM_MIB):
    smem = pl.BlockSpec(memory_space=pltpu.SMEM)
    large = pl.BlockSpec(memory_space=pl.ANY)
    size = lambda shape, dtype: math.prod(shape) * jnp.dtype(dtype).itemsize
    moved = sum(size(a.shape, a.dtype) for a in args) + sum(size(*o) for o in outs)
    return pl.pallas_call(
        kernel,
        in_specs=[smem] * len(scalars) + [large] * len(args),
        out_specs=[large] * len(outs),
        out_shape=[jax.ShapeDtypeStruct(*o) for o in outs],
        scratch_shapes=[pltpu.VMEM(*s) for s in scratch] + [pltpu.SemaphoreType.DMA((moves,))],
        input_output_aliases=aliases or {},
        cost_estimate=pl.CostEstimate(flops=flops, bytes_accessed=moved, transcendentals=0),
        compiler_params=pltpu.CompilerParams(vmem_limit_bytes=limit * MIB),
        name=name,
    )(*scalars, *args)


def forward_attention(info, own, other, skip_own, skip_other, wq, wk, wv, gain, shift):
    half, width = own.shape
    total = 2 * half
    group = wq.shape[1] // 2
    outs = [
        ((half, group), BF16),
        ((half, group), BF16),
        ((2, total, 128), BF16),
        ((2, total, 128), BF16),
        ((2, total, 128), BF16),
        ((2, total, 128), BF16),
        ((2, 8, total), F32),
        ((total, width), BF16),
    ]
    scratch = [
        ((half, width), BF16),
        ((half, width), BF16),
        ((half, 128), BF16),
        ((half, 128), BF16),
        ((width, group), BF16),
        ((width, group), BF16),
        ((width, 128), BF16),
        *outs,
        ((2, total, 256), BF16),
        (gain.shape, F32),
        (shift.shape, F32),
    ]
    return run_kernel(
        forward_kernel, "forward_attention", (info,),
        (own, other, skip_own, skip_other, wq, wk, wv, gain, shift), outs, scratch, 17, 10 * 10**9,
        limit=WHOLE_MIB,
    )


COLS = 512
TILE, PART = 512, 256
GELU_SLOPE = math.sqrt(2.0 / math.pi)
GELU_CUBE = 0.044715


def gelu_pair(v):
    square = v * v
    bend = jnp.tanh(v * (GELU_SLOPE + (GELU_SLOPE * GELU_CUBE) * square))
    front = 0.5 + 0.5 * bend
    steep = v * (2.0 * GELU_SLOPE + (6.0 * GELU_SLOPE * GELU_CUBE) * square)
    return v * front, front + steep * (front * (1.0 - front))


def rows_kernel(
    info, lengths, tokens_in, mixed_own_in, mixed_other_in, cotangent_in, mixing_in, expand_in,
    shrink_in, bias_in, gain_in, shift_in,
    output_out, after_grad_out, send_own_out, send_other_out,
    own_stay_out, own_away_out, other_stay_out, other_away_out, vectors_out,
    tokens, mixed_own, mixed_other, cotangent, mixing_weight, expand_weight, shrink_weight,
    expand_bias, gain, shift, output, after_grad, send_own, send_other, grads_own, grads_other,
    vectors, bias_grad, gain_grads, active, pre_grad, middle, out_grad, after_low, semaphores,
):
    mover = Mover(semaphores)
    for source, target, name in (
        (mixing_in, mixing_weight, "mixing"),
        (tokens_in, tokens, "tokens"),
        (mixed_own_in, mixed_own, "own"),
        (mixed_other_in, mixed_other, "other"),
        (gain_in, gain, "gain"),
        (shift_in, shift, "shift"),
        (bias_in, expand_bias, "bias"),
        (expand_in, expand_weight, "expand"),
        (shrink_in, shrink_weight, "shrink"),
        (cotangent_in, cotangent, "cotangent"),
    ):
        mover.start(source, target, name)
    count, head = info[0], info[1]
    half, width = tokens.shape
    hidden = expand_weight.shape[1]
    group = mixed_own.shape[1]
    shift_by = (
        (count >= 2).astype(jnp.int32)
        + (count >= 4).astype(jnp.int32)
        + (count >= 8).astype(jnp.int32)
    )
    here = pl.ds(pl.multiple_of(head * group, group), group)
    there = pl.ds(pl.multiple_of((1 - head) * group, group), group)
    bias_grad[...] = jnp.zeros_like(bias_grad)
    gain_grads[...] = jnp.zeros_like(gain_grads)
    mover.wait("mixing", "tokens", "own", "other", "gain", "shift", "bias")

    def tile(step, _):
        at = pl.ds(pl.multiple_of(step * TILE, TILE), TILE)
        row = head * half + step * TILE + lax.broadcasted_iota(jnp.int32, (TILE, 1), 0)
        slot = row & (count - 1)
        limit = jnp.zeros_like(row)
        for s in range(lengths.shape[0]):
            limit = jnp.where(slot == s, lengths[s], limit)
        valid = (row >> shift_by) < limit

        def first_wait(*names):
            pl.when(step == 0)(lambda: mover.wait(*names))

        after = (
            tokens[at, :].astype(F32)
            + nn(mixed_own[at, :], mixing_weight[here, :])
            + nn(mixed_other[at, :], mixing_weight[there, :])
        )
        hat, scale = normalized(after)
        low = (hat * gain[...] + shift[...]).astype(BF16)
        middle[at, :] = low
        first_wait("expand", "shrink", "cotangent")
        grad_out = jnp.where(valid, cotangent[at, :].astype(F32), 0.0)
        grad_low = grad_out.astype(BF16)
        out_grad[at, :] = grad_low

        def products(c):
            cs = slice(c, c + PART)
            return nn(low, expand_weight[:, cs]), nt(grad_low, shrink_weight[cs, :])

        ahead = products(0)
        for c in range(0, hidden, PART):
            cs = slice(c, c + PART)
            now = ahead
            if c + PART < hidden:
                ahead = products(c + PART)
            act, slope = gelu_pair(now[0] + expand_bias[:, cs])
            active[at, cs] = act.astype(BF16)
            g = now[1] * slope
            bias_grad[0:1, cs] += jnp.sum(g, axis=0, keepdims=True)
            pre_grad[at, cs] = g.astype(BF16)
        g_middle = nt(pre_grad[at, :], expand_weight[...])
        grown = nn(active[at, :], shrink_weight[...])
        gain_grads[0:1, :] += jnp.sum(g_middle * hat, axis=0, keepdims=True)
        gain_grads[1:2, :] += jnp.sum(g_middle, axis=0, keepdims=True)
        y = g_middle * gain[...]
        g_after = grad_out + scale * (
            y
            - jnp.mean(y, axis=-1, keepdims=True)
            - hat * jnp.mean(y * hat, axis=-1, keepdims=True)
        )
        after_grad[at, :] = g_after
        g_low = g_after.astype(BF16)
        after_low[at, :] = g_low
        output[at, :] = jnp.where(valid, after + grown, 0.0).astype(BF16)
        send_own[at, :] = nt(g_low, mixing_weight[here, :]).astype(BF16)
        send_other[at, :] = nt(g_low, mixing_weight[there, :]).astype(BF16)
        return 0

    lax.fori_loop(0, half // TILE, tile, 0)

    for source, target in (
        (send_other, send_other_out),
        (send_own, send_own_out),
        (output, output_out),
        (after_grad, after_grad_out),
    ):
        mover.start(source, target)
    vectors[...] = jnp.zeros_like(vectors)
    for n, c in enumerate(range(0, hidden, width)):
        vectors[n : n + 1, :] = bias_grad[0:1, c : c + width]
    vectors[4:6, :] = gain_grads[0:2, :]
    mover.start(vectors, vectors_out)
    first_half = grads_own.shape[0] // 2
    for grads, stay_out, away_out, mixed, which, side in (
        (grads_other, other_stay_out, other_away_out, mixed_other, 1 - head, info[4]),
        (grads_own, own_stay_out, own_away_out, mixed_own, head, info[2]),
    ):
        stay = pl.ds(pl.multiple_of(side * first_half, 16), first_half)
        away = pl.ds(pl.multiple_of((1 - side) * first_half, 16), first_half)

        def weights(step, _, grads=grads, which=which):
            cs = pl.ds(pl.multiple_of((2 * which + step) * COLS, COLS), COLS)
            at = pl.multiple_of(step * COLS, COLS)
            grads[pl.ds(at, COLS), :] = tn(active[:, cs], out_grad[...]).astype(BF16)
            grads[pl.ds(2 * COLS + at, COLS), :] = tn(middle[...], pre_grad[:, cs]).astype(BF16)
            return 0

        lax.fori_loop(0, 2, weights, 0)
        grads[4 * COLS :, :] = tn(mixed[...], after_low[...]).astype(BF16)
        mover.start(grads.at[away], away_out)
        mover.start(grads.at[stay], stay_out)
    mover.wait_all()


def row_part(info, lengths, tokens, mixed_own, mixed_other, cotangent, wo, we, ws, bias, gain, shift):
    half, width = tokens.shape
    hidden = we.shape[1]
    group = mixed_own.shape[1]
    outs = [
        ((half, width), BF16),
        ((half, width), F32),
        ((half, group), BF16),
        ((half, group), BF16),
        *[(((hidden + group) // 2, width), BF16)] * 4,
        ((8, width), F32),
    ]
    args = (tokens, mixed_own, mixed_other, cotangent, wo, we, ws, bias, gain, shift)
    scratch = [
        *[(a.shape, a.dtype) for a in args],
        *outs[:4],
        ((hidden + group, width), BF16),
        ((hidden + group, width), BF16),
        outs[8],
        ((8, hidden), F32),
        ((8, width), F32),
        ((half, hidden), BF16),
        ((half, hidden), BF16),
        ((half, width), BF16),
        ((half, width), BF16),
        ((half, width), BF16),
    ]
    return run_kernel(
        rows_kernel, "row_part", (info, lengths), args, outs, scratch, 19, 15 * 10**9,
        limit=WHOLE_MIB,
    )


def arrange_gradient(count, head, grad_own, grad_other, mixed, grad, inner):
    half = grad_own.shape[0]
    total = 2 * half

    for rows_ref, which in ((grad_own, head), (grad_other, 1 - head)):

        def arrange(step, _, rows_ref=rows_ref, which=which):
            at = pl.ds(pl.multiple_of(step * BLOCK, BLOCK), BLOCK)
            tile = which * (half // BLOCK) + step
            rows = rows_ref[at, :]

            def put(count_here):
                value = rows
                if count_here > 1:
                    value = nn(sorter(count_here), rows).astype(BF16)
                for pair in range(2):

                    def write(dst, piece, pair=pair):
                        grad[pair, dst, :] = piece

                    store_grouped(
                        write, value[:, pair * 128 : (pair + 1) * 128], tile, total, count_here
                    )

            for option in SLOT_OPTIONS:
                pl.when(count == option)(partial(put, option))
            return 0

        lax.fori_loop(0, half // BLOCK, arrange, 0)

    def inners(block, _):
        at = pl.ds(pl.multiple_of(block * BLOCK, BLOCK), BLOCK)
        for pair in range(2):
            flipped = jnp.transpose(grad[pair, at, :].astype(F32) * mixed[pair, at, :].astype(F32))
            for sub in range(2):
                inner[pair, sub : sub + 1, at] = jnp.sum(
                    flipped[sub * 64 : (sub + 1) * 64], axis=0, keepdims=True
                )
        return 0

    lax.fori_loop(0, total // BLOCK, inners, 0)


def attend_blocks(
    count, first, last, query, keys, values, grad, logsum, inner, query_total, kept, key_sums, value_sums
):
    blocks = first + query.shape[1] // BLOCK
    per_slot = blocks // count
    lane = lax.broadcasted_iota(jnp.int32, (1, 128), 1)
    tri = lax.broadcasted_iota(jnp.int32, (BLOCK, BLOCK), 0) <= lax.broadcasted_iota(
        jnp.int32, (BLOCK, BLOCK), 1
    )

    def attend(block, _):
        more = per_slot - block % per_slot - 1
        here = pl.multiple_of((block - first) * BLOCK, BLOCK)
        at = pl.ds(here, BLOCK)

        def part(start, size, diagonal):
            span = pl.ds(pl.multiple_of(start, BLOCK), size)

            def score(h):
                pair, sub = h // 2, h % 2
                pick = (lane < 64) == (sub == 0)
                k, v = keys[pair, at, :], values[pair, at, :]
                k = jnp.where(pick, k, jnp.zeros_like(k))
                v = jnp.where(pick, v, jnp.zeros_like(v))
                return k, nt(k, query[pair, span, :]), nt(v, grad[pair, span, :])

            def finish(h, k, raw, grad_probs):
                pair, sub = h // 2, h % 2
                probs = jnp.exp2(raw - logsum[pair, sub : sub + 1, span])
                if diagonal:
                    probs = jnp.where(tri, probs, 0.0)
                grad_scores = (probs * (grad_probs - inner[pair, sub : sub + 1, span])).astype(BF16)
                grad_value = nn(probs.astype(BF16), grad[pair, span, :])
                grad_key = nn(grad_scores, query[pair, span, :])
                if diagonal:
                    value_sums[h], key_sums[h] = grad_value, grad_key
                else:
                    value_sums[h] += grad_value
                    key_sums[h] += grad_key
                return tn(grad_scores, k)

            ahead = score(0)
            done = []
            for h in range(4):
                now = ahead
                if h < 3:
                    ahead = score(h + 1)
                done.append(finish(h, *now))
                if h % 2:
                    query_total[h // 2, span, :] += done[h - 1] + done[h]

        part(here, BLOCK, True)

        def two(n, _):
            part(here + BLOCK + n * (2 * BLOCK), 2 * BLOCK, False)
            return 0

        lax.fori_loop(0, more // 2, two, 0)

        @pl.when(more % 2 == 1)
        def _():
            part(here + more * BLOCK, BLOCK, False)

        for pair in range(2):
            for start, sums, scale in ((0, key_sums, 1.0 / LOG2E), (256, value_sums, 1.0)):
                picked = jnp.where(lane < 64, sums[2 * pair], sums[2 * pair + 1])
                kept[at, start + pair * 128 : start + (pair + 1) * 128] = (picked * scale).astype(BF16)
        return 0

    lax.fori_loop(first, last, attend, 0)


def arrange_kernel(
    info, grad_own_in, grad_other_in, mixed_in, grad_out, inner_out,
    grad_own, grad_other, mixed, grad, inner, semaphores,
):
    mover = Mover(semaphores)
    for source, target in ((grad_own_in, grad_own), (grad_other_in, grad_other), (mixed_in, mixed)):
        mover.start(source, target)
    mover.wait_all()
    arrange_gradient(info[0], info[1], grad_own, grad_other, mixed, grad, inner)
    mover.start(grad, grad_out)
    mover.start(inner, inner_out)
    mover.wait_all()


def arrange_rows(info, grad_own, grad_other, mixed):
    total = mixed.shape[1]
    outs = [((2, total, 128), BF16), ((2, 8, total), F32)]
    args = (grad_own, grad_other, mixed)
    scratch = [(a.shape, BF16) for a in args] + outs
    return run_kernel(arrange_kernel, "arrange_rows", (info,), args, outs, scratch, 5, 10**8, limit=WHOLE_MIB)


def fetch_blocks(mover, first, last, sources, targets):
    query, keys, values, grad, logsum, inner, *before = sources
    total = query.shape[1]
    span, rows = pl.ds(first * BLOCK, total - first * BLOCK), pl.ds(first * BLOCK, (last - first) * BLOCK)
    for source, target in zip(
        (
            keys.at[:, rows], query.at[:, span], values.at[:, rows], grad.at[:, span],
            logsum.at[:, :, span], inner.at[:, :, span], *[b.at[:, span] for b in before],
        ),
        targets,
    ):
        mover.start(source, target)


def next_kernel(first, last, info, *refs):
    count = 7 if first else 6
    sources, (query_total_out, kept_out), local, (key_sums, value_sums, kept, semaphores) = (
        refs[:count], refs[count : count + 2], refs[count + 2 : count + 9], refs[count + 9 :]
    )
    mover = Mover(semaphores)
    fetch_blocks(mover, first, last, sources, local)
    keys, query, values, grad, logsum, inner, query_total = local
    if not first:
        query_total[...] = jnp.zeros_like(query_total)
    mover.wait_all()
    attend_blocks(
        info[0], first, last, query, keys, values, grad, logsum, inner, query_total, kept,
        key_sums, value_sums,
    )
    total = sources[0].shape[1]
    span = pl.ds(first * BLOCK, total - first * BLOCK)
    mover.start(query_total, query_total_out.at[:, span])
    mover.start(kept, kept_out)
    mover.wait_all()


def local_blocks(first, last, total):
    rows, span = (last - first) * BLOCK, total - first * BLOCK
    return [
        ((2, rows, 128), BF16),
        ((2, span, 128), BF16),
        ((2, rows, 128), BF16),
        ((2, span, 128), BF16),
        ((2, 8, span), F32),
        ((2, 8, span), F32),
        ((2, span, 128), F32),
        ((4, BLOCK, 128), F32),
        ((4, BLOCK, 128), F32),
    ]


def next_blocks(first, last, info, before, query, keys, values, grad, logsum, inner):
    outs = [(query.shape, F32), (((last - first) * BLOCK, 512), BF16)]
    args = (query, keys, values, grad, logsum, inner) + ((before,) if first else ())
    return run_kernel(
        partial(next_kernel, first, last), f"blocks_{first}", (info,), args, outs,
        local_blocks(first, last, query.shape[1]) + [outs[1]], 9, 5 * 10**9, {7: 0} if first else {},
    )


def last_kernel(first, pieces, info, *refs):
    sources, refs = refs[:7], refs[7:]
    normed_in, gain_in, shift_in, vectors_in, query_in, key_in, value_in = refs[:7]
    kept_in, refs = refs[7 : 7 + pieces], refs[7 + pieces :]
    stay_out, away_out, packed_out = refs[:3]
    local, (key_sums, value_sums, *refs) = refs[3:10], refs[10:]
    kept, normed, gain, shift, vectors, query_weight, key_weight, value_weight, before, weight_grad, packed, semaphores = refs
    keys, query, values, grad, logsum, inner, query_total = local
    total = packed.shape[0]
    head = info[1]
    cols = pl.ds(pl.multiple_of(head * 256, 256), 256)
    fresh_cols = pl.ds(pl.multiple_of(head * 128, 128), 128)
    mover = Mover(semaphores)
    fetch_blocks(mover, first, total // BLOCK, sources, local)
    mover.start(sources[6].at[:, pl.ds(0, first * BLOCK)], before, "before")
    mover.start(normed_in, normed, "normed")
    mover.start(vectors_in, vectors, "vectors")
    mover.start(gain_in, gain, "gain")
    mover.start(shift_in, shift, "shift")
    mover.start(query_in.at[:, cols], query_weight, "q")
    mover.start(key_in.at[:, cols], key_weight, "k")
    mover.start(value_in.at[:, fresh_cols], value_weight, "v")
    row = 0
    for n, piece in enumerate(kept_in):
        mover.start(piece, packed.at[pl.ds(row, piece.shape[0]), pl.ds(256, 512)], f"p{n}")
        row += piece.shape[0]
    mover.wait(*range(7))
    attend_blocks(
        info[0], first, total // BLOCK, query, keys, values, grad, logsum, inner, query_total, kept,
        key_sums, value_sums,
    )
    mover.wait_all()
    packed[row:, 256:] = kept[...]
    for pair in range(2):
        lanes = slice(pair * 128, (pair + 1) * 128)
        packed[:row, lanes] = (before[pair, :, :] * 0.125).astype(BF16)
        packed[row:, lanes] = (query_total[pair, :, :] * 0.125).astype(BF16)
    mover.start(packed, packed_out)
    ones = jnp.ones((8, total), BF16)
    gain_grad = jnp.zeros((gain.shape[1], 1), F32)
    shift_grad = jnp.zeros((gain.shape[1], 1), F32)
    gain_column = jnp.transpose(jnp.broadcast_to(gain[...], (128, gain.shape[1])))[:, :1]
    shift_column = jnp.transpose(jnp.broadcast_to(shift[...], (128, gain.shape[1])))[:, :1]
    for start, stop, weight in ((0, 256, query_weight), (256, 512, key_weight), (512, 640, value_weight)):
        part = packed[:, start:stop]
        product = tn(normed[...], part)
        sums = nn(ones, part)[0:1, :]
        weight_grad[:, start:stop] = product.astype(BF16)
        weight = weight[...].astype(F32)
        shift_grad += jnp.sum(weight * sums, axis=1, keepdims=True)
        gain_grad += jnp.sum(weight * (product - shift_column * sums), axis=1, keepdims=True)
    lane = lax.broadcasted_iota(jnp.int32, (1, 128), 1)
    edge = jnp.where(lane == 0, gain_grad / gain_column, jnp.where(lane == 1, shift_grad, 0.0))
    stack = jnp.concatenate([vectors[...], jnp.zeros((120, vectors.shape[1]), F32)], axis=0)
    edge += jnp.where(lane >= 8, pltpu.roll(jnp.transpose(stack), 8, 1), 0.0)
    weight_grad[:, 640:] = edge.astype(BF16)
    rows = weight_grad.shape[0] // 2
    mover.start(weight_grad.at[pl.ds(pl.multiple_of((1 - info[3]) * rows, 16), rows)], away_out)
    mover.start(weight_grad.at[pl.ds(pl.multiple_of(info[3] * rows, 16), rows)], stay_out)
    mover.wait_all()


def last_blocks(first, info, before, query, keys, values, grad, logsum, inner, normed, gain, shift, vectors, wq, wk, wv, kept):
    total, width = normed.shape
    outs = [((width // 2, 768), BF16), ((width // 2, 768), BF16), ((total, 768), BF16)]
    scratch = local_blocks(first, total // BLOCK, total) + [
        ((total - first * BLOCK, 512), BF16),
        (normed.shape, BF16),
        (gain.shape, F32),
        (shift.shape, F32),
        (vectors.shape, F32),
        ((width, 256), BF16),
        ((width, 256), BF16),
        ((width, 128), BF16),
        ((2, first * BLOCK, 128), F32),
        ((width, 768), BF16),
        outs[2],
    ]
    return run_kernel(
        partial(last_kernel, first, len(kept)), "last_blocks", (info,),
        (query, keys, values, grad, logsum, inner, before, normed, gain, shift, vectors, wq, wk, wv, *kept),
        outs, scratch, 18 + len(kept), 5 * 10**9,
    )


def back_kernel(
    info, packed_in, query_in, key_in, value_in, back_own_out, back_other_out, skip_own_out, skip_other_out,
    packed, query_weight, key_weight, value_weight, back_own, back_other, skip_own, skip_other, back, semaphores,
):
    count, head = info[0], info[1]
    total = packed.shape[0]
    half = total // 2
    cols = pl.ds(pl.multiple_of(head * 256, 256), 256)
    fresh_cols = pl.ds(pl.multiple_of(head * 128, 128), 128)
    mover = Mover(semaphores)
    mover.start(packed_in, packed)
    mover.start(query_in.at[:, cols], query_weight)
    mover.start(key_in.at[:, cols], key_weight)
    mover.start(value_in.at[:, fresh_cols], value_weight)
    mover.wait_all()

    def close(block, _):
        at = pl.ds(pl.multiple_of(block * BLOCK, BLOCK), BLOCK)
        back[at, :] = (
            nt(packed[at, :256], query_weight[...])
            + nt(packed[at, 256:512], key_weight[...])
            + nt(packed[at, 512:640], value_weight[...])
        ).astype(BF16)
        return 0

    lax.fori_loop(0, total // BLOCK, close, 0)

    for back_ref, skip_ref, back_out, skip_out, which in (
        (back_other, skip_other, back_other_out, skip_other_out, 1 - head),
        (back_own, skip_own, back_own_out, skip_own_out, head),
    ):

        def give(step, _, back_ref=back_ref, skip_ref=skip_ref, which=which):
            at = pl.ds(pl.multiple_of(step * BLOCK, BLOCK), BLOCK)
            tile = which * (half // BLOCK) + step

            def put(count_here):
                g = load_grouped(lambda s: back[s, :], tile, total, count_here)
                k = load_grouped(lambda s: packed[s, 640:], tile, total, count_here)
                if count_here > 1:
                    order = sorter(count_here, True)
                    g = nn(order, g).astype(BF16)
                    k = nn(order, k).astype(BF16)
                back_ref[at, :] = g
                skip_ref[at, :] = k

            for option in SLOT_OPTIONS:
                pl.when(count == option)(partial(put, option))
            return 0

        lax.fori_loop(0, half // BLOCK, give, 0)
        mover.start(back_ref, back_out)
        mover.start(skip_ref, skip_out)
    mover.wait_all()


def back_rows(info, packed, wq, wk, wv):
    total, width = packed.shape[0], wq.shape[0]
    half = total // 2
    outs = [((half, width), BF16), ((half, width), BF16), ((half, 128), BF16), ((half, 128), BF16)]
    scratch = [
        (packed.shape, BF16),
        ((width, 256), BF16),
        ((width, 256), BF16),
        ((width, 128), BF16),
        *outs,
        ((total, width), BF16),
    ]
    return run_kernel(
        back_kernel, "back_rows", (info,), (packed, wq, wk, wv), outs, scratch, 8, 2 * 10**9
    )


def close_kernel(
    info, tokens_in, after_grad_in, back_own_in, back_other_in, kept_in, arrived_in, gain_in,
    result_out, skip_out,
    tokens, after_grad, back_own, back_other, gain, result, skip_grad, semaphores,
):
    head = info[1]
    mover = Mover(semaphores)
    mover.start(gain_in, gain)
    mover.start(tokens_in, tokens)
    mover.start(after_grad_in, after_grad)
    mover.start(back_own_in, back_own)
    mover.start(back_other_in, back_other)
    mover.start(kept_in, skip_grad.at[:, pl.ds(pl.multiple_of(head * 128, 128), 128)])
    mover.start(arrived_in, skip_grad.at[:, pl.ds(pl.multiple_of((1 - head) * 128, 128), 128)])
    mover.wait_all()
    mover.start(skip_grad, skip_out)

    def tile(step, _):
        at = pl.ds(pl.multiple_of(step * BLOCK, BLOCK), BLOCK)
        hat, scale = normalized(tokens[at, :].astype(F32))
        y = (back_own[at, :].astype(F32) + back_other[at, :].astype(F32)) * gain[...]
        result[at, :] = (
            after_grad[at, :]
            + scale
            * (
                y
                - jnp.mean(y, axis=-1, keepdims=True)
                - hat * jnp.mean(y * hat, axis=-1, keepdims=True)
            )
        ).astype(BF16)
        return 0

    lax.fori_loop(0, tokens.shape[0] // BLOCK, tile, 0)
    mover.start(result, result_out)
    mover.wait_all()


def close_rows(info, tokens, after_grad, back_own, back_other, kept, arrived, gain):
    args = (tokens, after_grad, back_own, back_other, kept, arrived, gain)
    outs = [(tokens.shape, BF16), ((tokens.shape[0], 256), BF16)]
    scratch = [(a.shape, a.dtype) for a in args[:4]] + [(gain.shape, F32)] + outs
    return run_kernel(close_kernel, "close_rows", (info,), args, outs, scratch, 9, 10**8)


def unpack_kernel(late, info, *refs):
    half_in, refs = refs[0], refs[1 + (3 if late else 0) :]
    shrink_out, expand_out, mixing_out, half, wide, semaphores = refs
    which = 1 - info[1] if late else info[1]
    width = half.shape[1]
    top = 4 * COLS + mixing_out.shape[0] // 2
    mover = Mover(semaphores)
    for at in range(0, 4 * COLS, COLS):
        mover.start(half_in.at[pl.ds(at, COLS)], half.at[pl.ds(at, COLS)], at)
    mover.start(half_in.at[pl.ds(4 * COLS, half.shape[0] - 4 * COLS)], half.at[pl.ds(4 * COLS, half.shape[0] - 4 * COLS)], "rest")
    for at in range(0, 4 * COLS, COLS):
        mover.wait(at)
        wide[at : at + COLS, :] = half[at : at + COLS, :].astype(F32)
        if at < 2 * COLS:
            row = pl.multiple_of(which * 2 * COLS + at, COLS)
            mover.start(wide.at[pl.ds(at, COLS)], shrink_out.at[pl.ds(row, COLS)])
        else:
            col = pl.multiple_of(which * 2 * COLS + at - 2 * COLS, COLS)
            mover.start(wide.at[pl.ds(at, COLS)], expand_out.at[:, pl.ds(col, COLS)])
    mover.wait("rest")
    wide[4 * COLS :, :] = half[4 * COLS :, :].astype(F32)
    row = pl.multiple_of(which * (top - 4 * COLS), 256)
    mover.start(wide.at[pl.ds(4 * COLS, top - 4 * COLS)], mixing_out.at[pl.ds(row, top - 4 * COLS)])
    mover.wait_all()


def unpack_half(info, half, before=()):
    rows, width = half.shape
    hidden = 4 * COLS
    outs = [((hidden, width), F32), ((width, hidden), F32), ((width, width), F32)]
    scratch = [(half.shape, BF16), ((rows, width), F32)]
    return run_kernel(
        partial(unpack_kernel, bool(before)), "unpack_late" if before else "unpack_half", (info,),
        (half, *before), outs, scratch, 10, 10**8, {2 + n: n for n in range(3)} if before else {},
        limit=20,
    )


def split_kernel(
    info, mine_in, arrived_in, query_out, key_out, value_out, *refs
):
    vectors_out, (mine, arrived, query, key, value), vectors, semaphores = refs[:5], refs[5:10], refs[10:15], refs[15]
    head = info[1]
    mover = Mover(semaphores)
    mover.start(mine_in, mine)
    mover.start(arrived_in, arrived)
    mover.wait_all()
    for half, which in ((mine, head), (arrived, 1 - head)):
        for target, wide, at in ((query, 256, 0), (key, 256, 256), (value, 128, 512)):
            cols = pl.ds(pl.multiple_of(which * wide, 128), wide)
            target[:, cols] = half[:, at : at + wide].astype(F32)
    for source, target in ((query, query_out), (key, key_out), (value, value_out)):
        mover.start(source, target)
    edges = jnp.transpose(mine[:, 640:].astype(F32) + arrived[:, 640:].astype(F32))
    gain, shift, bias, middle_gain, middle_shift = vectors
    width = gain.shape[1]
    for target, at in ((gain, 0), (shift, 1), (middle_gain, 12), (middle_shift, 13)):
        target[...] = edges[at : at + 1]
    for n in range(bias.shape[1] // width):
        bias[:, n * width : (n + 1) * width] = edges[8 + n : 9 + n]
    for source, target in zip(vectors, vectors_out):
        mover.start(source, target)
    mover.wait_all()


def split_projection(info, mine, arrived):
    width = mine.shape[0]
    outs = [((width, 512), F32), ((width, 512), F32), ((width, 256), F32)]
    outs += [((1, n * width), F32) for n in (1, 1, 4, 1, 1)]
    scratch = [(mine.shape, BF16), (mine.shape, BF16)] + outs
    return run_kernel(split_kernel, "split_projection", (info,), (mine, arrived), outs, scratch, 10, 10**8, limit=20)


def swap_cores(array):
    return lax.ppermute(array, "head", [(0, 1), (1, 0)])


def half_of(array, which):
    rows = array.shape[0] // 2
    return lax.dynamic_slice_in_dim(array, which * rows, rows, 0)


def add_low(a, b):
    return (a.astype(F32) + b.astype(F32)).astype(BF16)


def join(mine, theirs, which):
    both = jnp.concatenate([mine, mine], axis=0)
    return lax.dynamic_update_slice_in_dim(both, theirs, (1 - which) * mine.shape[0], 0)


def after_all(first, *rest):
    return lax.optimization_barrier((first, *rest))


class SeqSum:
    def __init__(self, orders):
        self.size = lax.axis_size("seq")
        bits = self.size.bit_length() - 1
        self.orders = [
            [b for b in order if b < bits] + [b for b in range(bits) if b not in order]
            for order in orders
        ]
        self.stage, self.bits = 0, bits
        self.fitting, self.whole, self.kept = False, False, None

    def begin(self, stay, stay_come, away, away_come):
        self.mine, self.coming, self.half = stay, stay_come, None if stay_come is None else -1
        self.sent = away if away_come is None else add_low(away, away_come)
        self.next, self.stage, self.trail = 0, 1, [0]

    def which(self, stage, other=0):
        bit = jnp.where(lax.axis_index("head") == other, self.orders[0][stage], self.orders[1][stage])
        return (lax.axis_index("seq") >> bit) & 1

    def swap(self, array, stage):
        pairs = []
        for i in range(self.size):
            for core in range(2):
                pairs.append((2 * i + core, 2 * (i ^ (1 << self.orders[core][stage])) + core))
        return lax.ppermute(array, ("seq", "head"), pairs)

    def added(self, which=None):
        parts = [a if which is None else half_of(a, which) for a in (self.mine, self.coming) if a is not None]
        return parts[0] if len(parts) == 1 else add_low(*parts)

    def prepare(self):
        if self.stage < self.bits:
            self.settle()
            if self.stage < self.bits - 1 and self.mine.shape[0] % 32 == 0:
                which = self.which(self.stage)
                self.trail.append(self.stage)
                self.sent, self.half = self.added(1 - which), which
            else:
                self.sent = self.mine = self.added()
                self.coming = None
            self.next = self.stage
            self.stage += 1
            return True
        self.settle()
        if self.fitting:
            self.mine = join(self.mine, self.coming, self.which(self.next))
        else:
            self.mine, self.fitting = self.added(), True
        if not self.trail:
            return False
        self.next, self.sent = self.trail.pop(), self.mine
        return True

    def launch(self):
        self.kept = self.coming
        self.coming = self.swap(self.sent, self.next)

    def settle(self):
        if self.half is not None:
            parts = [a for a in (self.mine, self.kept) if a is not None]
            if not isinstance(self.half, int):
                parts = [half_of(a, self.half) for a in parts]
            self.mine = parts[0] if len(parts) == 1 else add_low(*parts)
            self.half = None

    def via(self, stage):
        return lambda array: self.swap(array, stage)

    def flow(self, ready, small):
        while ready or self.stage < self.bits or len(self.trail) > 3:
            if not ready:
                self.prepare()
            ready = False
            (came,) = yield [(self.via(self.next), self.sent)]
            self.kept, self.coming = self.coming, came
        self.settle()
        piece = join(self.mine, self.coming, self.which(self.next)) if self.fitting else self.added()
        far, mid, near = self.trail
        rows = piece.shape[0]
        if small:
            (came_near,) = yield [(self.via(near), piece)]
        else:
            came_near, got_own = yield [(self.via(near), piece), (self.via(far), piece)]
        both = join(piece, came_near, self.which(near))
        if small:
            came_mid, got = yield [(self.via(mid), both), (self.via(far), both)]
            self.mine = join(both, came_mid, self.which(mid))
            got_mid, other_mine = yield [(self.via(far), came_mid), (swap_cores, self.mine)]
        else:
            (came_mid,) = yield [(self.via(mid), both)]
            cut = rows // 32 * 16
            (first,) = yield [(self.via(far), jnp.concatenate([came_near, came_mid[:cut]], axis=0))]
            (second,) = yield [(self.via(far), came_mid[cut:])]
            got = join(got_own, first[:rows], self.which(near))
            got_mid = jnp.concatenate([first[rows:], second], axis=0)
            self.mine = join(both, came_mid, self.which(mid))
        theirs = join(got, got_mid, self.which(mid))
        self.mine = join(self.mine, theirs, self.which(far))
        self.whole = True
        if small:
            (other_theirs,) = yield [(swap_cores, theirs)]
            self.other = join(other_mine, other_theirs, self.which(far, 1))
        else:
            (self.other,) = yield [(swap_cores, self.mine)]


ORDERS = ((0, 1, 2, 3), (1, 0, 3, 2))
PROJECTION_ORDERS = ((0, 1, 2, 3), (1, 0, 2, 3))
CUTS = (0, 2, 5, 8)


def on_device(
    tokens, first_values, cotangent, slot_count, seq_lengths, query_weight, key_weight, value_weight,
    mixing_weight, expand_weight, shrink_weight, expand_bias, before_gain, before_shift,
    middle_gain, middle_shift,
):
    head = lax.axis_index("head")
    sums, projection = SeqSum(ORDERS), SeqSum(PROJECTION_ORDERS)
    info = jnp.stack([slot_count[0], head, sums.which(0), projection.which(0), sums.which(0, 1)])
    info = info.astype(jnp.int32)
    lengths = seq_lengths[0]
    row = lambda v: v.reshape(1, -1)

    other = swap_cores(tokens)
    skip_other = swap_cores(first_values)
    mixed_own, mixed_away, query, keys, values, mixed, logsum, normed = forward_attention(
        info, tokens, other, first_values, skip_other, query_weight, key_weight, value_weight,
        row(before_gain), row(before_shift),
    )
    mixed_other = swap_cores(mixed_away)
    output, after_grad, grad_own, grad_away, own_stay, own_away, other_stay, other_away, row_vectors = row_part(
        info, lengths, tokens, mixed_own, mixed_other, cotangent, mixing_weight, expand_weight,
        shrink_weight, row(expand_bias), row(middle_gain), row(middle_shift),
    )
    grad_other = swap_cores(grad_away)
    grad_other, other_away = after_all(grad_other, other_away)
    away_come = swap_cores(other_away)
    grad, inner = arrange_rows(info, grad_own, grad_other, mixed)
    grad, away_come = after_all(grad, away_come)
    sums.begin(own_stay, swap_cores(other_stay), own_away, away_come)
    attention = (query, keys, values, grad, logsum, inner)
    query_total, pieces = None, []
    for first, last in zip(CUTS, CUTS[1:]):
        if first > 0:
            sums.prepare()
        *attention, sums.sent = after_all(*attention, sums.sent)
        sums.launch()
        if last < CUTS[-1]:
            query_total, kept = next_blocks(first, last, info, query_total, *attention)
            pieces.append(kept)
            query_total, sums.coming, sums.mine, sums.kept = after_all(
                query_total, sums.coming, sums.mine, sums.kept
            )
        else:
            projection_stay, projection_away, packed = last_blocks(
                first, info, query_total, *attention, normed, row(before_gain), row(before_shift),
                row_vectors, query_weight, key_weight, value_weight, pieces,
            )
            packed, sums.coming, sums.mine, sums.kept = after_all(packed, sums.coming, sums.mine, sums.kept)
    projection.begin(projection_stay, None, projection_away, None)

    lanes = [projection.flow(True, True), sums.flow(False, False)]
    pending = [next(lane) for lane in lanes]
    work, made, extra, finished = 0, None, (), False
    while pending:
        inputs = ()
        if work == 0:
            inputs, kernel = (packed,), lambda p: back_rows(info, p, query_weight, key_weight, value_weight)
        elif work == 1:
            extra = (back_away, skip_away)
        elif work == 2:
            inputs, kernel = (back_other, skip_arrived), lambda b, k: close_rows(
                info, tokens, after_grad, back_own, b, skip_own, k, row(before_gain)
            )
        elif sums.whole and made is None:
            inputs, kernel = (sums.mine,), lambda m: unpack_half(info, m)
        elif made is not None and not finished:
            inputs, kernel, finished = (sums.other, *made), lambda o, *m: unpack_half(info, o, tuple(m)), True
        moves = [move for group in pending for move in group]
        tied = after_all(*[array for _, array in moves], *extra, *inputs)
        count = len(moves)
        came = [swap(a) for (swap, _), a in zip(moves, tied)]
        came += [swap_cores(a) for a in tied[count : count + len(extra)]]
        results = kernel(*tied[count + len(extra) :]) if inputs else ()
        tied = after_all(*came, *results)
        came, results = tied[: len(came)], tied[len(came) :]
        if work == 0:
            back_own, back_away, skip_own, skip_away = results
        elif work == 1:
            back_other, skip_arrived = came[count:]
        elif work == 2:
            input_grad, skip_grad = results
        elif results:
            made = results
        work, extra = work + 1, ()
        later = []
        came = list(came)
        for lane, group in zip(lanes, pending):
            mine, came = came[: len(group)], came[len(group) :]
            try:
                later.append((lane, lane.send(mine)))
            except StopIteration:
                pass
        lanes, pending = [lane for lane, _ in later], [p for _, p in later]
    if made is None:
        made = unpack_half(info, sums.mine)
    if not finished:
        made = unpack_half(info, sums.other, tuple(made))
    shrink_grad, expand_grad, mixing_grad = made
    query_grad, key_grad, value_grad, *edges = split_projection(info, projection.mine, projection.other)
    before_gain_grad, before_shift_grad, bias_grad, middle_gain_grad, middle_shift_grad = [
        v.reshape(-1) for v in edges
    ]
    return (
        output, input_grad, skip_grad, query_grad, key_grad, value_grad, mixing_grad, expand_grad,
        shrink_grad, bias_grad, before_gain_grad, before_shift_grad, middle_gain_grad, middle_shift_grad,
    )


def solution(mesh):
    rows = P(("seq", "head"), None)
    return jax.shard_map(
        on_device,
        mesh=mesh,
        in_specs=(rows, rows, rows, P("seq"), P("seq", None)) + (P(),) * 11,
        out_specs=(rows, rows, rows) + (P(),) * 11,
        check_vma=False,
    )
```

```python
from functools import partial
import math
import jax
import jax.numpy as jnp
from jax import lax
from jax.experimental import pallas as pl
from jax.experimental.pallas import tpu as pltpu
from jax.sharding import PartitionSpec as P

BLOCK = 256
SLOT_OPTIONS = (1, 2, 4, 8)
LOG2E = math.log2(math.e)
F32, BF16 = jnp.float32, jnp.bfloat16
MASKED = -1e30
EPS = 1e-05
MIB = 1 << 20
VMEM_MIB, WHOLE_MIB = 56, 58


def nn(a, b):
    return lax.dot_general(a, b, (((1,), (0,)), ((), ())), preferred_element_type=F32)


def nt(a, b):
    return lax.dot_general(a, b, (((1,), (1,)), ((), ())), preferred_element_type=F32)


def tn(a, b):
    return lax.dot_general(a, b, (((0,), (0,)), ((), ())), preferred_element_type=F32)


def sorter(count, transposed=False):
    each = BLOCK // count
    grouped = lax.broadcasted_iota(jnp.int32, (BLOCK, BLOCK), 1 if transposed else 0)
    plain = lax.broadcasted_iota(jnp.int32, (BLOCK, BLOCK), 0 if transposed else 1)
    place = (plain & (count - 1)) * each + (plain >> (count.bit_length() - 1))
    return jnp.where(grouped == place, 1.0, 0.0).astype(BF16)


def store_grouped(write, values, tile, total, count):
    each = BLOCK // count
    for group in range(count):
        start = pl.multiple_of(group * (total // count) + tile * each, each)
        write(pl.ds(start, each), values[group * each : (group + 1) * each])


def load_grouped(read, tile, total, count):
    each = BLOCK // count
    parts = []
    for group in range(count):
        start = pl.multiple_of(group * (total // count) + tile * each, each)
        parts.append(read(pl.ds(start, each)))
    return parts[0] if count == 1 else jnp.concatenate(parts, axis=0)


def normalized(rows):
    average = jnp.mean(rows, axis=-1, keepdims=True)
    centred = rows - average
    spread = jnp.mean(centred * centred, axis=-1, keepdims=True)
    scale = lax.rsqrt(spread + EPS)
    return centred * scale, scale


def as_columns(vectors):
    stack = jnp.concatenate(vectors + [jnp.zeros((128 - len(vectors), vectors[0].shape[1]), F32)], axis=0)
    return jnp.transpose(stack).astype(BF16)


def forward_kernel(
    info, own_in, other_in, skip_own_in, skip_other_in, query_in, key_in, value_in, gain_in, shift_in,
    mixed_own_out, mixed_other_out, query_out, keys_out, saved_out, mixed_out, logsum_out, normed_out,
    own, other, skip_own, skip_other, query_weight, key_weight, value_weight,
    mixed_own, mixed_other, query, keys, saved, mixed, logsum, normed, values, gain, shift, semaphores,
):
    count, head = info[0], info[1]
    half = own.shape[0]
    total = 2 * half
    blocks = total // BLOCK
    cols = pl.ds(pl.multiple_of(head * 256, 256), 256)
    fresh_cols = pl.ds(pl.multiple_of(head * 128, 128), 128)
    mover = Mover(semaphores)
    mover.start(own_in, own, "own")
    mover.start(gain_in, gain, "gain")
    mover.start(shift_in, shift, "shift")
    mover.start(query_in.at[:, cols], query_weight, "q")
    mover.start(key_in.at[:, cols], key_weight, "k")
    mover.start(value_in.at[:, fresh_cols], value_weight, "v")
    mover.start(skip_own_in.at[:, fresh_cols], skip_own, "skip")
    values[:, :, 128:] = jnp.ones((2, total, 128), BF16)

    for rows_ref, skip_ref, which, needs in (
        (own, skip_own, head, ("own", "gain", "shift", "q", "k", "v", "skip")),
        (other, skip_other, 1 - head, ("other", "skip_other")),
    ):
        mover.wait(*needs)
        if needs[0] == "own":
            mover.start(other_in, other, "other")
            mover.start(skip_other_in.at[:, fresh_cols], skip_other, "skip_other")

        def project(step, _, rows_ref=rows_ref, skip_ref=skip_ref, which=which):
            at = pl.ds(pl.multiple_of(step * BLOCK, BLOCK), BLOCK)
            tile = which * (half // BLOCK) + step
            hat, _s = normalized(rows_ref[at, :].astype(F32))
            low = (hat * gain[...] + shift[...]).astype(BF16)
            skip = skip_ref[at, :]

            def put(count_here):
                rows, skipped = low, skip
                if count_here > 1:
                    order = sorter(count_here)
                    rows = nn(order, low).astype(BF16)
                    skipped = nn(order, skip).astype(BF16)
                q = nn(rows, query_weight[...]).astype(BF16)
                q = (q.astype(F32) * (0.125 * LOG2E)).astype(BF16)
                k = nn(rows, key_weight[...]).astype(BF16)
                f = nn(rows, value_weight[...]).astype(BF16)

                def put_in(ref, part, value):
                    def write(dst, piece):
                        if part is None:
                            ref[dst, :] = piece
                        else:
                            ref[part, dst, :128] = piece
                            if ref is values:
                                saved[part, dst, :] = piece

                    store_grouped(write, value, tile, total, count_here)

                put_in(normed, None, rows)
                put_in(query, 0, q[:, :128])
                put_in(query, 1, q[:, 128:])
                put_in(keys, 0, k[:, :128])
                put_in(keys, 1, k[:, 128:])
                put_in(values, 0, f)
                put_in(values, 1, skipped)

            for option in SLOT_OPTIONS:
                pl.when(count == option)(partial(put, option))
            return 0

        lax.fori_loop(0, half // BLOCK, project, 0)

    for source, target in ((query, query_out), (keys, keys_out), (saved, saved_out), (normed, normed_out)):
        mover.start(source, target)

    per_slot = blocks // count
    lane = lax.broadcasted_iota(jnp.int32, (1, 128), 1)
    tri = lax.broadcasted_iota(jnp.int32, (BLOCK, BLOCK), 1) <= lax.broadcasted_iota(
        jnp.int32, (BLOCK, BLOCK), 0
    )

    def attend(block, _):
        width = block % per_slot + 1
        here = pl.multiple_of(block * BLOCK, BLOCK)

        def run(wide):
            first = pl.multiple_of((block - (wide - 1)) * BLOCK, BLOCK)

            def score(h):
                pair, sub = h // 2, h % 2
                q = query[pair, pl.ds(here, BLOCK), :]
                qm = jnp.where((lane < 64) == (sub == 0), q, jnp.zeros_like(q))
                diag = nt(qm, keys[pair, pl.ds(here, BLOCK), :])
                rest = None
                if wide > 1:
                    rest = nt(qm, keys[pair, pl.ds(first, (wide - 1) * BLOCK), :])
                return diag, rest

            def soften(diag, rest):
                diag = jnp.where(tri, diag, MASKED)
                top = jnp.max(diag, axis=1, keepdims=True)
                if wide > 1:
                    top = jnp.maximum(top, jnp.max(rest, axis=1, keepdims=True))
                raised = [jnp.exp2(diag - top).astype(BF16)]
                if wide > 1:
                    raised.append(jnp.exp2(rest - top).astype(BF16))
                return top, raised

            def finish(h, top, raised):
                acc = nn(raised[0], values[h // 2, pl.ds(here, BLOCK), :])
                if wide > 1:
                    acc += nn(raised[1], values[h // 2, pl.ds(first, (wide - 1) * BLOCK), :])
                sums = acc[:, 128:]
                return acc[:, :128] / sums, jnp.transpose(top + jnp.log2(sums))[0:1, :]

            scores = [score(h) for h in range(4)]
            softened = [soften(*scores[h]) for h in range(4)]
            outs = [finish(h, *softened[h]) for h in range(4)]
            for pair in range(2):
                mixed[pair, pl.ds(here, BLOCK), :] = jnp.where(lane < 64, outs[2*pair][0], outs[2*pair+1][0]).astype(BF16)
                for sub in range(2):
                    logsum[pair, sub : sub + 1, pl.ds(here, BLOCK)] = outs[2*pair+sub][1]

        for wide in range(1, blocks + 1):
            pl.when(width == wide)(partial(run, wide))
        return 0

    lax.fori_loop(0, blocks, attend, 0)
    mover.start(mixed, mixed_out)
    mover.start(logsum, logsum_out)

    for out_ref, target, which in (
        (mixed_other, mixed_other_out, 1 - head),
        (mixed_own, mixed_own_out, head),
    ):

        def give(step, _, out_ref=out_ref, which=which):
            at = pl.ds(pl.multiple_of(step * BLOCK, BLOCK), BLOCK)
            tile = which * (half // BLOCK) + step

            def put(count_here):
                for pair in range(2):
                    part = load_grouped(lambda s: mixed[pair, s, :], tile, total, count_here)
                    if count_here > 1:
                        part = nn(sorter(count_here, True), part).astype(BF16)
                    out_ref[at, pair * 128 : (pair + 1) * 128] = part

            for option in SLOT_OPTIONS:
                pl.when(count == option)(partial(put, option))
            return 0

        lax.fori_loop(0, half // BLOCK, give, 0)
        mover.start(out_ref, target)
    mover.wait_all()


class Mover:
    def __init__(self, semaphores):
        self.semaphores, self.used, self.open = semaphores, 0, {}

    def start(self, source, target, name=None):
        copy = pltpu.make_async_copy(source, target, self.semaphores.at[self.used])
        copy.start()
        self.open[self.used if name is None else name] = copy
        self.used += 1

    def wait(self, *names):
        for name in names:
            self.open.pop(name).wait()

    def wait_all(self):
        self.wait(*list(self.open))


def run_kernel(kernel, name, scalars, args, outs, scratch, moves, flops, aliases=None, limit=VMEM_MIB):
    smem = pl.BlockSpec(memory_space=pltpu.SMEM)
    large = pl.BlockSpec(memory_space=pl.ANY)
    size = lambda shape, dtype: math.prod(shape) * jnp.dtype(dtype).itemsize
    moved = sum(size(a.shape, a.dtype) for a in args) + sum(size(*o) for o in outs)
    return pl.pallas_call(
        kernel,
        in_specs=[smem] * len(scalars) + [large] * len(args),
        out_specs=[large] * len(outs),
        out_shape=[jax.ShapeDtypeStruct(*o) for o in outs],
        scratch_shapes=[pltpu.VMEM(*s) for s in scratch] + [pltpu.SemaphoreType.DMA((moves,))],
        input_output_aliases=aliases or {},
        cost_estimate=pl.CostEstimate(flops=flops, bytes_accessed=moved, transcendentals=0),
        compiler_params=pltpu.CompilerParams(vmem_limit_bytes=limit * MIB),
        name=name,
    )(*scalars, *args)


def forward_attention(info, own, other, skip_own, skip_other, wq, wk, wv, gain, shift):
    half, width = own.shape
    total = 2 * half
    group = wq.shape[1] // 2
    outs = [
        ((half, group), BF16),
        ((half, group), BF16),
        ((2, total, 128), BF16),
        ((2, total, 128), BF16),
        ((2, total, 128), BF16),
        ((2, total, 128), BF16),
        ((2, 8, total), F32),
        ((total, width), BF16),
    ]
    scratch = [
        ((half, width), BF16),
        ((half, width), BF16),
        ((half, 128), BF16),
        ((half, 128), BF16),
        ((width, group), BF16),
        ((width, group), BF16),
        ((width, 128), BF16),
        *outs,
        ((2, total, 256), BF16),
        (gain.shape, F32),
        (shift.shape, F32),
    ]
    return run_kernel(
        forward_kernel, "forward_attention", (info,),
        (own, other, skip_own, skip_other, wq, wk, wv, gain, shift), outs, scratch, 17, 10 * 10**9,
        limit=WHOLE_MIB,
    )


COLS = 512
TILE, PART = 512, 256
GELU_SLOPE = math.sqrt(2.0 / math.pi)
GELU_CUBE = 0.044715


def gelu_pair(v):
    square = v * v
    bend = jnp.tanh(v * (GELU_SLOPE + (GELU_SLOPE * GELU_CUBE) * square))
    front = 0.5 + 0.5 * bend
    steep = v * (2.0 * GELU_SLOPE + (6.0 * GELU_SLOPE * GELU_CUBE) * square)
    return v * front, front + steep * (front * (1.0 - front))


def rows_kernel(
    info, lengths, tokens_in, mixed_own_in, mixed_other_in, cotangent_in, mixing_in, expand_in,
    shrink_in, bias_in, gain_in, shift_in,
    output_out, after_grad_out, send_own_out, send_other_out,
    own_stay_out, own_away_out, other_stay_out, other_away_out, vectors_out,
    tokens, mixed_own, mixed_other, cotangent, mixing_weight, expand_weight, shrink_weight,
    expand_bias, gain, shift, output, after_grad, send_own, send_other, grads_own, grads_other,
    vectors, bias_grad, gain_grads, active, pre_grad, middle, out_grad, after_low, semaphores,
):
    mover = Mover(semaphores)
    for source, target, name in (
        (mixing_in, mixing_weight, "mixing"),
        (tokens_in, tokens, "tokens"),
        (mixed_own_in, mixed_own, "own"),
        (mixed_other_in, mixed_other, "other"),
        (gain_in, gain, "gain"),
        (shift_in, shift, "shift"),
        (bias_in, expand_bias, "bias"),
        (expand_in, expand_weight, "expand"),
        (shrink_in, shrink_weight, "shrink"),
        (cotangent_in, cotangent, "cotangent"),
    ):
        mover.start(source, target, name)
    count, head = info[0], info[1]
    half, width = tokens.shape
    hidden = expand_weight.shape[1]
    group = mixed_own.shape[1]
    shift_by = (
        (count >= 2).astype(jnp.int32)
        + (count >= 4).astype(jnp.int32)
        + (count >= 8).astype(jnp.int32)
    )
    here = pl.ds(pl.multiple_of(head * group, group), group)
    there = pl.ds(pl.multiple_of((1 - head) * group, group), group)
    bias_grad[...] = jnp.zeros_like(bias_grad)
    gain_grads[...] = jnp.zeros_like(gain_grads)
    mover.wait("mixing", "tokens", "own", "other", "gain", "shift", "bias")

    def tile(step, _):
        at = pl.ds(pl.multiple_of(step * TILE, TILE), TILE)
        row = head * half + step * TILE + lax.broadcasted_iota(jnp.int32, (TILE, 1), 0)
        slot = row & (count - 1)
        limit = jnp.zeros_like(row)
        for s in range(lengths.shape[0]):
            limit = jnp.where(slot == s, lengths[s], limit)
        valid = (row >> shift_by) < limit

        def first_wait(*names):
            pl.when(step == 0)(lambda: mover.wait(*names))

        after = (
            tokens[at, :].astype(F32)
            + nn(mixed_own[at, :], mixing_weight[here, :])
            + nn(mixed_other[at, :], mixing_weight[there, :])
        )
        hat, scale = normalized(after)
        low = (hat * gain[...] + shift[...]).astype(BF16)
        middle[at, :] = low
        first_wait("expand", "shrink", "cotangent")
        grad_out = jnp.where(valid, cotangent[at, :].astype(F32), 0.0)
        grad_low = grad_out.astype(BF16)
        out_grad[at, :] = grad_low

        def products(c):
            cs = slice(c, c + PART)
            return nn(low, expand_weight[:, cs]), nt(grad_low, shrink_weight[cs, :])

        ahead = products(0)
        for c in range(0, hidden, PART):
            cs = slice(c, c + PART)
            now = ahead
            if c + PART < hidden:
                ahead = products(c + PART)
            act, slope = gelu_pair(now[0] + expand_bias[:, cs])
            active[at, cs] = act.astype(BF16)
            g = now[1] * slope
            bias_grad[0:1, cs] += jnp.sum(g, axis=0, keepdims=True)
            pre_grad[at, cs] = g.astype(BF16)
        g_middle = nt(pre_grad[at, :], expand_weight[...])
        grown = nn(active[at, :], shrink_weight[...])
        gain_grads[0:1, :] += jnp.sum(g_middle * hat, axis=0, keepdims=True)
        gain_grads[1:2, :] += jnp.sum(g_middle, axis=0, keepdims=True)
        y = g_middle * gain[...]
        g_after = grad_out + scale * (
            y
            - jnp.mean(y, axis=-1, keepdims=True)
            - hat * jnp.mean(y * hat, axis=-1, keepdims=True)
        )
        after_grad[at, :] = g_after
        g_low = g_after.astype(BF16)
        after_low[at, :] = g_low
        output[at, :] = jnp.where(valid, after + grown, 0.0).astype(BF16)
        send_own[at, :] = nt(g_low, mixing_weight[here, :]).astype(BF16)
        send_other[at, :] = nt(g_low, mixing_weight[there, :]).astype(BF16)
        return 0

    lax.fori_loop(0, half // TILE, tile, 0)

    for source, target in (
        (send_other, send_other_out),
        (send_own, send_own_out),
        (output, output_out),
        (after_grad, after_grad_out),
    ):
        mover.start(source, target)
    vectors[...] = jnp.zeros_like(vectors)
    for n, c in enumerate(range(0, hidden, width)):
        vectors[n : n + 1, :] = bias_grad[0:1, c : c + width]
    vectors[4:6, :] = gain_grads[0:2, :]
    mover.start(vectors, vectors_out)
    first_half = grads_own.shape[0] // 2
    for grads, stay_out, away_out, mixed, which, side in (
        (grads_other, other_stay_out, other_away_out, mixed_other, 1 - head, info[4]),
        (grads_own, own_stay_out, own_away_out, mixed_own, head, info[2]),
    ):
        stay = pl.ds(pl.multiple_of(side * first_half, 16), first_half)
        away = pl.ds(pl.multiple_of((1 - side) * first_half, 16), first_half)

        def weights(step, _, grads=grads, which=which):
            cs = pl.ds(pl.multiple_of((2 * which + step) * COLS, COLS), COLS)
            at = pl.multiple_of(step * COLS, COLS)
            grads[pl.ds(at, COLS), :] = tn(active[:, cs], out_grad[...]).astype(BF16)
            grads[pl.ds(2 * COLS + at, COLS), :] = tn(middle[...], pre_grad[:, cs]).astype(BF16)
            return 0

        lax.fori_loop(0, 2, weights, 0)
        grads[4 * COLS :, :] = tn(mixed[...], after_low[...]).astype(BF16)
        mover.start(grads.at[away], away_out)
        mover.start(grads.at[stay], stay_out)
    mover.wait_all()


def row_part(info, lengths, tokens, mixed_own, mixed_other, cotangent, wo, we, ws, bias, gain, shift):
    half, width = tokens.shape
    hidden = we.shape[1]
    group = mixed_own.shape[1]
    outs = [
        ((half, width), BF16),
        ((half, width), F32),
        ((half, group), BF16),
        ((half, group), BF16),
        *[(((hidden + group) // 2, width), BF16)] * 4,
        ((8, width), F32),
    ]
    args = (tokens, mixed_own, mixed_other, cotangent, wo, we, ws, bias, gain, shift)
    scratch = [
        *[(a.shape, a.dtype) for a in args],
        *outs[:4],
        ((hidden + group, width), BF16),
        ((hidden + group, width), BF16),
        outs[8],
        ((8, hidden), F32),
        ((8, width), F32),
        ((half, hidden), BF16),
        ((half, hidden), BF16),
        ((half, width), BF16),
        ((half, width), BF16),
        ((half, width), BF16),
    ]
    return run_kernel(
        rows_kernel, "row_part", (info, lengths), args, outs, scratch, 19, 15 * 10**9,
        limit=WHOLE_MIB,
    )


def arrange_gradient(count, head, grad_own, grad_other, mixed, grad, inner):
    half = grad_own.shape[0]
    total = 2 * half

    for rows_ref, which in ((grad_own, head), (grad_other, 1 - head)):

        def arrange(step, _, rows_ref=rows_ref, which=which):
            at = pl.ds(pl.multiple_of(step * BLOCK, BLOCK), BLOCK)
            tile = which * (half // BLOCK) + step
            rows = rows_ref[at, :]

            def put(count_here):
                value = rows
                if count_here > 1:
                    value = nn(sorter(count_here), rows).astype(BF16)
                for pair in range(2):

                    def write(dst, piece, pair=pair):
                        grad[pair, dst, :] = piece

                    store_grouped(
                        write, value[:, pair * 128 : (pair + 1) * 128], tile, total, count_here
                    )

            for option in SLOT_OPTIONS:
                pl.when(count == option)(partial(put, option))
            return 0

        lax.fori_loop(0, half // BLOCK, arrange, 0)

    def inners(block, _):
        at = pl.ds(pl.multiple_of(block * BLOCK, BLOCK), BLOCK)
        for pair in range(2):
            flipped = jnp.transpose(grad[pair, at, :].astype(F32) * mixed[pair, at, :].astype(F32))
            for sub in range(2):
                inner[pair, sub : sub + 1, at] = jnp.sum(
                    flipped[sub * 64 : (sub + 1) * 64], axis=0, keepdims=True
                )
        return 0

    lax.fori_loop(0, total // BLOCK, inners, 0)


def attend_blocks(
    count, first, last, query, keys, values, grad, logsum, inner, query_total, kept, key_sums, value_sums
):
    blocks = first + query.shape[1] // BLOCK
    per_slot = blocks // count
    lane = lax.broadcasted_iota(jnp.int32, (1, 128), 1)
    tri = lax.broadcasted_iota(jnp.int32, (BLOCK, BLOCK), 0) <= lax.broadcasted_iota(
        jnp.int32, (BLOCK, BLOCK), 1
    )

    def attend(block, _):
        more = per_slot - block % per_slot - 1
        here = pl.multiple_of((block - first) * BLOCK, BLOCK)
        at = pl.ds(here, BLOCK)

        def part(start, size, diagonal):
            span = pl.ds(pl.multiple_of(start, BLOCK), size)

            def score(h):
                pair, sub = h // 2, h % 2
                pick = (lane < 64) == (sub == 0)
                k, v = keys[pair, at, :], values[pair, at, :]
                k = jnp.where(pick, k, jnp.zeros_like(k))
                v = jnp.where(pick, v, jnp.zeros_like(v))
                return k, nt(k, query[pair, span, :]), nt(v, grad[pair, span, :])

            def finish(h, k, raw, grad_probs):
                pair, sub = h // 2, h % 2
                probs = jnp.exp2(raw - logsum[pair, sub : sub + 1, span])
                if diagonal:
                    probs = jnp.where(tri, probs, 0.0)
                grad_scores = (probs * (grad_probs - inner[pair, sub : sub + 1, span])).astype(BF16)
                grad_value = nn(probs.astype(BF16), grad[pair, span, :])
                grad_key = nn(grad_scores, query[pair, span, :])
                if diagonal:
                    value_sums[h], key_sums[h] = grad_value, grad_key
                else:
                    value_sums[h] += grad_value
                    key_sums[h] += grad_key
                return tn(grad_scores, k)

            ahead = score(0)
            done = []
            for h in range(4):
                now = ahead
                if h < 3:
                    ahead = score(h + 1)
                done.append(finish(h, *now))
                if h % 2:
                    query_total[h // 2, span, :] += done[h - 1] + done[h]

        part(here, BLOCK, True)

        def two(n, _):
            part(here + BLOCK + n * (2 * BLOCK), 2 * BLOCK, False)
            return 0

        lax.fori_loop(0, more // 2, two, 0)

        @pl.when(more % 2 == 1)
        def _():
            part(here + more * BLOCK, BLOCK, False)

        for pair in range(2):
            for start, sums, scale in ((0, key_sums, 1.0 / LOG2E), (256, value_sums, 1.0)):
                picked = jnp.where(lane < 64, sums[2 * pair], sums[2 * pair + 1])
                kept[at, start + pair * 128 : start + (pair + 1) * 128] = (picked * scale).astype(BF16)
        return 0

    lax.fori_loop(first, last, attend, 0)


def arrange_kernel(
    info, grad_own_in, grad_other_in, mixed_in, grad_out, inner_out,
    grad_own, grad_other, mixed, grad, inner, semaphores,
):
    mover = Mover(semaphores)
    for source, target in ((grad_own_in, grad_own), (grad_other_in, grad_other), (mixed_in, mixed)):
        mover.start(source, target)
    mover.wait_all()
    arrange_gradient(info[0], info[1], grad_own, grad_other, mixed, grad, inner)
    mover.start(grad, grad_out)
    mover.start(inner, inner_out)
    mover.wait_all()


def arrange_rows(info, grad_own, grad_other, mixed):
    total = mixed.shape[1]
    outs = [((2, total, 128), BF16), ((2, 8, total), F32)]
    args = (grad_own, grad_other, mixed)
    scratch = [(a.shape, BF16) for a in args] + outs
    return run_kernel(arrange_kernel, "arrange_rows", (info,), args, outs, scratch, 5, 10**8, limit=WHOLE_MIB)


def fetch_blocks(mover, first, last, sources, targets):
    query, keys, values, grad, logsum, inner, *before = sources
    total = query.shape[1]
    span, rows = pl.ds(first * BLOCK, total - first * BLOCK), pl.ds(first * BLOCK, (last - first) * BLOCK)
    for source, target in zip(
        (
            keys.at[:, rows], query.at[:, span], values.at[:, rows], grad.at[:, span],
            logsum.at[:, :, span], inner.at[:, :, span], *[b.at[:, span] for b in before],
        ),
        targets,
    ):
        mover.start(source, target)


def next_kernel(first, last, info, *refs):
    count = 7 if first else 6
    sources, (query_total_out, kept_out), local, (key_sums, value_sums, kept, semaphores) = (
        refs[:count], refs[count : count + 2], refs[count + 2 : count + 9], refs[count + 9 :]
    )
    mover = Mover(semaphores)
    fetch_blocks(mover, first, last, sources, local)
    keys, query, values, grad, logsum, inner, query_total = local
    if not first:
        query_total[...] = jnp.zeros_like(query_total)
    mover.wait_all()
    attend_blocks(
        info[0], first, last, query, keys, values, grad, logsum, inner, query_total, kept,
        key_sums, value_sums,
    )
    total = sources[0].shape[1]
    span = pl.ds(first * BLOCK, total - first * BLOCK)
    mover.start(query_total, query_total_out.at[:, span])
    mover.start(kept, kept_out)
    mover.wait_all()


def local_blocks(first, last, total):
    rows, span = (last - first) * BLOCK, total - first * BLOCK
    return [
        ((2, rows, 128), BF16),
        ((2, span, 128), BF16),
        ((2, rows, 128), BF16),
        ((2, span, 128), BF16),
        ((2, 8, span), F32),
        ((2, 8, span), F32),
        ((2, span, 128), F32),
        ((4, BLOCK, 128), F32),
        ((4, BLOCK, 128), F32),
    ]


def next_blocks(first, last, info, before, query, keys, values, grad, logsum, inner):
    outs = [(query.shape, F32), (((last - first) * BLOCK, 512), BF16)]
    args = (query, keys, values, grad, logsum, inner) + ((before,) if first else ())
    return run_kernel(
        partial(next_kernel, first, last), f"blocks_{first}", (info,), args, outs,
        local_blocks(first, last, query.shape[1]) + [outs[1]], 9, 5 * 10**9, {7: 0} if first else {},
    )


def last_kernel(first, pieces, info, *refs):
    sources, refs = refs[:7], refs[7:]
    normed_in, gain_in, shift_in, vectors_in, query_in, key_in, value_in = refs[:7]
    kept_in, refs = refs[7 : 7 + pieces], refs[7 + pieces :]
    stay_out, away_out, packed_out = refs[:3]
    local, (key_sums, value_sums, *refs) = refs[3:10], refs[10:]
    kept, normed, gain, shift, vectors, query_weight, key_weight, value_weight, before, weight_grad, packed, semaphores = refs
    keys, query, values, grad, logsum, inner, query_total = local
    total = packed.shape[0]
    head = info[1]
    cols = pl.ds(pl.multiple_of(head * 256, 256), 256)
    fresh_cols = pl.ds(pl.multiple_of(head * 128, 128), 128)
    mover = Mover(semaphores)
    fetch_blocks(mover, first, total // BLOCK, sources, local)
    mover.start(sources[6].at[:, pl.ds(0, first * BLOCK)], before, "before")
    mover.start(normed_in, normed, "normed")
    mover.start(vectors_in, vectors, "vectors")
    mover.start(gain_in, gain, "gain")
    mover.start(shift_in, shift, "shift")
    mover.start(query_in.at[:, cols], query_weight, "q")
    mover.start(key_in.at[:, cols], key_weight, "k")
    mover.start(value_in.at[:, fresh_cols], value_weight, "v")
    row = 0
    for n, piece in enumerate(kept_in):
        mover.start(piece, packed.at[pl.ds(row, piece.shape[0]), pl.ds(256, 512)], f"p{n}")
        row += piece.shape[0]
    mover.wait(*range(7))
    attend_blocks(
        info[0], first, total // BLOCK, query, keys, values, grad, logsum, inner, query_total, kept,
        key_sums, value_sums,
    )
    mover.wait_all()
    packed[row:, 256:] = kept[...]
    for pair in range(2):
        lanes = slice(pair * 128, (pair + 1) * 128)
        packed[:row, lanes] = (before[pair, :, :] * 0.125).astype(BF16)
        packed[row:, lanes] = (query_total[pair, :, :] * 0.125).astype(BF16)
    mover.start(packed, packed_out)
    ones = jnp.ones((8, total), BF16)
    gain_grad = jnp.zeros((gain.shape[1], 1), F32)
    shift_grad = jnp.zeros((gain.shape[1], 1), F32)
    gain_column = jnp.transpose(jnp.broadcast_to(gain[...], (128, gain.shape[1])))[:, :1]
    shift_column = jnp.transpose(jnp.broadcast_to(shift[...], (128, gain.shape[1])))[:, :1]
    for start, stop, weight in ((0, 256, query_weight), (256, 512, key_weight), (512, 640, value_weight)):
        part = packed[:, start:stop]
        product = tn(normed[...], part)
        sums = nn(ones, part)[0:1, :]
        weight_grad[:, start:stop] = product.astype(BF16)
        weight = weight[...].astype(F32)
        shift_grad += jnp.sum(weight * sums, axis=1, keepdims=True)
        gain_grad += jnp.sum(weight * (product - shift_column * sums), axis=1, keepdims=True)
    lane = lax.broadcasted_iota(jnp.int32, (1, 128), 1)
    edge = jnp.where(lane == 0, gain_grad / gain_column, jnp.where(lane == 1, shift_grad, 0.0))
    stack = jnp.concatenate([vectors[...], jnp.zeros((120, vectors.shape[1]), F32)], axis=0)
    edge += jnp.where(lane >= 8, pltpu.roll(jnp.transpose(stack), 8, 1), 0.0)
    weight_grad[:, 640:] = edge.astype(BF16)
    rows = weight_grad.shape[0] // 2
    mover.start(weight_grad.at[pl.ds(pl.multiple_of((1 - info[3]) * rows, 16), rows)], away_out)
    mover.start(weight_grad.at[pl.ds(pl.multiple_of(info[3] * rows, 16), rows)], stay_out)
    mover.wait_all()


def last_blocks(first, info, before, query, keys, values, grad, logsum, inner, normed, gain, shift, vectors, wq, wk, wv, kept):
    total, width = normed.shape
    outs = [((width // 2, 768), BF16), ((width // 2, 768), BF16), ((total, 768), BF16)]
    scratch = local_blocks(first, total // BLOCK, total) + [
        ((total - first * BLOCK, 512), BF16),
        (normed.shape, BF16),
        (gain.shape, F32),
        (shift.shape, F32),
        (vectors.shape, F32),
        ((width, 256), BF16),
        ((width, 256), BF16),
        ((width, 128), BF16),
        ((2, first * BLOCK, 128), F32),
        ((width, 768), BF16),
        outs[2],
    ]
    return run_kernel(
        partial(last_kernel, first, len(kept)), "last_blocks", (info,),
        (query, keys, values, grad, logsum, inner, before, normed, gain, shift, vectors, wq, wk, wv, *kept),
        outs, scratch, 18 + len(kept), 5 * 10**9,
    )


def back_kernel(
    info, packed_in, query_in, key_in, value_in, back_own_out, back_other_out, skip_own_out, skip_other_out,
    packed, query_weight, key_weight, value_weight, back_own, back_other, skip_own, skip_other, back, semaphores,
):
    count, head = info[0], info[1]
    total = packed.shape[0]
    half = total // 2
    cols = pl.ds(pl.multiple_of(head * 256, 256), 256)
    fresh_cols = pl.ds(pl.multiple_of(head * 128, 128), 128)
    mover = Mover(semaphores)
    mover.start(packed_in, packed)
    mover.start(query_in.at[:, cols], query_weight)
    mover.start(key_in.at[:, cols], key_weight)
    mover.start(value_in.at[:, fresh_cols], value_weight)
    mover.wait_all()

    def close(block, _):
        at = pl.ds(pl.multiple_of(block * BLOCK, BLOCK), BLOCK)
        back[at, :] = (
            nt(packed[at, :256], query_weight[...])
            + nt(packed[at, 256:512], key_weight[...])
            + nt(packed[at, 512:640], value_weight[...])
        ).astype(BF16)
        return 0

    lax.fori_loop(0, total // BLOCK, close, 0)

    for back_ref, skip_ref, back_out, skip_out, which in (
        (back_other, skip_other, back_other_out, skip_other_out, 1 - head),
        (back_own, skip_own, back_own_out, skip_own_out, head),
    ):

        def give(step, _, back_ref=back_ref, skip_ref=skip_ref, which=which):
            at = pl.ds(pl.multiple_of(step * BLOCK, BLOCK), BLOCK)
            tile = which * (half // BLOCK) + step

            def put(count_here):
                g = load_grouped(lambda s: back[s, :], tile, total, count_here)
                k = load_grouped(lambda s: packed[s, 640:], tile, total, count_here)
                if count_here > 1:
                    order = sorter(count_here, True)
                    g = nn(order, g).astype(BF16)
                    k = nn(order, k).astype(BF16)
                back_ref[at, :] = g
                skip_ref[at, :] = k

            for option in SLOT_OPTIONS:
                pl.when(count == option)(partial(put, option))
            return 0

        lax.fori_loop(0, half // BLOCK, give, 0)
        mover.start(back_ref, back_out)
        mover.start(skip_ref, skip_out)
    mover.wait_all()


def back_rows(info, packed, wq, wk, wv):
    total, width = packed.shape[0], wq.shape[0]
    half = total // 2
    outs = [((half, width), BF16), ((half, width), BF16), ((half, 128), BF16), ((half, 128), BF16)]
    scratch = [
        (packed.shape, BF16),
        ((width, 256), BF16),
        ((width, 256), BF16),
        ((width, 128), BF16),
        *outs,
        ((total, width), BF16),
    ]
    return run_kernel(
        back_kernel, "back_rows", (info,), (packed, wq, wk, wv), outs, scratch, 8, 2 * 10**9
    )


def close_kernel(
    info, tokens_in, after_grad_in, back_own_in, back_other_in, kept_in, arrived_in, gain_in,
    result_out, skip_out,
    tokens, after_grad, back_own, back_other, gain, result, skip_grad, semaphores,
):
    head = info[1]
    mover = Mover(semaphores)
    mover.start(gain_in, gain)
    mover.start(tokens_in, tokens)
    mover.start(after_grad_in, after_grad)
    mover.start(back_own_in, back_own)
    mover.start(back_other_in, back_other)
    mover.start(kept_in, skip_grad.at[:, pl.ds(pl.multiple_of(head * 128, 128), 128)])
    mover.start(arrived_in, skip_grad.at[:, pl.ds(pl.multiple_of((1 - head) * 128, 128), 128)])
    mover.wait_all()
    mover.start(skip_grad, skip_out)

    def tile(step, _):
        at = pl.ds(pl.multiple_of(step * BLOCK, BLOCK), BLOCK)
        hat, scale = normalized(tokens[at, :].astype(F32))
        y = (back_own[at, :].astype(F32) + back_other[at, :].astype(F32)) * gain[...]
        result[at, :] = (
            after_grad[at, :]
            + scale
            * (
                y
                - jnp.mean(y, axis=-1, keepdims=True)
                - hat * jnp.mean(y * hat, axis=-1, keepdims=True)
            )
        ).astype(BF16)
        return 0

    lax.fori_loop(0, tokens.shape[0] // BLOCK, tile, 0)
    mover.start(result, result_out)
    mover.wait_all()


def close_rows(info, tokens, after_grad, back_own, back_other, kept, arrived, gain):
    args = (tokens, after_grad, back_own, back_other, kept, arrived, gain)
    outs = [(tokens.shape, BF16), ((tokens.shape[0], 256), BF16)]
    scratch = [(a.shape, a.dtype) for a in args[:4]] + [(gain.shape, F32)] + outs
    return run_kernel(close_kernel, "close_rows", (info,), args, outs, scratch, 9, 10**8)


def unpack_kernel(late, info, *refs):
    half_in, refs = refs[0], refs[1 + (3 if late else 0) :]
    shrink_out, expand_out, mixing_out, half, wide, semaphores = refs
    which = 1 - info[1] if late else info[1]
    width = half.shape[1]
    top = 4 * COLS + mixing_out.shape[0] // 2
    mover = Mover(semaphores)
    for at in range(0, 4 * COLS, COLS):
        mover.start(half_in.at[pl.ds(at, COLS)], half.at[pl.ds(at, COLS)], at)
    mover.start(half_in.at[pl.ds(4 * COLS, half.shape[0] - 4 * COLS)], half.at[pl.ds(4 * COLS, half.shape[0] - 4 * COLS)], "rest")
    for at in range(0, 4 * COLS, COLS):
        mover.wait(at)
        wide[at : at + COLS, :] = half[at : at + COLS, :].astype(F32)
        if at < 2 * COLS:
            row = pl.multiple_of(which * 2 * COLS + at, COLS)
            mover.start(wide.at[pl.ds(at, COLS)], shrink_out.at[pl.ds(row, COLS)])
        else:
            col = pl.multiple_of(which * 2 * COLS + at - 2 * COLS, COLS)
            mover.start(wide.at[pl.ds(at, COLS)], expand_out.at[:, pl.ds(col, COLS)])
    mover.wait("rest")
    wide[4 * COLS :, :] = half[4 * COLS :, :].astype(F32)
    row = pl.multiple_of(which * (top - 4 * COLS), 256)
    mover.start(wide.at[pl.ds(4 * COLS, top - 4 * COLS)], mixing_out.at[pl.ds(row, top - 4 * COLS)])
    mover.wait_all()


def unpack_half(info, half, before=()):
    rows, width = half.shape
    hidden = 4 * COLS
    outs = [((hidden, width), F32), ((width, hidden), F32), ((width, width), F32)]
    scratch = [(half.shape, BF16), ((rows, width), F32)]
    return run_kernel(
        partial(unpack_kernel, bool(before)), "unpack_late" if before else "unpack_half", (info,),
        (half, *before), outs, scratch, 10, 10**8, {2 + n: n for n in range(3)} if before else {},
        limit=20,
    )


def split_kernel(
    info, mine_in, arrived_in, query_out, key_out, value_out, *refs
):
    vectors_out, (mine, arrived, query, key, value), vectors, semaphores = refs[:5], refs[5:10], refs[10:15], refs[15]
    head = info[1]
    mover = Mover(semaphores)
    mover.start(mine_in, mine)
    mover.start(arrived_in, arrived)
    mover.wait_all()
    for half, which in ((mine, head), (arrived, 1 - head)):
        for target, wide, at in ((query, 256, 0), (key, 256, 256), (value, 128, 512)):
            cols = pl.ds(pl.multiple_of(which * wide, 128), wide)
            target[:, cols] = half[:, at : at + wide].astype(F32)
    for source, target in ((query, query_out), (key, key_out), (value, value_out)):
        mover.start(source, target)
    edges = jnp.transpose(mine[:, 640:].astype(F32) + arrived[:, 640:].astype(F32))
    gain, shift, bias, middle_gain, middle_shift = vectors
    width = gain.shape[1]
    for target, at in ((gain, 0), (shift, 1), (middle_gain, 12), (middle_shift, 13)):
        target[...] = edges[at : at + 1]
    for n in range(bias.shape[1] // width):
        bias[:, n * width : (n + 1) * width] = edges[8 + n : 9 + n]
    for source, target in zip(vectors, vectors_out):
        mover.start(source, target)
    mover.wait_all()


def split_projection(info, mine, arrived):
    width = mine.shape[0]
    outs = [((width, 512), F32), ((width, 512), F32), ((width, 256), F32)]
    outs += [((1, n * width), F32) for n in (1, 1, 4, 1, 1)]
    scratch = [(mine.shape, BF16), (mine.shape, BF16)] + outs
    return run_kernel(split_kernel, "split_projection", (info,), (mine, arrived), outs, scratch, 10, 10**8, limit=20)


def swap_cores(array):
    return lax.ppermute(array, "head", [(0, 1), (1, 0)])


def half_of(array, which):
    rows = array.shape[0] // 2
    return lax.dynamic_slice_in_dim(array, which * rows, rows, 0)


def add_low(a, b):
    return (a.astype(F32) + b.astype(F32)).astype(BF16)


def join(mine, theirs, which):
    both = jnp.concatenate([mine, mine], axis=0)
    return lax.dynamic_update_slice_in_dim(both, theirs, (1 - which) * mine.shape[0], 0)


def after_all(first, *rest):
    return lax.optimization_barrier((first, *rest))


class SeqSum:
    def __init__(self, orders):
        self.size = lax.axis_size("seq")
        bits = self.size.bit_length() - 1
        self.orders = [
            [b for b in order if b < bits] + [b for b in range(bits) if b not in order]
            for order in orders
        ]
        self.stage, self.bits = 0, bits
        self.fitting, self.whole, self.kept = False, False, None

    def begin(self, stay, stay_come, away, away_come):
        self.mine, self.coming, self.half = stay, stay_come, None if stay_come is None else -1
        self.sent = away if away_come is None else add_low(away, away_come)
        self.next, self.stage, self.trail = 0, 1, [0]

    def which(self, stage, other=0):
        bit = jnp.where(lax.axis_index("head") == other, self.orders[0][stage], self.orders[1][stage])
        return (lax.axis_index("seq") >> bit) & 1

    def swap(self, array, stage):
        pairs = []
        for i in range(self.size):
            for core in range(2):
                pairs.append((2 * i + core, 2 * (i ^ (1 << self.orders[core][stage])) + core))
        return lax.ppermute(array, ("seq", "head"), pairs)

    def added(self, which=None):
        parts = [a if which is None else half_of(a, which) for a in (self.mine, self.coming) if a is not None]
        return parts[0] if len(parts) == 1 else add_low(*parts)

    def prepare(self):
        if self.stage < self.bits:
            self.settle()
            if self.stage < self.bits - 1 and self.mine.shape[0] % 32 == 0:
                which = self.which(self.stage)
                self.trail.append(self.stage)
                self.sent, self.half = self.added(1 - which), which
            else:
                self.sent = self.mine = self.added()
                self.coming = None
            self.next = self.stage
            self.stage += 1
            return True
        self.settle()
        if self.fitting:
            self.mine = join(self.mine, self.coming, self.which(self.next))
        else:
            self.mine, self.fitting = self.added(), True
        if not self.trail:
            return False
        self.next, self.sent = self.trail.pop(), self.mine
        return True

    def launch(self):
        self.kept = self.coming
        self.coming = self.swap(self.sent, self.next)

    def settle(self):
        if self.half is not None:
            parts = [a for a in (self.mine, self.kept) if a is not None]
            if not isinstance(self.half, int):
                parts = [half_of(a, self.half) for a in parts]
            self.mine = parts[0] if len(parts) == 1 else add_low(*parts)
            self.half = None

    def via(self, stage):
        return lambda array: self.swap(array, stage)

    def flow(self, ready, small):
        while ready or self.stage < self.bits or len(self.trail) > 3:
            if not ready:
                self.prepare()
            ready = False
            (came,) = yield [(self.via(self.next), self.sent)]
            self.kept, self.coming = self.coming, came
        self.settle()
        piece = join(self.mine, self.coming, self.which(self.next)) if self.fitting else self.added()
        far, mid, near = self.trail
        rows = piece.shape[0]
        if small:
            (came_near,) = yield [(self.via(near), piece)]
        else:
            came_near, got_own = yield [(self.via(near), piece), (self.via(far), piece)]
        both = join(piece, came_near, self.which(near))
        if small:
            came_mid, got = yield [(self.via(mid), both), (self.via(far), both)]
            self.mine = join(both, came_mid, self.which(mid))
            got_mid, other_mine = yield [(self.via(far), came_mid), (swap_cores, self.mine)]
        else:
            (came_mid,) = yield [(self.via(mid), both)]
            cut = rows // 32 * 16
            (first,) = yield [(self.via(far), jnp.concatenate([came_near, came_mid[:cut]], axis=0))]
            (second,) = yield [(self.via(far), came_mid[cut:])]
            got = join(got_own, first[:rows], self.which(near))
            got_mid = jnp.concatenate([first[rows:], second], axis=0)
            self.mine = join(both, came_mid, self.which(mid))
        theirs = join(got, got_mid, self.which(mid))
        self.mine = join(self.mine, theirs, self.which(far))
        self.whole = True
        if small:
            (other_theirs,) = yield [(swap_cores, theirs)]
            self.other = join(other_mine, other_theirs, self.which(far, 1))
        else:
            (self.other,) = yield [(swap_cores, self.mine)]


ORDERS = ((0, 1, 2, 3), (1, 0, 3, 2))
PROJECTION_ORDERS = ((0, 1, 2, 3), (1, 0, 2, 3))
CUTS = (0, 2, 5, 8)


def on_device(
    tokens, first_values, cotangent, slot_count, seq_lengths, query_weight, key_weight, value_weight,
    mixing_weight, expand_weight, shrink_weight, expand_bias, before_gain, before_shift,
    middle_gain, middle_shift,
):
    head = lax.axis_index("head")
    sums, projection = SeqSum(ORDERS), SeqSum(PROJECTION_ORDERS)
    info = jnp.stack([slot_count[0], head, sums.which(0), projection.which(0), sums.which(0, 1)])
    info = info.astype(jnp.int32)
    lengths = seq_lengths[0]
    row = lambda v: v.reshape(1, -1)

    other = swap_cores(tokens)
    skip_other = swap_cores(first_values)
    mixed_own, mixed_away, query, keys, values, mixed, logsum, normed = forward_attention(
        info, tokens, other, first_values, skip_other, query_weight, key_weight, value_weight,
        row(before_gain), row(before_shift),
    )
    mixed_other = swap_cores(mixed_away)
    output, after_grad, grad_own, grad_away, own_stay, own_away, other_stay, other_away, row_vectors = row_part(
        info, lengths, tokens, mixed_own, mixed_other, cotangent, mixing_weight, expand_weight,
        shrink_weight, row(expand_bias), row(middle_gain), row(middle_shift),
    )
    grad_other = swap_cores(grad_away)
    grad_other, other_away = after_all(grad_other, other_away)
    away_come = swap_cores(other_away)
    grad, inner = arrange_rows(info, grad_own, grad_other, mixed)
    grad, away_come = after_all(grad, away_come)
    sums.begin(own_stay, swap_cores(other_stay), own_away, away_come)
    attention = (query, keys, values, grad, logsum, inner)
    query_total, pieces = None, []
    for first, last in zip(CUTS, CUTS[1:]):
        if first > 0:
            sums.prepare()
        *attention, sums.sent = after_all(*attention, sums.sent)
        sums.launch()
        if last < CUTS[-1]:
            query_total, kept = next_blocks(first, last, info, query_total, *attention)
            pieces.append(kept)
            query_total, sums.coming, sums.mine, sums.kept = after_all(
                query_total, sums.coming, sums.mine, sums.kept
            )
        else:
            projection_stay, projection_away, packed = last_blocks(
                first, info, query_total, *attention, normed, row(before_gain), row(before_shift),
                row_vectors, query_weight, key_weight, value_weight, pieces,
            )
            packed, sums.coming, sums.mine, sums.kept = after_all(packed, sums.coming, sums.mine, sums.kept)
    projection.begin(projection_stay, None, projection_away, None)

    lanes = [sums.flow(False, False), projection.flow(True, True)]
    pending = [next(lane) for lane in lanes]
    work, made, extra, finished = 0, None, (), False
    while pending:
        inputs = ()
        if work == 0:
            inputs, kernel = (packed,), lambda p: back_rows(info, p, query_weight, key_weight, value_weight)
        elif work == 1:
            extra = (back_away, skip_away)
        elif work == 2:
            inputs, kernel = (back_other, skip_arrived), lambda b, k: close_rows(
                info, tokens, after_grad, back_own, b, skip_own, k, row(before_gain)
            )
        elif sums.whole and made is None:
            inputs, kernel = (sums.mine,), lambda m: unpack_half(info, m)
        elif made is not None and not finished:
            inputs, kernel, finished = (sums.other, *made), lambda o, *m: unpack_half(info, o, tuple(m)), True
        moves = [move for group in pending for move in group]
        tied = after_all(*[array for _, array in moves], *extra, *inputs)
        count = len(moves)
        came = [swap(a) for (swap, _), a in zip(moves, tied)]
        came += [swap_cores(a) for a in tied[count : count + len(extra)]]
        results = kernel(*tied[count + len(extra) :]) if inputs else ()
        tied = after_all(*came, *results)
        came, results = tied[: len(came)], tied[len(came) :]
        if work == 0:
            back_own, back_away, skip_own, skip_away = results
        elif work == 1:
            back_other, skip_arrived = came[count:]
        elif work == 2:
            input_grad, skip_grad = results
        elif results:
            made = results
        work, extra = work + 1, ()
        later = []
        came = list(came)
        for lane, group in zip(lanes, pending):
            mine, came = came[: len(group)], came[len(group) :]
            try:
                later.append((lane, lane.send(mine)))
            except StopIteration:
                pass
        lanes, pending = [lane for lane, _ in later], [p for _, p in later]
    if made is None:
        made = unpack_half(info, sums.mine)
    if not finished:
        made = unpack_half(info, sums.other, tuple(made))
    shrink_grad, expand_grad, mixing_grad = made
    query_grad, key_grad, value_grad, *edges = split_projection(info, projection.mine, projection.other)
    before_gain_grad, before_shift_grad, bias_grad, middle_gain_grad, middle_shift_grad = [
        v.reshape(-1) for v in edges
    ]
    return (
        output, input_grad, skip_grad, query_grad, key_grad, value_grad, mixing_grad, expand_grad,
        shrink_grad, bias_grad, before_gain_grad, before_shift_grad, middle_gain_grad, middle_shift_grad,
    )


def solution(mesh):
    rows = P(("seq", "head"), None)
    return jax.shard_map(
        on_device,
        mesh=mesh,
        in_specs=(rows, rows, rows, P("seq"), P("seq", None)) + (P(),) * 11,
        out_specs=(rows, rows, rows) + (P(),) * 11,
        check_vma=False,
    )
```
